32 devices in a mesh: narrow: 4 (over x, core), wide: 8 (over z, y).
Axes of the slice: x: 2, y: 2, z: 4, core: 2. Of those that a mesh axis runs over, the one named last changes fastest.
Arguments:
- inputs: bfloat16 [4, 1024, 768], P('narrow', 'wide'), may hold values from -6 to 6
- segment_ids: int32 [4, 1024], P('narrow', 'wide'), may hold values from 0 to 3, as said below
- gain_attn: float32 [768], replicated, may hold values from 0.1 to 1.9
- w_query: bfloat16 [768, 768], replicated, may hold values from -0.0546875 to 0.0546875
- w_key: bfloat16 [768, 768], replicated, may hold values from -0.21875 to 0.21875
- w_value: bfloat16 [768, 768], replicated, may hold values from -0.21875 to 0.21875
- w_out: bfloat16 [768, 768], replicated, may hold values from -2.5 to 2.5
- gain_ffn: float32 [768], replicated, may hold values from 0.1 to 1.9
- w_gate: bfloat16 [768, 2048], replicated, may hold values from -0.21875 to 0.21875
- w_up: bfloat16 [768, 2048], replicated, may hold values from -0.21875 to 0.21875
- w_down: bfloat16 [2048, 768], replicated, may hold values from -0.125 to 0.125
- bias_table: float32 [32, 12], replicated, may hold values from -4 to 4
- cotangent: bfloat16 [4, 1024, 768], P('narrow', 'wide'), may hold values from -6 to 6
Outputs:
- output: bfloat16 [4, 1024, 768], P('narrow', 'wide')
- input_grad: float32 [4, 1024, 768], P('narrow', 'wide')
- grad_gain_attn: float32 [768], replicated
- grad_w_query: float32 [768, 768], P('wide', 'narrow')
- grad_w_key: float32 [768, 768], P('wide', 'narrow')
- grad_w_value: float32 [768, 768], P('wide', 'narrow')
- grad_w_out: float32 [768, 768], P('wide', 'narrow')
- grad_gain_ffn: float32 [768], replicated
- grad_w_gate: float32 [768, 2048], P('wide', 'narrow')
- grad_w_up: float32 [768, 2048], P('wide', 'narrow')
- grad_w_down: float32 [2048, 768], P('wide', 'narrow')
- grad_bias_table: float32 [32, 12], replicated
The draws below stay inside these ranges and needn't reach their ends.
Inputs may be any that keep to these rules, and one draw needn't show every extreme that they name: `segment_ids`: each row holds groups 1, 2 and 3 in this order, then padding (0) of 1 to 32 tokens at its end; group 1 ends within the first 64 tokens, group 3 has 1 to 32 tokens and so lies within the last 64 tokens.
All inputs are finite; a program needn't handle non-finite values.
Results may differ from the reference program's by a relative error of at most 0.02.
Values may be sent and summed in bfloat16 or wider, within the bound.
No kernel may reach another device: no remote copies, remote signals or barrier semaphores. Data moves between devices by JAX's collectives and lax.ppermute only.
A program may use at most 128 MiB of HBM per device.

```python
import math
import jax
import jax.numpy as jnp
from jax import lax

D = 768
H = 12
FF = 2048
BUCKETS = 32
TOK_DEV = 128
SEQ = 1024
ROWS = 4


def draw_segment_ids(key, part):
    key = jax.random.fold_in(key, 7)
    subkeys = jax.random.split(key, 3)
    quarter = max(TOK_DEV // 4, 1)
    half = max(TOK_DEV // 2, 2)
    positions = jnp.arange(SEQ, dtype=jnp.int32)[None, :]
    row_number = jnp.arange(ROWS, dtype=jnp.int32)[:, None]
    opening = jax.random.randint(subkeys[0], (ROWS, 1), 1, half, dtype=jnp.int32)
    opening = jnp.where(row_number == 2, half, opening)
    padding = jax.random.randint(subkeys[1], (ROWS, 1), 1, quarter + 1, dtype=jnp.int32)
    padding = jnp.where(row_number == 0, quarter, padding)
    last_group = jax.random.randint(subkeys[2], (ROWS, 1), 1, quarter + 1, dtype=jnp.int32)
    last_group = jnp.where(row_number == 1, quarter, last_group)
    closing = SEQ - padding - last_group
    numbers = 1 + (positions >= opening).astype(jnp.int32) + (positions >= closing).astype(jnp.int32)
    return jnp.where(positions >= SEQ - padding, 0, numbers).astype(jnp.int32)


def raised(entries, own_key, source, target, shards_of, factor):
    def block_of(dim):
        return (jnp.arange(entries.shape[dim]) // (entries.shape[dim] // shards_of)).reshape((-1,) + (1,) * (entries.ndim - 1 - dim))

    near = jax.random.permutation(own_key, shards_of)[block_of(target)]
    other_side = (block_of(target) + shards_of // 2) % shards_of
    return jnp.where((block_of(source) == near) | (block_of(source) == other_side), factor * entries, entries)


def shard_levels(rng, extent, shards, low, largest):
    factor_of = 1.0
    for dim, shards_of in shards:
        draws = jax.random.uniform(jax.random.fold_in(jax.random.fold_in(rng, 6), dim), (shards_of,), jnp.float32, low / len(shards), largest / len(shards))
        factor_of = factor_of * jnp.repeat(jnp.exp(draws), extent[dim] // shards_of).reshape((-1,) + (1,) * (len(extent) - 1 - dim))
    return factor_of


def scatter_about(key, dims, width, limit, cuts=(), kind=jnp.bfloat16):
    result = jax.random.normal(key, dims, jnp.float32) * width
    if len(cuts) > 0:
        result = shard_levels(key, dims, cuts, -0.22, 0.18) * result
    return jnp.clip(result, min=-limit, max=limit).astype(kind)


def heavy_noise(rng, extent, width, bound, cuts, heavy, held_as=jnp.bfloat16):
    drawn = width * jax.random.normal(rng, extent, jnp.float32)
    if cuts:
        drawn = drawn * shard_levels(rng, extent, cuts, -0.22, 0.18)
    return jnp.clip(raised(drawn, jax.random.fold_in(rng, 3), *heavy), -bound, bound).astype(held_as)


def setup_inputs(seed: int = 0) -> dict:
    key_of = jax.random.split(jax.random.key(seed), 14)
    return {
        "inputs": scatter_about(key_of[0], (ROWS, SEQ, D), 1.0, 6.0, ((0, 4), (1, 8))),
        "segment_ids": draw_segment_ids(jax.random.fold_in(key_of[13], 71), 0),
        "gain_attn": jnp.clip(1.0 + 0.18 * jax.random.normal(key_of[2], (D,), jnp.float32), 0.1, 1.9),
        "w_query": scatter_about(key_of[3], (D, D), (16 * D) ** -0.5, 0.0546875),
        "w_key": scatter_about(key_of[4], (D, D), D ** -0.5, 0.21875),
        "w_value": scatter_about(key_of[5], (D, D), D ** -0.5, 0.21875),
        "w_out": scatter_about(key_of[6], (D, D), (max(D // 128, 1)) ** -0.5, 2.5),
        "gain_ffn": jnp.clip(1.0 + 0.18 * jax.random.normal(key_of[7], (D,), jnp.float32), 0.1, 1.9),
        "w_gate": scatter_about(key_of[8], (D, FF), D ** -0.5, 0.21875),
        "w_up": scatter_about(key_of[9], (D, FF), D ** -0.5, 0.21875),
        "w_down": scatter_about(key_of[10], (FF, D), FF ** -0.5, 0.125),
        "bias_table": scatter_about(key_of[11], (BUCKETS, H), 1.0, 4.0, (), jnp.float32),
        "cotangent": heavy_noise(key_of[12], (ROWS, SEQ, D), 1.0, 6.0, ((0, 4), (1, 8)), (1, 2, 8, 2.0)),
    }


@jax.custom_vjp
def low(v):
    return lax.optimization_barrier(v.astype(jnp.bfloat16)).astype(jnp.float32)

@jax.custom_vjp
def low_back(v):
    return v

def low_keep(v):
    return (low(v), None)

def low_pass(kept, grad):
    return (grad,)

def back_keep(v):
    return (v, None)

def back_low(kept, grad):
    return (low(grad),)
low.defvjp(low_keep, low_pass)
low_back.defvjp(back_keep, back_low)
cutoffs = (1, 2, 3, 4, 5, 6, 7, 8, 12, 16, 23, 32, 46, 64, 91)
epsilon = 1e-06
masked_score = -1000000000.0
highest = lax.Precision.HIGHEST

def bucket_of(offset, half_count):
    distance = jnp.abs(offset)
    bucket = jnp.zeros(offset.shape, jnp.int32)
    for cutoff in cutoffs:
        bucket = bucket + (distance >= cutoff).astype(jnp.int32)
    return bucket + half_count * (offset > 0).astype(jnp.int32)

def rms_norm(values, gain):
    return values * lax.rsqrt(lax.optimization_barrier(jnp.mean(values * values, axis=-1, keepdims=True)) + epsilon) * gain

def project(values, weight):
    return jnp.einsum('rtd,de->rte', values, weight, precision=highest)

def attend_row(queries, key_rows, value_rows, segments, bias_table):
    length = queries.shape[0]
    block_rows = math.gcd(length, 512)
    head_count = bias_table.shape[1]
    head_size = queries.shape[1] // head_count
    key_heads = key_rows.reshape(length, head_count, head_size)
    value_heads = value_rows.reshape(length, head_count, head_size)
    key_places = jnp.arange(length, dtype=jnp.int32)

    @jax.checkpoint
    def attend_block(anchor):
        query_blk = lax.dynamic_slice_in_dim(queries, anchor, block_rows, 0).reshape(block_rows, head_count, head_size)
        seg_q = lax.dynamic_slice_in_dim(segments, anchor, block_rows, 0)
        query_places = anchor + jnp.arange(block_rows, dtype=jnp.int32)
        offset = key_places[None, :] - query_places[:, None]
        bias_blk = jnp.take(bias_table, bucket_of(offset, bias_table.shape[0] // 2), axis=0)
        products = jnp.einsum('qhd,khd->hqk', query_blk, key_heads, precision=highest)
        scores = products + jnp.transpose(bias_blk, (2, 0, 1))
        allowed = seg_q[:, None] == segments[None, :]
        scores = low_back(jnp.where(allowed[None], scores, masked_score))
        row_max = lax.optimization_barrier(jnp.max(scores, axis=-1, keepdims=True))
        exp_scores = jnp.exp(scores - row_max)
        probs = exp_scores / lax.optimization_barrier(jnp.sum(exp_scores, axis=-1, keepdims=True))
        context = jnp.einsum('hqk,khd->qhd', low(probs), value_heads, precision=highest)
        return context.reshape(block_rows, head_count * head_size)
    anchors = jnp.arange(length // block_rows, dtype=jnp.int32) * block_rows
    return lax.map(attend_block, anchors).reshape(length, head_count * head_size)

def encoder_layer(inputs, gain_attn, w_query, w_key, w_value, w_out, gain_ffn, w_gate, w_up, w_down, bias_table, segment_ids):
    normed = low(rms_norm(inputs, gain_attn))
    queries = low(low_back(project(normed, w_query)))
    key_rows = low(low_back(project(normed, w_key)))
    value_rows = low(low_back(project(normed, w_value)))

    def row_attention(row_items):
        return attend_row(row_items[0], row_items[1], row_items[2], row_items[3], bias_table)
    context = lax.map(row_attention, (queries, key_rows, value_rows, segment_ids))
    context = low(low_back(context))
    middle = inputs + low_back(project(context, w_out))
    normed_ffn = low(rms_norm(middle, gain_ffn))
    gate_pre = low_back(project(normed_ffn, w_gate))
    up_pre = low_back(project(normed_ffn, w_up))
    hidden = low(jax.nn.gelu(gate_pre, approximate=True) * up_pre)
    return middle + low_back(project(hidden, w_down))

def reference(inputs, segment_ids, gain_attn, w_query, w_key, w_value, w_out, gain_ffn, w_gate, w_up, w_down, bias_table, cotangent):
    primals = (inputs.astype(jnp.float32), gain_attn.astype(jnp.float32), w_query.astype(jnp.float32), w_key.astype(jnp.float32), w_value.astype(jnp.float32), w_out.astype(jnp.float32), gain_ffn.astype(jnp.float32), w_gate.astype(jnp.float32), w_up.astype(jnp.float32), w_down.astype(jnp.float32), bias_table.astype(jnp.float32))

    def layer_call(*weights):
        return encoder_layer(*weights, segment_ids)
    output, pullback = jax.vjp(layer_call, *primals)
    gradients = pullback(cotangent.astype(jnp.float32))
    return (output.astype(jnp.bfloat16), gradients[0], gradients[1], gradients[2], gradients[3], gradients[4], gradients[5], gradients[6], gradients[7], gradients[8], gradients[9], gradients[10])
```

```python
import functools

import jax
import jax.numpy as jnp
import numpy as np
from jax import lax
from jax.experimental import pallas as pl
from jax.experimental.pallas import tpu as pltpu
from jax.sharding import PartitionSpec as P

cutoffs = (1, 2, 3, 4, 5, 6, 7, 8, 12, 16, 23, 32, 46, 64, 91)
epsilon = 1e-06
masked_score = -1000000000.0
highest = lax.Precision.HIGHEST
axes = ("narrow", "wide")
groups = 4
bf16 = jnp.bfloat16
f32 = jnp.float32


def dot(left, right, left_dim, right_dim):
    return lax.dot_general(
        left, right, (((left_dim,), (right_dim,)), ((), ())), preferred_element_type=f32
    )


class Layout:
    def __init__(self, narrow, wide):
        self.narrow = narrow
        self.wide = wide
        self.s_count = wide // (groups * 2)

    def index(self, x, c, g, s, y):
        return (x * 2 + c) * self.wide + (g * self.s_count + s) * 2 + y

    def send(self, block, target):
        route = []
        for x in range(self.narrow // 2):
            for c in range(2):
                for g in range(groups):
                    for s in range(self.s_count):
                        for y in range(2):
                            route.append(
                                (self.index(x, c, g, s, y), self.index(*target(x, c, g, s, y)))
                            )
        return lax.ppermute(block, axes, route)

    def turned(self, block, d):
        return self.send(block, lambda x, c, g, s, y: (x, y, g ^ d, s, c))

    def core(self, block):
        return self.send(block, lambda x, c, g, s, y: (x, 1 - c, g, s, y))

    def across(self, block):
        return self.send(block, lambda x, c, g, s, y: (x ^ 1, c, g, s, y))

    def wide_bit(self, block, bit):
        def target(x, c, g, s, y):
            w = ((g * self.s_count + s) * 2 + y) ^ (1 << bit)
            return (x, c, w // (2 * self.s_count), (w // 2) % self.s_count, w % 2)

        return self.send(block, target)


def rms_scale(values):
    return lax.rsqrt(jnp.mean(values * values, axis=-1, keepdims=True) + epsilon)


def offsets_onehot(span, bucket_count):
    offset = np.arange(span) - span // 2
    distance = np.abs(offset)
    bucket = sum((distance >= cutoff).astype(np.int32) for cutoff in cutoffs)
    bucket = bucket + bucket_count // 2 * (offset > 0)
    return jnp.asarray(bucket[:, None] == np.arange(bucket_count)[None, :], f32)


def forward_kernel(place, *refs, blocks, chunk):
    own = refs[0:4]
    other = refs[4:8]
    gain_ref, weight_ref, bias_ref = refs[8:11]
    ctx = refs[11:15]
    normed_ref, q_ref, k_ref, v_ref, o_ref, p_hbm = refs[15:21]
    normed_scr, kv_scr, segk, strip, s_scr, p_scr, sems = refs[21:28]
    group, core = place[0], place[1]
    s_own = place[2]
    s_count = own[0].shape[0]
    tok = 128
    width = gain_ref.shape[1]
    head_size = 64
    seq = blocks * tok
    chunks = seq // chunk

    def block_of(d, e, k):
        return (((group ^ d) * s_count + (s_own ^ e)) * 2) + (core if k == 0 else 1 - core)

    def load_chunk(e):
        for k in range(2):
            for d in range(4):
                raw = (own, other)[k][d][e]
                values = raw[:tok, :].astype(f32)
                low = (values * rms_scale(values) * gain_ref[...]).astype(bf16)
                slot = k * 4 + d
                normed_scr[slot * tok : (slot + 1) * tok, :] = low
                start = pl.multiple_of(block_of(d, e, k) * tok, tok)
                segk[0:1, pl.ds(start, tok)] = raw[tok : tok + 1, :tok].astype(f32)
        kv_scr[...] = jnp.dot(
            normed_scr[...], weight_ref[:, width // 4 :], preferred_element_type=f32
        ).astype(bf16)
        for k in range(2):
            for d in range(4):
                slot = k * 4 + d
                start = pl.multiple_of(block_of(d, e, k) * tok, tok)
                rows = kv_scr[slot * tok : (slot + 1) * tok, :]
                k_ref[pl.ds(start, tok), :] = rows[:, : width // 4]
                v_ref[pl.ds(start, tok), :] = rows[:, width // 4 :]

    load_chunk(0)
    normed_ref[...] = normed_scr[: 4 * tok, :]
    q_ref[...] = jnp.dot(
        normed_ref[...], weight_ref[:, : width // 4], preferred_element_type=f32
    ).astype(bf16)
    if s_count > 1:

        @pl.loop(1, s_count)
        def _(e):
            load_chunk(e)

    def p_copy(slot, h, d):
        return pltpu.make_async_copy(
            p_scr.at[slot], p_hbm.at[h, :, pl.ds(d * tok, tok), :], sems.at[slot]
        )

    heads = width // groups // head_size
    rows_at_once = 32
    pending = {}
    for h in range(heads):
        cols = slice(h * head_size, (h + 1) * head_size)
        spread = jnp.broadcast_to(bias_ref[h : h + 1, :], (tok, bias_ref.shape[1]))
        near = pltpu.roll(spread, 0, 1, stride=1, stride_axis=0)
        strip[:, tok * (blocks - 2) : tok * (blocks + 1)] = near[:, tok : 4 * tok]
        strip[:, : tok * (blocks - 2)] = jnp.broadcast_to(
            bias_ref[h : h + 1, :1], (tok, tok * (blocks - 2))
        )
        strip[:, tok * (blocks + 1) :] = jnp.broadcast_to(
            bias_ref[h : h + 1, bias_ref.shape[1] - 1 :], (tok, tok * (blocks - 2))
        )
        for d in range(4):
            query_block = block_of(d, 0, 0)
            strip_base = tok * (blocks - 1) - query_block * tok
            seg_row = own[d][0][tok : tok + 1, :tok].astype(f32)
            seg_col = jnp.transpose(jnp.broadcast_to(seg_row, (tok, tok)))[:, :1]
            slot = (h * 4 + d) % 2
            if slot in pending:
                pending.pop(slot).wait()
            queries = q_ref[d * tok : (d + 1) * tok, cols]
            if chunks == 1:
                s_scr[slot] = dot(queries, k_ref[:, cols], 1, 1)
                for r in range(0, tok, rows_at_once):
                    rows = slice(r, r + rows_at_once)
                    bias = strip[rows, pl.ds(pl.multiple_of(strip_base, tok), seq)]
                    scores = s_scr[slot, rows, :] + bias
                    scores = jnp.where(seg_col[rows] == segk[0:1, :], scores, masked_score)
                    top = jnp.max(scores, axis=1, keepdims=True)
                    exps = jnp.exp(scores - top)
                    total = jnp.sum(exps, axis=1, keepdims=True)
                    p_scr[slot, 0, rows, :] = (exps * (1.0 / total)).astype(bf16)
                weighted = jnp.dot(
                    p_scr[slot, 0], v_ref[:, cols], preferred_element_type=f32
                )
            else:
                def score_chunk(i, top):
                    start = pl.multiple_of(i * chunk, chunk)
                    scores = dot(queries, k_ref[pl.ds(start, chunk), cols], 1, 1)
                    base = pl.multiple_of(strip_base + start, tok)
                    scores = scores + strip[:, pl.ds(base, chunk)]
                    same = seg_col == segk[0:1, pl.ds(start, chunk)]
                    scores = jnp.where(same, scores, masked_score)
                    s_scr[0, :, pl.ds(start, chunk)] = scores
                    return jnp.maximum(top, jnp.max(scores, axis=1, keepdims=True))

                top = lax.fori_loop(
                    0, chunks, score_chunk, jnp.full((tok, 1), -3e38, f32)
                )

                def exp_chunk(i, total):
                    start = pl.multiple_of(i * chunk, chunk)
                    exps = jnp.exp(s_scr[0, :, pl.ds(start, chunk)] - top)
                    s_scr[0, :, pl.ds(start, chunk)] = exps
                    return total + jnp.sum(exps, axis=1, keepdims=True)

                total = lax.fori_loop(0, chunks, exp_chunk, jnp.zeros((tok, 1), f32))
                inverse = 1.0 / total

                def weigh_chunk(i, weighted):
                    start = pl.multiple_of(i * chunk, chunk)
                    low = (s_scr[0, :, pl.ds(start, chunk)] * inverse).astype(bf16)
                    p_scr[slot, i] = low
                    return weighted + jnp.dot(
                        low, v_ref[pl.ds(start, chunk), cols], preferred_element_type=f32
                    )

                weighted = lax.fori_loop(
                    0, chunks, weigh_chunk, jnp.zeros((tok, head_size), f32)
                )
            copy = p_copy(slot, h, d)
            copy.start()
            pending[slot] = copy
            o_ref[d * tok : (d + 1) * tok, cols] = weighted
            ctx[d][:, cols] = weighted.astype(bf16)
    for copy in pending.values():
        copy.wait()


def backward_kernel(place, *refs, blocks, chunk):
    dctx = refs[0:4]
    q_ref, k_ref, v_ref, o_ref, p_hbm = refs[4:9]
    dq = refs[9:13]
    keep_ref, send_ref, table_ref = refs[13:16]
    p_scr, ds_scr, dctx_scr, strip, dq_scr, kv_scr, sems = refs[16:23]
    group, core, s_own = place[0], place[1], place[2]
    tok = 128
    head_size = 64
    seq = blocks * tok
    chunks = seq // chunk
    heads = q_ref.shape[1] // head_size
    s_count = blocks // 8

    def p_copy(h, i, slot):
        return pltpu.make_async_copy(p_hbm.at[h, i], p_scr.at[slot], sems.at[slot])

    p_copy(0, 0, 0).start()
    for d in range(4):
        dctx_scr[d * tok : (d + 1) * tok, :] = dctx[d][...]
    rows_at_once = 32
    for h in range(heads):
        cols = slice(h * head_size, (h + 1) * head_size)
        strip[...] = jnp.zeros_like(strip)
        out_grad = dctx_scr[:, cols]
        delta = jnp.sum(out_grad.astype(f32) * o_ref[:, cols], axis=1, keepdims=True)

        def run_chunk(i, h=h, cols=cols, out_grad=out_grad, delta=delta):
            start = pl.multiple_of(i * chunk, chunk)
            slot = (h * chunks + i) % 2
            following = h * chunks + i + 1

            @pl.when(following < heads * chunks)
            def _():
                p_copy(following // chunks, following % chunks, 1 - slot).start()

            p_copy(h, i, slot).wait()
            keys = k_ref[pl.ds(start, chunk), cols]
            values = v_ref[pl.ds(start, chunk), cols]
            for d in range(4):
                query_block = ((group ^ d) * s_count + s_own) * 2 + core
                base = pl.multiple_of(tok * (blocks - 1) - query_block * tok + start, tok)
                prob_grad = dot(out_grad[d * tok : (d + 1) * tok], values, 1, 1)
                for r in range(0, tok, rows_at_once):
                    rows = slice(d * tok + r, d * tok + r + rows_at_once)
                    here = prob_grad[r : r + rows_at_once] - delta[rows]
                    low = (p_scr[slot, rows, :].astype(f32) * here).astype(bf16)
                    ds_scr[rows, :] = low
                    strip[r : r + rows_at_once, pl.ds(base, chunk)] += low.astype(f32)
            scores_grad = ds_scr[...]
            part = jnp.dot(scores_grad, keys, preferred_element_type=f32)
            if chunks == 1:
                dq_scr[:, cols] = part
            else:
                dq_scr[:, cols] += part
            queries = q_ref[:, cols]
            kv_scr[0, pl.ds(start, chunk), :] = dot(scores_grad, queries, 0, 0).astype(bf16)
            kv_scr[1, pl.ds(start, chunk), :] = dot(p_scr[slot], out_grad, 0, 0).astype(bf16)

        if chunks == 1:
            run_chunk(0)
        else:
            dq_scr[:, cols] = jnp.zeros((4 * tok, head_size), f32)
            pl.loop(0, chunks)(run_chunk)

        def place_rows(e, h=h, cols=cols):
            for d in range(4):
                for k, target in ((0, keep_ref), (1, send_ref)):
                    block = ((group ^ d) * s_count + (s_own ^ e)) * 2 + (core if k == 0 else 1 - core)
                    start = pl.multiple_of(block * tok, tok)
                    width = heads * head_size
                    target[e, d, :, cols] = kv_scr[0, pl.ds(start, tok), :]
                    shifted = slice(width + h * head_size, width + (h + 1) * head_size)
                    target[e, d, :, shifted] = kv_scr[1, pl.ds(start, tok), :]

        if s_count == 1:
            place_rows(0)
        else:
            pl.loop(0, s_count)(place_rows)
        near = strip[:, tok * (blocks - 2) : tok * (blocks + 1)]
        left = jnp.zeros((1, tok), f32)
        right = jnp.zeros((1, tok), f32)
        for t in range(blocks - 2):
            left = left + jnp.sum(strip[:, t * tok : (t + 1) * tok], axis=0, keepdims=True)
            far = (blocks + 1 + t) * tok
            right = right + jnp.sum(strip[:, far : far + tok], axis=0, keepdims=True)
        table_ref[h : h + 1, :] = jnp.concatenate([left, jnp.zeros((1, 2 * tok), f32), right], axis=1)
        spread = jnp.concatenate([jnp.zeros((tok, tok), f32), near], axis=1)
        skewed = spread[:8]
        for j in range(1, tok // 8):
            skewed = skewed + pltpu.roll(spread[8 * j : 8 * j + 8], 4 * tok - 8 * j, 1)
        row = lax.broadcasted_iota(jnp.int32, skewed.shape, 0)
        for step in (1, 2, 4):
            moved = pltpu.roll(skewed, 4 * tok - step, 1)
            skewed = jnp.where((row & step) != 0, moved, skewed)
        table_ref[h : h + 1, :] += jnp.sum(skewed, axis=0, keepdims=True)
    for d in range(4):
        dq[d][...] = dq_scr[d * tok : (d + 1) * tok, :].astype(bf16)


def vmem(count):
    return [pl.BlockSpec(memory_space=pltpu.VMEM)] * count


def attention_forward(place, own, other, gain, weight, bias):
    s_count, rows, width = own[0].shape
    tok = 128
    blocks = 8 * s_count
    seq = blocks * tok
    chunk = min(seq, 1024)
    local = width // groups
    shapes = (
        [jax.ShapeDtypeStruct((tok, local), bf16)] * 4
        + [jax.ShapeDtypeStruct((4 * tok, width), bf16)]
        + [jax.ShapeDtypeStruct((4 * tok, local), bf16)]
        + [jax.ShapeDtypeStruct((seq, local), bf16)] * 2
        + [jax.ShapeDtypeStruct((4 * tok, local), f32)]
        + [jax.ShapeDtypeStruct((local // 64, seq // chunk, 4 * tok, chunk), bf16)]
    )
    return pl.pallas_call(
        functools.partial(forward_kernel, blocks=blocks, chunk=chunk),
        out_shape=shapes,
        in_specs=[pl.BlockSpec(memory_space=pltpu.SMEM)] + vmem(11),
        out_specs=vmem(9) + [pl.BlockSpec(memory_space=pl.ANY)],
        scratch_shapes=[
            pltpu.VMEM((8 * tok, width), bf16),
            pltpu.VMEM((8 * tok, 2 * local), bf16),
            pltpu.VMEM((8, seq), f32),
            pltpu.VMEM((tok, (2 * blocks - 1) * tok), f32),
            pltpu.VMEM((2 if seq == chunk else 1, tok, seq), f32),
            pltpu.VMEM((2, seq // chunk, tok, chunk), bf16),
            pltpu.SemaphoreType.DMA((2,)),
        ],
        compiler_params=pltpu.CompilerParams(vmem_limit_bytes=60 * 2**20),
        name="attention_forward",
    )(place, *own, *other, gain, weight, bias)


def attention_backward(place, dctx, q, k, v, o, p):
    tok, local = dctx[0].shape
    seq = k.shape[0]
    blocks = seq // tok
    s_count = blocks // 8
    chunk = p.shape[3]
    heads = local // 64
    shapes = (
        [jax.ShapeDtypeStruct((tok, local), bf16)] * 4
        + [jax.ShapeDtypeStruct((s_count, 4, tok, 2 * local), bf16)] * 2
        + [jax.ShapeDtypeStruct((heads, 4 * tok), f32)]
    )
    return pl.pallas_call(
        functools.partial(backward_kernel, blocks=blocks, chunk=chunk),
        out_shape=shapes,
        in_specs=[pl.BlockSpec(memory_space=pltpu.SMEM)]
        + vmem(8)
        + [pl.BlockSpec(memory_space=pl.ANY)],
        out_specs=vmem(7),
        scratch_shapes=[
            pltpu.VMEM((2, 4 * tok, chunk), bf16),
            pltpu.VMEM((4 * tok, chunk), bf16),
            pltpu.VMEM((4 * tok, local), bf16),
            pltpu.VMEM((tok, (2 * blocks - 1) * tok), f32),
            pltpu.VMEM((4 * tok, local), f32),
            pltpu.VMEM((2, seq, 64), bf16),
            pltpu.SemaphoreType.DMA((2,)),
        ],
        compiler_params=pltpu.CompilerParams(vmem_limit_bytes=60 * 2**20),
        name="attention_backward",
    )(place, *dctx, q, k, v, o, p)


def halved(block, axis, keep):
    return (
        lax.dynamic_index_in_dim(block, keep, axis, keepdims=False),
        lax.dynamic_index_in_dim(block, 1 - keep, axis, keepdims=False),
    )


def wide_scatter(layout, grad, wide_index):
    rows, columns = grad.shape
    remaining = layout.wide
    block = rows // remaining
    current = grad.reshape(remaining, block, columns)
    bit = 0
    while remaining > 1:
        remaining //= 2
        current = current.reshape(remaining, 2, block, columns)
        kept, sent = halved(current, 1, (wide_index >> bit) & 1)
        received = layout.wide_bit(sent.astype(bf16), bit)
        current = kept.astype(f32) + received.astype(f32)
        bit += 1
    return current.reshape(block, columns)


def on_device(
    inputs,
    segment_ids,
    gain_attn,
    w_query,
    w_key,
    w_value,
    w_out,
    gain_ffn,
    w_gate,
    w_up,
    w_down,
    bias_table,
    cotangent,
):
    layout = Layout(lax.axis_size("narrow"), lax.axis_size("wide"))
    s_count = layout.s_count
    tokens = inputs[0]
    tok, width = tokens.shape
    local = width // groups
    bucket_count, head_count = bias_table.shape
    heads = head_count // groups
    narrow = lax.axis_index("narrow")
    wide = lax.axis_index("wide")
    core = narrow % 2
    across = narrow // 2
    group = wide // (2 * s_count)
    s_own = (wide // 2) % s_count
    y_own = wide % 2
    place = jnp.stack([group, core, s_own, y_own]).astype(jnp.int32)

    extra = jnp.pad(segment_ids.astype(bf16), ((0, 15), (0, width - tok)))
    packed = jnp.concatenate([tokens, extra], axis=0)
    own = []
    for d in range(4):
        block = layout.turned(packed, d)[None]
        size = 1
        while size < s_count:
            block = jnp.concatenate(
                [block, layout.wide_bit(block, size.bit_length())], axis=0
            )
            size *= 2
        own.append(block)
    other = [layout.core(block) for block in own]

    def group_cols(weight, d):
        return lax.dynamic_slice_in_dim(weight, (group ^ d) * local, local, 1)

    w_qkv = [
        jnp.concatenate([group_cols(w, d) for w in (w_query, w_key, w_value)], axis=1)
        for d in range(4)
    ]
    w_out_turned = jnp.concatenate(
        [lax.dynamic_slice_in_dim(w_out, (group ^ d) * local, local, 0) for d in range(4)], axis=0
    )
    onehot = offsets_onehot(4 * tok, bucket_count)
    own_table = lax.dynamic_slice_in_dim(bias_table, group * heads, heads, 1)
    bias = jnp.einsum("bh,mb->hm", own_table, onehot, precision=highest)

    outs = attention_forward(place, own, other, gain_attn[None], w_qkv[0], bias)
    ctx_parts, normed_own, q_own, k_all, v_all, o_own, probs = (
        outs[:4],
        outs[4],
        outs[5],
        outs[6],
        outs[7],
        outs[8],
        outs[9],
    )
    context = jnp.concatenate([layout.turned(ctx_parts[d], d) for d in range(4)], axis=1)

    input_f32 = tokens.astype(f32)
    middle = input_f32 + dot(context, w_out_turned, 1, 0)
    scale_mid = rms_scale(middle)
    normed_ffn = (middle * scale_mid * gain_ffn).astype(bf16)
    gate_pre = dot(normed_ffn, w_gate, 1, 0)
    up_pre = dot(normed_ffn, w_up, 1, 0)
    activated, gelu_back = jax.vjp(lambda v: jax.nn.gelu(v, approximate=True), gate_pre)
    hidden = (activated * up_pre).astype(bf16)
    output = (middle + dot(hidden, w_down, 1, 0)).astype(bf16)
    out_grad = cotangent[0]
    hidden_grad = dot(out_grad, w_down, 1, 1)
    gate_grad = gelu_back(hidden_grad * up_pre)[0].astype(bf16)
    up_grad = (hidden_grad * activated).astype(bf16)
    normed_ffn_grad = dot(gate_grad, w_gate, 1, 1) + dot(up_grad, w_up, 1, 1)
    scaled = normed_ffn_grad * gain_ffn
    middle_grad = (
        out_grad.astype(f32)
        + scale_mid * scaled
        - middle * scale_mid**3 * jnp.mean(middle * scaled, axis=-1, keepdims=True)
    )
    grad_gain_ffn = jnp.sum(normed_ffn_grad * middle * scale_mid, axis=0)
    attn_grad = middle_grad.astype(bf16)
    context_grad = dot(attn_grad, w_out_turned, 1, 1).astype(bf16)
    dctx = [
        layout.turned(context_grad[:, d * local : (d + 1) * local], d) for d in range(4)
    ]

    ff = w_gate.shape[1]

    def half_cols(block, which):
        return lax.dynamic_slice_in_dim(block, which * (block.shape[1] // 2), block.shape[1] // 2, 1)

    def from_narrow(full, split):
        full_width = sum(f.shape[1] for f in full)
        message = jnp.concatenate([*full, *[half_cols(b, 1 - across) for b in split]], axis=1)
        received = layout.across(message)
        mine_full = jnp.concatenate([*full], axis=1) if full else None
        kept = [half_cols(b, across) for b in split]
        at = full_width
        theirs = []
        for b in kept:
            theirs.append(received[:, at : at + b.shape[1]])
            at += b.shape[1]
        both = [jnp.concatenate([a, b], axis=0) for a, b in zip(kept, theirs)]
        pieces = [half_cols(b, 1 - core) for b in both]
        if full:
            both_full = jnp.concatenate([mine_full, received[:, :full_width]], axis=0)
            pieces = [both_full] + pieces
        swapped = layout.core(jnp.concatenate(pieces, axis=1))
        at = 0
        gathered_full = []
        if full:
            whole = jnp.concatenate([both_full, swapped[:, :full_width]], axis=0)
            for f in full:
                gathered_full.append(whole[:, at : at + f.shape[1]])
                at += f.shape[1]
        gathered = []
        for b in both:
            quarter = b.shape[1] // 2
            gathered.append(
                jnp.concatenate([half_cols(b, core), swapped[:, at : at + quarter]], axis=0)
            )
            at += quarter
        return gathered_full, gathered

    (all_normed, all_context, all_hidden), (all_cot,) = from_narrow(
        [normed_ffn, context, hidden], [out_grad]
    )
    part_down = dot(all_hidden, all_cot, 0, 0)
    unused, (all_gate, all_up, all_attn) = from_narrow([], [gate_grad, up_grad, attn_grad])
    part_ffn = dot(all_normed, jnp.concatenate([all_gate, all_up], axis=1), 0, 0)
    part_out = dot(all_context, all_attn, 0, 0)
    row_groups = [
        lax.dynamic_slice_in_dim(part_out, (group ^ d) * local, local, 0) for d in range(4)
    ]
    part_out = jnp.concatenate(row_groups, axis=0)
    final_down = wide_scatter(layout, part_down, wide)
    final_rest = wide_scatter(layout, jnp.concatenate([part_ffn, part_out], axis=1), wide)
    quarter_ff = ff // layout.narrow
    final_gate = final_rest[:, :quarter_ff]
    final_up = final_rest[:, quarter_ff : 2 * quarter_ff]
    final_out = final_rest[:, 2 * quarter_ff :]

    back = attention_backward(place, dctx, q_own, k_all, v_all, o_own, probs)
    dq, kv_keep, kv_send, table_rows = back[:4], back[4], back[5], back[6]
    kv = kv_keep.astype(f32) + layout.core(kv_send).astype(f32)
    size = s_count
    while size > 1:
        size //= 2
        kv = kv[:size] + layout.wide_bit(kv[size:].astype(bf16), size.bit_length()).astype(f32)
    kv = kv.astype(bf16)[0]
    low_grads = [jnp.concatenate([dq[d], kv[d]], axis=1) for d in range(4)]
    returned = [layout.turned(low_grads[d], d) for d in range(4)]

    qkv_grad = jnp.concatenate(low_grads, axis=0)
    part = dot(normed_own, qkv_grad, 0, 0).astype(f32)
    x_count = layout.narrow // 2
    rows = width // layout.wide
    part = part.reshape(x_count, 2, s_count, 2, rows, 3 * local)
    kept, sent = halved(part, 1, core)
    part = kept + layout.core(sent.astype(bf16)).astype(f32)
    kept, sent = halved(part, 2, y_own)
    part = kept + layout.wide_bit(sent.astype(bf16), 0).astype(f32)
    kept, sent = halved(part, 0, across)
    part = kept + layout.across(sent.astype(bf16)).astype(f32)
    size = s_count
    bit = 1
    while size > 1:
        size //= 2
        part = part.reshape(size, 2, rows, 3 * local)
        kept, sent = halved(part, 1, (s_own >> (bit - 1)) & 1)
        part = kept + layout.wide_bit(sent.astype(bf16), bit).astype(f32)
        bit += 1
    part = part.reshape(rows, 3 * local).astype(bf16)
    final_qkv = layout.send(part, lambda x, c, g, s, y: (g // 2, g % 2, x * 2 + c, s, y)).astype(f32)

    x_own = jnp.concatenate([block[0, :tok] for block in own], axis=0).astype(f32)
    part_normed_grad = dot(qkv_grad, w_qkv[0], 1, 1)
    grad_gain_attn = jnp.sum(part_normed_grad * x_own * rms_scale(x_own), axis=0)
    own_table_grad = jnp.einsum("hm,mb->bh", table_rows, onehot, precision=highest)
    table_grad = lax.dynamic_update_slice_in_dim(
        jnp.zeros_like(bias_table), own_table_grad, group * heads, 1
    )
    small = jnp.concatenate([grad_gain_attn, grad_gain_ffn, table_grad.reshape(-1)])
    small = small.reshape(-1, 128)
    small = small + layout.core(small)
    small = small + layout.across(small)
    for bit in range(layout.wide.bit_length() - 1):
        small = small + layout.wide_bit(small, bit)
    small = small.reshape(-1)
    sum_gain_attn = small[:width]
    sum_gain_ffn = small[width : 2 * width]
    sum_table = small[2 * width :].reshape(bias_table.shape)

    normed_grad = dot(returned[0], w_qkv[0], 1, 1)
    for d in range(1, 4):
        normed_grad = normed_grad + dot(returned[d], w_qkv[d], 1, 1)
    scale_in = rms_scale(input_f32)
    scaled_in = normed_grad * gain_attn
    input_grad = (
        middle_grad
        + scale_in * scaled_in
        - input_f32 * scale_in**3 * jnp.mean(input_f32 * scaled_in, axis=-1, keepdims=True)
    )
    return (
        output[None],
        input_grad[None],
        sum_gain_attn,
        final_qkv[:, :local],
        final_qkv[:, local : 2 * local],
        final_qkv[:, 2 * local :],
        final_out,
        sum_gain_ffn,
        final_gate,
        final_up,
        final_down,
        sum_table,
    )


def solution(mesh):
    tokens = P("narrow", "wide", None)
    share = P("wide", "narrow")
    return jax.shard_map(
        on_device,
        mesh=mesh,
        in_specs=(tokens, P("narrow", "wide")) + (P(),) * 10 + (tokens,),
        out_specs=(
            tokens,
            tokens,
            P(),
            share,
            share,
            share,
            share,
            P(),
            share,
            share,
            share,
            P(),
        ),
        check_vma=False,
    )
```

```python
import functools

import jax
import jax.numpy as jnp
import numpy as np
from jax import lax
from jax.experimental import pallas as pl
from jax.experimental.pallas import tpu as pltpu
from jax.sharding import PartitionSpec as P

cutoffs = (1, 2, 3, 4, 5, 6, 7, 8, 12, 16, 23, 32, 46, 64, 91)
epsilon = 1e-06
masked_score = -1000000000.0
highest = lax.Precision.HIGHEST
axes = ("narrow", "wide")
groups = 4
bf16 = jnp.bfloat16
f32 = jnp.float32


def dot(left, right, left_dim, right_dim):
    return lax.dot_general(
        left, right, (((left_dim,), (right_dim,)), ((), ())), preferred_element_type=f32
    )


class Layout:
    def __init__(self, narrow, wide):
        self.narrow = narrow
        self.wide = wide
        self.s_count = wide // (groups * 2)

    def index(self, x, c, g, s, y):
        return (x * 2 + c) * self.wide + (g * self.s_count + s) * 2 + y

    def send(self, block, target):
        route = []
        for x in range(self.narrow // 2):
            for c in range(2):
                for g in range(groups):
                    for s in range(self.s_count):
                        for y in range(2):
                            route.append(
                                (self.index(x, c, g, s, y), self.index(*target(x, c, g, s, y)))
                            )
        return lax.ppermute(block, axes, route)

    def turned(self, block, d):
        return self.send(block, lambda x, c, g, s, y: (x, y, g ^ d, s, c))

    def core(self, block):
        return self.send(block, lambda x, c, g, s, y: (x, 1 - c, g, s, y))

    def across(self, block):
        return self.send(block, lambda x, c, g, s, y: (x ^ 1, c, g, s, y))

    def wide_bit(self, block, bit):
        def target(x, c, g, s, y):
            w = ((g * self.s_count + s) * 2 + y) ^ (1 << bit)
            return (x, c, w // (2 * self.s_count), (w // 2) % self.s_count, w % 2)

        return self.send(block, target)


def rms_scale(values):
    return lax.rsqrt(jnp.mean(values * values, axis=-1, keepdims=True) + epsilon)


def bucket_row(span, half_count):
    offset = lax.broadcasted_iota(jnp.int32, (1, span), 1) - span // 2
    distance = jnp.abs(offset)
    bucket = jnp.where(offset > 0, half_count, 0)
    for cutoff in cutoffs:
        bucket = bucket + jnp.where(distance >= cutoff, 1, 0)
    return bucket


def cost(microseconds):
    return pl.CostEstimate(
        flops=int(microseconds * 1.15e9), bytes_accessed=1024, transcendentals=0
    )


def kernel_call(
    body, name, smem, inputs, outputs, scratch=(), in_hbm=(), staged=(), mebibytes=4, us=3
):
    n_smem, n_in, n_out = len(smem), len(inputs), len(outputs)

    def kernel(*refs):
        given = refs[n_smem : n_smem + n_in]
        outs = refs[n_smem + n_in : n_smem + n_in + n_out]
        rest = refs[n_smem + n_in + n_out :]
        buffers = dict(zip(staged, rest[: len(staged)]))
        arrivals = {}
        for at, i in enumerate(staged):
            arrivals[i] = pltpu.make_async_copy(given[i], buffers[i], rest[-1].at[at])
            arrivals[i].start()

        def get(i):
            if i in arrivals:
                arrivals.pop(i).wait()
            return buffers.get(i, given[i])

        body(refs[:n_smem], get, outs, *rest[len(staged) : len(rest) - (1 if staged else 0)])
        for i in staged:
            get(i)

    hbm = pl.BlockSpec(memory_space=pltpu.HBM)
    vmem = pl.BlockSpec(memory_space=pltpu.VMEM)
    copies = [pltpu.SemaphoreType.DMA((len(staged),))] if staged else []
    return pl.pallas_call(
        kernel,
        out_shape=outputs,
        in_specs=[pl.BlockSpec(memory_space=pltpu.SMEM)] * n_smem
        + [hbm if i in in_hbm or i in staged else vmem for i in range(n_in)],
        out_specs=[hbm if ("out", i) in in_hbm else vmem for i in range(n_out)],
        scratch_shapes=[pltpu.VMEM(inputs[i].shape, inputs[i].dtype) for i in staged]
        + list(scratch)
        + copies,
        compiler_params=pltpu.CompilerParams(vmem_limit_bytes=mebibytes * 2**20),
        cost_estimate=cost(us),
        name=name,
    )(*smem, *inputs)


def shaped(dtype, *shape):
    return jax.ShapeDtypeStruct(shape, dtype)


def group_window(group, local):
    start = (group * local) // 128 * 128
    return pl.multiple_of(start, 128), (group * local) % 128 != 0


def pack_body(smem, get, outs, sems):
    tokens_ref, segment_ref = get(0), get(1)
    packet, spare = outs[0], sems[0]
    tok, width = tokens_ref.shape
    copy = pltpu.make_async_copy(tokens_ref, packet.at[pl.ds(0, tok)], sems[1].at[0])
    copy.start()
    row = jnp.broadcast_to(segment_ref[...].astype(f32), (spare.shape[0], tok))
    spare[:, :tok] = row.astype(bf16)
    spare[:, tok:] = jnp.zeros((spare.shape[0], width - tok), bf16)
    more = pltpu.make_async_copy(spare, packet.at[pl.ds(tok, spare.shape[0])], sems[1].at[1])
    more.start()
    more.wait()
    copy.wait()


def packed(tokens, segment_ids):
    tok, width = tokens.shape
    return kernel_call(
        lambda smem, get, outs, *scratch: pack_body(smem, get, outs, scratch),
        "pack",
        [],
        [tokens, segment_ids],
        [shaped(bf16, tok + 16, width)],
        scratch=[pltpu.VMEM((16, width), bf16), pltpu.SemaphoreType.DMA((2,))],
        in_hbm=(0, ("out", 0)),
        staged=(1,),
        mebibytes=2,
        us=1,
    )[0]


def bias_body(smem, get, outs):
    place, table = smem
    (rows_ref,) = outs
    span = rows_ref.shape[1]
    heads = table.shape[1] // groups
    buckets = bucket_row(span, table.shape[0] // 2)
    for h in range(heads):
        head = place[0] * heads + h
        row = jnp.full((1, span), table[0, head], f32)
        for b in range(1, table.shape[0]):
            row = jnp.where(buckets == b, table[b, head], row)
        rows_ref[h : h + 1, :] = row


def bias_rows(place, table, span):
    return kernel_call(bias_body, "bias_rows", [place, table], [], [shaped(f32, 8, span)], us=1)[0]


def project(place, tokens, segment_ids, gain, w_query, w_key, w_value):
    tok, width = tokens.shape
    span = -(-(3 * width // groups + 1) // 128) * 128
    return kernel_call(
        project_body,
        "project",
        [place],
        [tokens, segment_ids, gain, w_query, w_key, w_value],
        [shaped(bf16, tok, span)] * 4 + [shaped(bf16, tok, width)],
        scratch=[pltpu.VMEM((3, tok, width), bf16)],
        staged=(0, 1, 3, 4, 5),
        mebibytes=10,
        us=4,
    )


def forward_body(
    smem, get, outs, weight_scr, normed_scr, kv_scr, segk, strip, s_scr, p_scr, sems, *, blocks, chunk
):
    (place,) = smem
    ctx = outs[0:4]
    q_ref, k_ref, v_ref, o_ref, normed_ref, p_hbm = outs[4:10]
    group, core, s_own = place[0], place[1], place[2]
    tok = 128
    head_size = 64
    s_count = blocks // 8
    width = normed_scr.shape[1]
    local = q_ref.shape[1]
    seq = blocks * tok
    chunks = seq // chunk
    window, late = group_window(group, local)
    for i in range(3):
        both = get(10 + i)[:, pl.ds(window, -(-local // 128) * 128)]
        weight_scr[:, i * local : (i + 1) * local] = jnp.where(
            late, both[:, both.shape[1] - local :], both[:, :local]
        )
    gain = get(9)[...]

    def block_of(d, e, k):
        return (((group ^ d) * s_count + (s_own ^ e)) * 2) + (core if k == 0 else 1 - core)

    def load_chunk(e):
        for k in range(2):
            for d in range(4):
                raw = get(k * 4 + d)
                values = raw[e, :tok, :].astype(f32)
                slot = k * 4 + d
                normed_scr[slot * tok : (slot + 1) * tok, :] = (
                    values * rms_scale(values) * gain
                ).astype(bf16)
                start = pl.multiple_of(block_of(d, e, k) * tok, tok)
                segk[0:1, pl.ds(start, tok)] = raw[e, tok : tok + 1, :tok].astype(f32)
        kv_scr[...] = dot(normed_scr[...], weight_scr[:, local:], 1, 0).astype(bf16)
        for k in range(2):
            for d in range(4):
                slot = k * 4 + d
                start = pl.multiple_of(block_of(d, e, k) * tok, tok)
                rows = kv_scr[slot * tok : (slot + 1) * tok, :]
                k_ref[pl.ds(start, tok), :] = rows[:, :local]
                v_ref[pl.ds(start, tok), :] = rows[:, local:]

    load_chunk(0)
    normed_ref[...] = normed_scr[: 4 * tok, :]
    q_ref[...] = dot(normed_scr[: 4 * tok, :], weight_scr[:, :local], 1, 0).astype(bf16)
    if s_count > 1:

        @pl.loop(1, s_count)
        def _(e):
            load_chunk(e)

    def p_copy(slot, h, d):
        return pltpu.make_async_copy(
            p_scr.at[slot], p_hbm.at[h, :, pl.ds(d * tok, tok), :], sems.at[slot]
        )

    heads = local // head_size
    rows_at_once = 32
    pending = {}
    span = 4 * tok
    for h in range(heads):
        cols = slice(h * head_size, (h + 1) * head_size)
        bias_row = get(8)[h : h + 1, :]
        spread = jnp.broadcast_to(bias_row, (tok, span))
        near = pltpu.roll(spread, 0, 1, stride=1, stride_axis=0)
        strip[:, tok * (blocks - 2) : tok * (blocks + 1)] = near[:, tok : 4 * tok]
        strip[:, : tok * (blocks - 2)] = jnp.broadcast_to(
            bias_row[:, :1], (tok, tok * (blocks - 2))
        )
        strip[:, tok * (blocks + 1) :] = jnp.broadcast_to(
            bias_row[:, span - 1 :], (tok, tok * (blocks - 2))
        )
        for d in range(4):
            query_block = block_of(d, 0, 0)
            strip_base = tok * (blocks - 1) - query_block * tok
            seg_row = get(d)[0, tok : tok + 1, :tok].astype(f32)
            seg_col = jnp.transpose(jnp.broadcast_to(seg_row, (tok, tok)))[:, :1]
            slot = (h * 4 + d) % 2
            if slot in pending:
                pending.pop(slot).wait()
            queries = q_ref[d * tok : (d + 1) * tok, cols]
            if chunks == 1:
                s_scr[slot] = dot(queries, k_ref[:, cols], 1, 1)
                for r in range(0, tok, rows_at_once):
                    rows = slice(r, r + rows_at_once)
                    bias = strip[rows, pl.ds(pl.multiple_of(strip_base, tok), seq)]
                    scores = s_scr[slot, rows, :] + bias
                    scores = jnp.where(seg_col[rows] == segk[0:1, :], scores, masked_score)
                    top = jnp.max(scores, axis=1, keepdims=True)
                    exps = jnp.exp(scores - top)
                    total = jnp.sum(exps, axis=1, keepdims=True)
                    p_scr[slot, 0, rows, :] = (exps * (1.0 / total)).astype(bf16)
                weighted = jnp.dot(
                    p_scr[slot, 0], v_ref[:, cols], preferred_element_type=f32
                )
            else:
                def score_chunk(i, top):
                    start = pl.multiple_of(i * chunk, chunk)
                    scores = dot(queries, k_ref[pl.ds(start, chunk), cols], 1, 1)
                    base = pl.multiple_of(strip_base + start, tok)
                    scores = scores + strip[:, pl.ds(base, chunk)]
                    same = seg_col == segk[0:1, pl.ds(start, chunk)]
                    scores = jnp.where(same, scores, masked_score)
                    s_scr[0, :, pl.ds(start, chunk)] = scores
                    return jnp.maximum(top, jnp.max(scores, axis=1, keepdims=True))

                top = lax.fori_loop(
                    0, chunks, score_chunk, jnp.full((tok, 1), -3e38, f32)
                )

                def exp_chunk(i, total):
                    start = pl.multiple_of(i * chunk, chunk)
                    exps = jnp.exp(s_scr[0, :, pl.ds(start, chunk)] - top)
                    s_scr[0, :, pl.ds(start, chunk)] = exps
                    return total + jnp.sum(exps, axis=1, keepdims=True)

                total = lax.fori_loop(0, chunks, exp_chunk, jnp.zeros((tok, 1), f32))
                inverse = 1.0 / total

                def weigh_chunk(i, weighted):
                    start = pl.multiple_of(i * chunk, chunk)
                    low = (s_scr[0, :, pl.ds(start, chunk)] * inverse).astype(bf16)
                    p_scr[slot, i] = low
                    return weighted + jnp.dot(
                        low, v_ref[pl.ds(start, chunk), cols], preferred_element_type=f32
                    )

                weighted = lax.fori_loop(
                    0, chunks, weigh_chunk, jnp.zeros((tok, head_size), f32)
                )
            copy = p_copy(slot, h, d)
            copy.start()
            pending[slot] = copy
            o_ref[d * tok : (d + 1) * tok, cols] = weighted
            ctx[d][:, cols] = weighted.astype(bf16)
    for copy in pending.values():
        copy.wait()


def attention_forward(place, own, other, bias, gain, w_query, w_key, w_value):
    s_count, rows, width = own[0].shape
    tok = rows - 16
    local = width // groups
    blocks = 8 * s_count
    seq = blocks * tok
    chunk = min(seq, 1024)
    shapes = (
        [shaped(bf16, tok, local)] * 4
        + [shaped(bf16, 4 * tok, local)]
        + [shaped(bf16, seq, local)] * 2
        + [shaped(f32, 4 * tok, local), shaped(bf16, 4 * tok, width)]
        + [shaped(bf16, local // 64, seq // chunk, 4 * tok, chunk)]
    )
    return kernel_call(
        functools.partial(forward_body, blocks=blocks, chunk=chunk),
        "attention_forward",
        [place],
        [*own, *other, bias, gain, w_query, w_key, w_value],
        shapes,
        scratch=[
            pltpu.VMEM((width, 3 * local), bf16),
            pltpu.VMEM((8 * tok, width), bf16),
            pltpu.VMEM((8 * tok, 2 * local), bf16),
            pltpu.VMEM((8, seq), f32),
            pltpu.VMEM((tok, (2 * blocks - 1) * tok), f32),
            pltpu.VMEM((2 if seq == chunk else 1, tok, seq), f32),
            pltpu.VMEM((2, seq // chunk, tok, chunk), bf16),
            pltpu.SemaphoreType.DMA((2,)),
        ],
        in_hbm=(("out", 9),),
        staged=tuple(range(8)) if s_count == 1 else (),
        mebibytes=12 if s_count == 1 else 60,
        us=25,
    )


def backward_body(
    smem, get, outs, p_scr, ds_scr, dctx_scr, strip, dq_scr, kv_scr, rows_scr, sems, *, blocks, chunk
):
    (place,) = smem
    p_hbm = get(8)
    dq = outs[0:4]
    keep_ref, send_ref, table_ref = outs[4:7]
    group, core, s_own = place[0], place[1], place[2]
    tok = 128
    head_size = 64
    seq = blocks * tok
    chunks = seq // chunk
    s_count = blocks // 8

    def p_copy(h, i, slot):
        return pltpu.make_async_copy(p_hbm.at[h, i], p_scr.at[slot], sems.at[slot])

    p_copy(0, 0, 0).start()
    for d in range(4):
        dctx_scr[d * tok : (d + 1) * tok, :] = get(d)[...]
    q_ref, k_ref, v_ref, o_ref = get(4), get(5), get(6), get(7)
    heads = q_ref.shape[1] // head_size
    rows_scr[...] = jnp.zeros_like(rows_scr)
    rows_at_once = 32
    for h in range(heads):
        cols = slice(h * head_size, (h + 1) * head_size)
        strip[...] = jnp.zeros_like(strip)
        out_grad = dctx_scr[:, cols]
        delta = jnp.sum(out_grad.astype(f32) * o_ref[:, cols], axis=1, keepdims=True)

        def run_chunk(i, h=h, cols=cols, out_grad=out_grad, delta=delta):
            start = pl.multiple_of(i * chunk, chunk)
            slot = (h * chunks + i) % 2
            following = h * chunks + i + 1

            @pl.when(following < heads * chunks)
            def _():
                p_copy(following // chunks, following % chunks, 1 - slot).start()

            p_copy(h, i, slot).wait()
            keys = k_ref[pl.ds(start, chunk), cols]
            values = v_ref[pl.ds(start, chunk), cols]
            for d in range(4):
                query_block = ((group ^ d) * s_count + s_own) * 2 + core
                base = pl.multiple_of(tok * (blocks - 1) - query_block * tok + start, tok)
                prob_grad = dot(out_grad[d * tok : (d + 1) * tok], values, 1, 1)
                for r in range(0, tok, rows_at_once):
                    rows = slice(d * tok + r, d * tok + r + rows_at_once)
                    here = prob_grad[r : r + rows_at_once] - delta[rows]
                    low = (p_scr[slot, rows, :].astype(f32) * here).astype(bf16)
                    ds_scr[rows, :] = low
                    strip[r : r + rows_at_once, pl.ds(base, chunk)] += low.astype(f32)
            scores_grad = ds_scr[...]
            part = jnp.dot(scores_grad, keys, preferred_element_type=f32)
            if chunks == 1:
                dq_scr[:, cols] = part
            else:
                dq_scr[:, cols] += part
            queries = q_ref[:, cols]
            kv_scr[0, pl.ds(start, chunk), :] = dot(scores_grad, queries, 0, 0).astype(bf16)
            kv_scr[1, pl.ds(start, chunk), :] = dot(p_scr[slot], out_grad, 0, 0).astype(bf16)

        if chunks == 1:
            run_chunk(0)
        else:
            dq_scr[:, cols] = jnp.zeros((4 * tok, head_size), f32)
            pl.loop(0, chunks)(run_chunk)

        def place_rows(e, h=h, cols=cols):
            for d in range(4):
                for k, target in ((0, keep_ref), (1, send_ref)):
                    block = ((group ^ d) * s_count + (s_own ^ e)) * 2 + (core if k == 0 else 1 - core)
                    start = pl.multiple_of(block * tok, tok)
                    width = heads * head_size
                    target[e, d, :, cols] = kv_scr[0, pl.ds(start, tok), :]
                    shifted = slice(width + h * head_size, width + (h + 1) * head_size)
                    target[e, d, :, shifted] = kv_scr[1, pl.ds(start, tok), :]

        if s_count == 1:
            place_rows(0)
        else:
            pl.loop(0, s_count)(place_rows)
        near = strip[:, tok * (blocks - 2) : tok * (blocks + 1)]
        left = jnp.zeros((1, tok), f32)
        right = jnp.zeros((1, tok), f32)
        for t in range(blocks - 2):
            left = left + jnp.sum(strip[:, t * tok : (t + 1) * tok], axis=0, keepdims=True)
            far = (blocks + 1 + t) * tok
            right = right + jnp.sum(strip[:, far : far + tok], axis=0, keepdims=True)
        rows_scr[h : h + 1, :] = jnp.concatenate([left, jnp.zeros((1, 2 * tok), f32), right], axis=1)
        spread = jnp.concatenate([jnp.zeros((tok, tok), f32), near], axis=1)
        skewed = spread[:8]
        for j in range(1, tok // 8):
            skewed = skewed + pltpu.roll(spread[8 * j : 8 * j + 8], 4 * tok - 8 * j, 1)
        row = lax.broadcasted_iota(jnp.int32, skewed.shape, 0)
        for step in (1, 2, 4):
            moved = pltpu.roll(skewed, 4 * tok - step, 1)
            skewed = jnp.where((row & step) != 0, moved, skewed)
        rows_scr[h : h + 1, :] += jnp.sum(skewed, axis=0, keepdims=True)
    for d in range(4):
        dq[d][...] = dq_scr[d * tok : (d + 1) * tok, :].astype(bf16)
    span = 4 * tok
    bucket_count = 2 * (len(cutoffs) + 1)
    buckets = bucket_row(span, bucket_count // 2)
    sums = rows_scr[...]
    lane = lax.broadcasted_iota(jnp.int32, (8, tok), 1)
    table = jnp.zeros((8, tok), f32)
    for b in range(bucket_count):
        picked = jnp.where(buckets == b, sums, 0.0)
        table = jnp.where(lane == b, jnp.sum(picked, axis=1, keepdims=True), table)
    table_ref[...] = table


def attention_backward(place, dctx, q, k, v, o, p):
    tok, local = dctx[0].shape
    seq = k.shape[0]
    blocks = seq // tok
    s_count = blocks // 8
    chunk = p.shape[3]
    shapes = (
        [shaped(bf16, tok, local)] * 4
        + [shaped(bf16, s_count, 4, tok, 2 * local)] * 2
        + [shaped(f32, 8, tok)]
    )
    return kernel_call(
        functools.partial(backward_body, blocks=blocks, chunk=chunk),
        "attention_backward",
        [place],
        [*dctx, q, k, v, o, p],
        shapes,
        scratch=[
            pltpu.VMEM((2, 4 * tok, chunk), bf16),
            pltpu.VMEM((4 * tok, chunk), bf16),
            pltpu.VMEM((4 * tok, local), bf16),
            pltpu.VMEM((tok, (2 * blocks - 1) * tok), f32),
            pltpu.VMEM((4 * tok, local), f32),
            pltpu.VMEM((2, seq, 64), bf16),
            pltpu.VMEM((8, 4 * tok), f32),
            pltpu.SemaphoreType.DMA((2,)),
        ],
        in_hbm=(8,),
        mebibytes=11 if s_count == 1 else 60,
        us=20,
    )


def ffn_forward_body(smem, get, outs):
    (place,) = smem
    middle_ref, left_ref, act_ref, slope_ref = outs
    count = 4
    w_out, w_gate, w_up = get(6), get(7), get(8)
    group = place[0]
    tok, width = middle_ref.shape
    local = width // groups
    total = get(4)[...].astype(f32)
    for d in range(4):
        start = pl.multiple_of((group ^ d) * local, local)
        total = total + dot(get(d)[...], w_out[pl.ds(start, local), :], 1, 0)
    middle_ref[...] = total
    normed = (total * rms_scale(total) * get(5)[...]).astype(bf16)
    left_ref[:, :width] = normed
    step = w_gate.shape[1] // count
    for i in range(count):
        cols = slice(i * step, (i + 1) * step)
        gate = dot(normed, w_gate[:, cols], 1, 0)
        up = dot(normed, w_up[:, cols], 1, 0)
        root = 0.7978845608028654
        square = gate * gate
        bend = jnp.tanh(root * (gate + 0.044715 * (gate * square)))
        act = 0.5 * gate * (1.0 + bend)
        slope = 0.5 * (1.0 + bend) + 0.5 * gate * (1.0 - bend * bend) * (
            root * (1.0 + 3.0 * 0.044715 * square)
        )
        act_ref[:, cols] = act
        slope_ref[:, cols] = up * slope
        left_ref[:, width + i * step : width + (i + 1) * step] = (act * up).astype(bf16)


def ffn_forward(place, ctx, tokens, gain, w_out, w_gate, w_up):
    tok, width = tokens.shape
    ff = w_gate.shape[1]
    return kernel_call(
        ffn_forward_body,
        "ffn_forward",
        [place],
        [*ctx, tokens, gain, w_out, w_gate, w_up],
        [
            shaped(f32, tok, width),
            shaped(bf16, tok, width + ff),
            shaped(f32, tok, ff),
            shaped(f32, tok, ff),
        ],
        us=14,
    )


def ffn_backward_body(smem, get, outs, gate_scr, up_scr, attn_scr):
    (place,) = smem
    out_ref, grad_ref, gain_grad_ref = outs[0:3]
    dctx = outs[3:7]
    mine_ref, near_ref, far_gate_ref, far_up_ref = outs[7:11]
    count = 4
    w_down, w_gate, w_up, w_out = get(10), get(11), get(12), get(13)
    group, core, across = place[0], place[1], place[4]
    tok, width = grad_ref.shape
    ff = w_gate.shape[1]
    local = width // groups
    quarter = ff // 4
    cot = get(0)[...]
    step = ff // count
    act_ref, slope_ref = get(3), get(4)
    normed_grad = jnp.zeros((tok, width), f32)
    for i in range(count):
        cols = slice(i * step, (i + 1) * step)
        hidden_grad = dot(cot, w_down[cols, :], 1, 1)
        gate = (hidden_grad * slope_ref[:, cols]).astype(bf16)
        up = (hidden_grad * act_ref[:, cols]).astype(bf16)
        gate_scr[:, cols] = gate
        up_scr[:, cols] = up
        normed_grad = (
            normed_grad + dot(gate, w_gate[:, cols], 1, 1) + dot(up, w_up[:, cols], 1, 1)
        )
    def quarter_of(ref, x, c):
        return ref[:, pl.ds(pl.multiple_of((x * 2 + c) * quarter, quarter), quarter)]

    mine_ref[:, :quarter] = quarter_of(gate_scr, across, core)
    mine_ref[:, quarter : 2 * quarter] = quarter_of(up_scr, across, core)
    near_ref[:, :quarter] = quarter_of(gate_scr, across, 1 - core)
    near_ref[:, quarter : 2 * quarter] = quarter_of(up_scr, across, 1 - core)
    for ref, source in ((far_gate_ref, gate_scr), (far_up_ref, up_scr)):
        ref[:, :quarter] = quarter_of(source, 1 - across, core)
        ref[:, quarter : 2 * quarter] = quarter_of(source, 1 - across, 1 - core)
    middle = get(1)[...]
    scale = rms_scale(middle)
    unit = middle * scale
    scaled = normed_grad * get(5)[...]
    gain_grad_ref[...] = jnp.sum(normed_grad * unit, axis=0, keepdims=True)
    middle_grad = cot.astype(f32) + scale * (
        scaled - unit * jnp.mean(unit * scaled, axis=1, keepdims=True)
    )
    grad_ref[...] = middle_grad
    attn = middle_grad.astype(bf16)
    attn_scr[...] = attn
    for d in range(4):
        start = pl.multiple_of((group ^ d) * local, local)
        dctx[d][...] = dot(attn, w_out[pl.ds(start, local), :], 1, 1).astype(bf16)
    at = 2 * quarter
    for ref, which in ((mine_ref, across), (near_ref, across), (far_up_ref, 1 - across)):
        for d in range(4):
            ref[:, at + d * local : at + (d + 1) * local] = get(6 + d)[...]
        start = pl.multiple_of(which * (width // 2), width // 2)
        ref[:, at + width :] = attn_scr[:, pl.ds(start, width // 2)]
    out_ref[...] = (middle + dot(get(2)[:, width:], w_down[...], 1, 0)).astype(bf16)


def ffn_backward(place, cot, middle, hidden, act, slope, gain, ctx, w_down, w_gate, w_up, w_out):
    tok, width = cot.shape
    ff = w_gate.shape[1]
    local = width // groups
    return kernel_call(
        ffn_backward_body,
        "ffn_backward",
        [place],
        [cot, middle, hidden, act, slope, gain, *ctx, w_down, w_gate, w_up, w_out],
        [shaped(bf16, tok, width), shaped(f32, tok, width), shaped(f32, 1, width)]
        + [shaped(bf16, tok, local)] * 4
        + [shaped(bf16, tok, ff // 2 + width + width // 2)] * 2
        + [shaped(bf16, tok, ff // 2), shaped(bf16, tok, ff // 2 + width + width // 2)],
        scratch=[
            pltpu.VMEM((tok, ff), bf16),
            pltpu.VMEM((tok, ff), bf16),
            pltpu.VMEM((tok, width), bf16),
        ],
        mebibytes=6,
        us=6,
    )


def split_rows(total, wide, odd, kept_ref, sent_ref, cols):
    block = total.shape[0] // wide
    for i in range(wide // 2):
        even_rows = total[2 * i * block : (2 * i + 1) * block, :]
        odd_rows = total[(2 * i + 1) * block : (2 * i + 2) * block, :]
        kept_ref[i, :, cols] = jnp.where(odd, odd_rows, even_rows)
        sent_ref[i, :, cols] = jnp.where(odd, even_rows, odd_rows).astype(bf16)


def down_grad_body(smem, get, outs, left_scr, right_scr, total_scr, *, wide):
    (place,) = smem
    kept_ref, sent_ref = outs
    core, odd = place[1], place[3] == 1
    tok, half = get(4).shape
    local = half // 2
    for i in range(4):
        rows = slice(i * tok, (i + 1) * tok)
        left_scr[rows, :] = get(i)[:, 2 * half :]
        both = get(4 + i)[...]
        right_scr[rows, :] = jnp.where(core == 0, both[:, :local], both[:, local:])
    total_scr[...] = dot(left_scr[...], right_scr[...], 0, 0)
    split_rows(total_scr, wide, odd, kept_ref, sent_ref, slice(None))


def down_grad(place, lefts, rights, wide):
    tok, half = rights[0].shape
    ff = lefts[0].shape[1] - 2 * half
    shape = (wide // 2, ff // wide, half // 2)
    return kernel_call(
        functools.partial(down_grad_body, wide=wide),
        "down_grad",
        [place],
        [*lefts, *rights],
        [shaped(f32, *shape), shaped(bf16, *shape)],
        scratch=[
            pltpu.VMEM((4 * tok, ff), bf16),
            pltpu.VMEM((4 * tok, half // 2), bf16),
            pltpu.VMEM((ff, half // 2), f32),
        ],
        mebibytes=6,
        us=8,
    )


def gate_grad_body(smem, get, outs, left_scr, right_scr, total_scr, *, wide):
    (place,) = smem
    tok, width = left_scr.shape[0] // 4, left_scr.shape[1]
    quarter = right_scr.shape[1]
    for i in range(4):
        rows = slice(i * tok, (i + 1) * tok)
        left_scr[rows, :] = get(i)[:, :width]
        at = quarter if i == 3 else 0
        right_scr[rows, :] = get(4 + i)[:, at : at + quarter]
    total_scr[...] = dot(left_scr[...], right_scr[...], 0, 0)
    split_rows(total_scr, wide, place[3] == 1, *outs, slice(None))


def gate_grad(place, lefts, rights, width, wide):
    tok = lefts[0].shape[0]
    quarter = rights[2].shape[1] // 2
    shape = (wide // 2, width // wide, quarter)
    return kernel_call(
        functools.partial(gate_grad_body, wide=wide),
        "gate_grad",
        [place],
        [*lefts, *rights],
        [shaped(f32, *shape), shaped(bf16, *shape)],
        scratch=[
            pltpu.VMEM((4 * tok, width), bf16),
            pltpu.VMEM((4 * tok, quarter), bf16),
            pltpu.VMEM((width, quarter), f32),
        ],
        mebibytes=5,
        us=2,
    )


def up_grad_body(
    smem, get, outs, left_scr, right_scr, ctx_scr, attn_scr, total_scr, out_scr, *, wide
):
    (place,) = smem
    group, core, odd = place[0], place[1], place[3] == 1
    tok, width = left_scr.shape[0] // 4, left_scr.shape[1]
    local = width // groups
    quarter = right_scr.shape[1]
    for i in range(4):
        rows = slice(i * tok, (i + 1) * tok)
        left_scr[rows, :] = get(i)[:, :width]
        at = 0 if i == 2 else quarter
        right_scr[rows, :] = get(4 + i)[:, at : at + quarter]
        ctx_scr[rows, :] = get(4 + i)[:, 2 * quarter : 2 * quarter + width]
        both = get(4 + i)[:, 2 * quarter + width :]
        attn_scr[rows, :] = jnp.where(core == 0, both[:, :local], both[:, local:])
    total_scr[...] = dot(left_scr[...], right_scr[...], 0, 0)
    split_rows(total_scr, wide, odd, *outs, slice(0, quarter))
    turned = dot(ctx_scr[...], attn_scr[...], 0, 0)
    for d in range(4):
        start = pl.multiple_of((group ^ d) * local, local)
        out_scr[pl.ds(start, local), :] = turned[d * local : (d + 1) * local]
    split_rows(out_scr, wide, odd, *outs, slice(quarter, quarter + local))


def up_grad(place, lefts, rights, width, wide):
    tok = lefts[0].shape[0]
    quarter = (rights[0].shape[1] - width - width // 2) // 2
    local = width // groups
    shape = (wide // 2, width // wide, quarter + local)
    return kernel_call(
        functools.partial(up_grad_body, wide=wide),
        "up_grad",
        [place],
        [*lefts, *rights],
        [shaped(f32, *shape), shaped(bf16, *shape)],
        scratch=[
            pltpu.VMEM((4 * tok, width), bf16),
            pltpu.VMEM((4 * tok, quarter), bf16),
            pltpu.VMEM((4 * tok, width), bf16),
            pltpu.VMEM((4 * tok, local), bf16),
            pltpu.VMEM((width, quarter), f32),
            pltpu.VMEM((width, local), f32),
        ],
        mebibytes=8,
        us=3,
    )


def collect_body(smem, get, outs):
    local = outs[0].shape[1] // 3
    for d in range(4):
        outs[d][:, :local] = get(d)[...]
    for d in range(4):
        total = get(4)[d].astype(f32) + get(5)[d].astype(f32)
        outs[d][:, local:] = total.astype(bf16)


def collect(dq, kept, received):
    tok, local = dq[0].shape
    return kernel_call(
        collect_body,
        "collect",
        [],
        [*dq, kept, received],
        [shaped(bf16, tok, 3 * local)] * 4,
        us=2,
    )


def qkv_grad_body(smem, get, outs, grad_scr, total_scr):
    (place,) = smem
    kept_ref, sent_ref, small_ref = outs
    group, core = place[0], place[1]
    width, span = total_scr.shape
    local = span // 3
    tok = grad_scr.shape[0] // 4
    for d in range(4):
        grad_scr[d * tok : (d + 1) * tok, :] = get(d)[...]
    total_scr[...] = dot(get(4)[...], grad_scr[...], 0, 0)
    quarter = width // 4
    for i in range(2):
        for ref, which in ((sent_ref, 1 - core), (kept_ref, core)):
            start = pl.multiple_of((2 * i + which) * quarter, quarter)
            ref[i] = total_scr[pl.ds(start, quarter), :].astype(ref.dtype)
    window, late = group_window(group, local)
    ones = jnp.ones((8, local), bf16)
    gain_grad = jnp.zeros((8, width), f32)
    for i in range(3):
        both = get(8 + i)[:, pl.ds(window, -(-local // 128) * 128)]
        weight = jnp.where(late, both[:, both.shape[1] - local :], both[:, :local])
        product = total_scr[:, i * local : (i + 1) * local] * weight.astype(f32)
        high = product.astype(bf16)
        rest = (product - high.astype(f32)).astype(bf16)
        gain_grad = gain_grad + dot(ones, high, 1, 1) + dot(ones, rest, 1, 1)
    gain_grad = gain_grad[0:1] / get(5)[...]
    ffn_gain = get(6)[...]
    lanes = 128
    rows = width // lanes
    for i in range(rows):
        small_ref[i : i + 1, :] = gain_grad[:, i * lanes : (i + 1) * lanes]
        small_ref[rows + i : rows + i + 1, :] = ffn_gain[:, i * lanes : (i + 1) * lanes]
    heads = (small_ref.shape[0] - 2 * rows) // groups
    table = get(7)[:heads, :]
    for i in range(groups):
        at = 2 * rows + i * heads
        small_ref[at : at + heads, :] = jnp.where(group == i, table, 0.0)


def qkv_grad(place, grads, normed, gain, gain_grad, table, head_count, w_query, w_key, w_value):
    rows, width = normed.shape
    span = grads[0].shape[1]
    return kernel_call(
        qkv_grad_body,
        "qkv_grad",
        [place],
        [*grads, normed, gain, gain_grad, table, w_query, w_key, w_value],
        [
            shaped(f32, 2, width // 4, span),
            shaped(bf16, 2, width // 4, span),
            shaped(f32, 2 * width // 128 + head_count, 128),
        ],
        scratch=[pltpu.VMEM((rows, span), bf16), pltpu.VMEM((width, span), f32)],
        mebibytes=7,
        us=4,
    )


def input_grad_body(smem, get, outs):
    (place,) = smem
    group = place[0]
    weights = [get(7 + i) for i in range(3)]
    local = get(0).shape[1] // 3
    window = -(-local // 128) * 128
    tok = get(0).shape[0]
    spare = jnp.zeros((tok, window - local), bf16)
    normed_grad = None
    for d in range(4):
        start, late = group_window(group ^ d, local)
        grads = get(d)[...]
        for i in range(3):
            part = grads[:, i * local : (i + 1) * local]
            part = jnp.where(
                late,
                jnp.concatenate([spare, part], axis=1),
                jnp.concatenate([part, spare], axis=1),
            )
            product = dot(part, weights[i][:, pl.ds(start, window)], 1, 1)
            normed_grad = product if normed_grad is None else normed_grad + product
    values = get(4)[...].astype(f32)
    scale = rms_scale(values)
    unit = values * scale
    scaled = normed_grad * get(5)[...]
    outs[0][...] = get(6)[...] + scale * (
        scaled - unit * jnp.mean(unit * scaled, axis=1, keepdims=True)
    )


def final_input_grad(place, grads, tokens, gain, middle_grad, w_query, w_key, w_value):
    return kernel_call(
        input_grad_body,
        "input_grad",
        [place],
        [*grads, tokens, gain, middle_grad, w_query, w_key, w_value],
        [shaped(f32, *tokens.shape)],
        staged=(0, 1, 2, 3, 4, 6),
        mebibytes=6,
        us=4,
    )[0]


def add_split_body(smem, get, outs, *, bit, splits):
    (place,) = smem
    kept, received = get(0), get(1)
    if kept.shape[0] == 1:
        total = kept[0].astype(f32) + received[0].astype(f32)
        at = 0
        for i, span in enumerate(splits):
            outs[i][...] = total[:, at : at + span]
            at += span
        return
    odd = ((place[5] >> bit) & 1) == 1
    for i in range(kept.shape[0] // 2):
        even_rows = kept[2 * i].astype(f32) + received[2 * i].astype(f32)
        odd_rows = kept[2 * i + 1].astype(f32) + received[2 * i + 1].astype(f32)
        outs[1][i] = jnp.where(odd, even_rows, odd_rows).astype(bf16)
        outs[0][i] = jnp.where(odd, odd_rows, even_rows)


def wide_sum(layout, place, kept, sent, bit, splits, name, us, first=()):
    received = layout.wide_bit(sent, bit)
    kept = after(kept, first)
    remaining, block, columns = kept.shape
    if remaining == 1:
        outputs = [shaped(f32, block, span) for span in splits]
    else:
        shape = (remaining // 2, block, columns)
        outputs = [shaped(f32, *shape), shaped(bf16, *shape)]
    return kernel_call(
        functools.partial(add_split_body, bit=bit + 1, splits=splits),
        f"{name}_sum",
        [place],
        [kept, received],
        outputs,
        us=us,
    )


def after(values, done):
    return lax.optimization_barrier((values, done))[0]


def halved(block, axis, keep):
    return (
        lax.dynamic_index_in_dim(block, keep, axis, keepdims=False),
        lax.dynamic_index_in_dim(block, 1 - keep, axis, keepdims=False),
    )


def on_device(
    inputs,
    segment_ids,
    gain_attn,
    w_query,
    w_key,
    w_value,
    w_out,
    gain_ffn,
    w_gate,
    w_up,
    w_down,
    bias_table,
    cotangent,
):
    layout = Layout(lax.axis_size("narrow"), lax.axis_size("wide"))
    s_count = layout.s_count
    tokens = inputs[0]
    out_grad = cotangent[0]
    tok, width = tokens.shape
    local = width // groups
    ff = w_gate.shape[1]
    bucket_count, head_count = bias_table.shape
    narrow = lax.axis_index("narrow")
    wide = lax.axis_index("wide")
    core = narrow % 2
    across = narrow // 2
    group = wide // (2 * s_count)
    s_own = (wide // 2) % s_count
    y_own = wide % 2
    place = jnp.stack([group, core, s_own, y_own, across, wide]).astype(jnp.int32)
    gain_attn = gain_attn[None]
    gain_ffn = gain_ffn[None]

    packet = packed(tokens, segment_ids)
    own = [layout.turned(packet, d)[None] for d in range(3)]
    own.append(layout.wide_bit(own[2], layout.wide.bit_length() - 3))
    for d in range(4):
        size = 1
        while size < s_count:
            own[d] = jnp.concatenate([own[d], layout.wide_bit(own[d], size.bit_length())], axis=0)
            size *= 2
    bias = bias_rows(place, bias_table, 4 * tok)
    own = after(own, bias)
    other = [layout.core(block) for block in own]

    def half_cols(block, which):
        return lax.dynamic_slice_in_dim(block, which * (block.shape[1] // 2), block.shape[1] // 2, 1)

    cot_own = half_cols(out_grad, across)
    cot_across = layout.across(half_cols(out_grad, 1 - across))
    cot_parts = [cot_own, layout.core(cot_own), cot_across, layout.core(cot_across)]

    outs = attention_forward(
        place, own, other, bias, gain_attn, w_query, w_key, w_value
    )
    ctx_parts = outs[:4]
    q_own, k_all, v_all, o_own, normed_own, probs = outs[4:]
    ctx = [layout.turned(ctx_parts[d], d) for d in range(4)]
    ctx = after(ctx, cot_parts)

    middle, left, act, slope = ffn_forward(place, ctx, tokens, gain_ffn, w_out, w_gate, w_up)
    left_across = layout.across(left)
    left_core = layout.core(left)
    back = ffn_backward(
        place, out_grad, middle, left, act, slope, gain_ffn, ctx, w_down, w_gate, w_up, w_out
    )
    output, middle_grad, grad_gain_ffn = back[0:3]
    dctx = [layout.turned(back[3 + d], d) for d in range(4)]
    mine, near, far_gate, far_up = back[7:11]
    near = layout.core(near)
    far_gate = layout.across(far_gate)
    far_up = layout.across(far_up)
    dctx = after(dctx, left_across)

    back = attention_backward(place, dctx, q_own, k_all, v_all, o_own, probs)
    dq, kept, sent, table_rows = back[:4], back[4], back[5], back[6]
    received = layout.core(sent)
    left_across = after(left_across, sent)
    lefts = [left, left_core, left_across, layout.core(left_across)]
    down_kept, down_sent = down_grad(place, lefts, cot_parts, layout.wide)
    size = s_count
    while size > 1:
        size //= 2
        total = kept.astype(f32) + received.astype(f32)
        kept = total[:size]
        received = layout.wide_bit(total[size:].astype(bf16), size.bit_length())
    received = after(received, down_sent)
    low_grads = collect(dq, kept[0], received[0])
    returned = [layout.turned(low_grads[d], d) for d in range(4)]

    far_gate = after(far_gate, down_sent)
    far_gate_both = layout.core(far_gate)
    lefts = after(lefts, low_grads)
    gate_kept, gate_sent = gate_grad(
        place, lefts, [mine, near, far_gate, far_gate_both], width, layout.wide
    )
    normed_own = after(normed_own, gate_sent)

    qkv_kept, qkv_sent, small = qkv_grad(
        place,
        low_grads,
        normed_own,
        gain_attn,
        grad_gain_ffn,
        table_rows,
        head_count,
        w_query,
        w_key,
        w_value,
    )
    far_up = after(far_up, qkv_sent)
    far_up_both = layout.core(far_up)
    up_kept, up_sent = up_grad(place, lefts, [mine, near, far_up, far_up_both], width, layout.wide)

    rows = width // layout.wide
    part = qkv_kept + layout.core(qkv_sent).astype(f32)
    part = part.reshape(2, s_count, 2, rows, 3 * local)
    kept, sent = halved(part, 0, across)
    part = kept + layout.across(sent.astype(bf16)).astype(f32)
    kept, sent = halved(part, 1, y_own)
    part = kept + layout.wide_bit(sent.astype(bf16), 0).astype(f32)
    size = s_count
    bit = 1
    while size > 1:
        size //= 2
        part = part.reshape(size, 2, rows, 3 * local)
        kept, sent = halved(part, 1, (s_own >> (bit - 1)) & 1)
        part = kept + layout.wide_bit(sent.astype(bf16), bit).astype(f32)
        bit += 1
    part = part.reshape(rows, 3 * local).astype(bf16)
    final_qkv = layout.send(part, lambda x, c, g, s, y: (g // 2, g % 2, x * 2 + c, s, y)).astype(f32)

    input_grad = final_input_grad(
        place, returned, tokens, gain_attn, middle_grad, w_query, w_key, w_value
    )
    quarter_ff = ff // layout.narrow
    bits = layout.wide.bit_length() - 1
    down, gate, up = (down_kept, down_sent), (gate_kept, gate_sent), (up_kept, up_sent)
    for bit in range(bits):
        down = wide_sum(layout, place, *down, bit, (local,), "down", 6)
        gate = wide_sum(layout, place, *gate, bit, (quarter_ff,), "gate", 8)
        first = returned if bit == 0 else (input_grad, down, gate) if bit == bits - 1 else ()
        up = wide_sum(layout, place, *up, bit, (quarter_ff, local), "up", 12, first)
        if bit == 0:
            small = after(small, up)
    (final_down,), (final_gate,), (final_up, final_out) = down, gate, up

    for bit in range(bits):
        small = small + layout.wide_bit(small, bit)
    small = small + layout.across(small)
    small = small + layout.core(small)
    gain_rows = width // 128
    sum_gain_attn = small[:gain_rows].reshape(width)
    sum_gain_ffn = small[gain_rows : 2 * gain_rows].reshape(width)
    sum_table = small[2 * gain_rows :, :bucket_count].T

    return (
        output[None],
        input_grad[None],
        sum_gain_attn,
        final_qkv[:, :local],
        final_qkv[:, local : 2 * local],
        final_qkv[:, 2 * local :],
        final_out,
        sum_gain_ffn,
        final_gate,
        final_up,
        final_down,
        sum_table,
    )


def solution(mesh):
    tokens = P("narrow", "wide", None)
    share = P("wide", "narrow")
    return jax.shard_map(
        on_device,
        mesh=mesh,
        in_specs=(tokens, P("narrow", "wide")) + (P(),) * 10 + (tokens,),
        out_specs=(
            tokens,
            tokens,
            P(),
            share,
            share,
            share,
            share,
            P(),
            share,
            share,
            share,
            P(),
        ),
        check_vma=False,
    )
```

```python
import functools

import jax
import jax.numpy as jnp
import numpy as np
from jax import lax
from jax.experimental import pallas as pl
from jax.experimental.pallas import tpu as pltpu
from jax.sharding import PartitionSpec as P

cutoffs = (1, 2, 3, 4, 5, 6, 7, 8, 12, 16, 23, 32, 46, 64, 91)
epsilon = 1e-06
masked_score = -1000000000.0
highest = lax.Precision.HIGHEST
axes = ("narrow", "wide")
groups = 4
bf16 = jnp.bfloat16
f32 = jnp.float32


def dot(left, right, left_dim, right_dim):
    return lax.dot_general(
        left, right, (((left_dim,), (right_dim,)), ((), ())), preferred_element_type=f32
    )


class Layout:
    def __init__(self, narrow, wide):
        self.narrow = narrow
        self.wide = wide
        self.s_count = wide // (groups * 2)

    def index(self, x, c, g, s, y):
        return (x * 2 + c) * self.wide + (g * self.s_count + s) * 2 + y

    def send(self, block, target):
        route = []
        for x in range(self.narrow // 2):
            for c in range(2):
                for g in range(groups):
                    for s in range(self.s_count):
                        for y in range(2):
                            route.append(
                                (self.index(x, c, g, s, y), self.index(*target(x, c, g, s, y)))
                            )
        return lax.ppermute(block, axes, route)

    def turned(self, block, d):
        return self.send(block, lambda x, c, g, s, y: (x, y, g ^ d, s, c))

    def core(self, block):
        return self.send(block, lambda x, c, g, s, y: (x, 1 - c, g, s, y))

    def across(self, block):
        return self.send(block, lambda x, c, g, s, y: (x ^ 1, c, g, s, y))

    def wide_bit(self, block, bit):
        def target(x, c, g, s, y):
            w = ((g * self.s_count + s) * 2 + y) ^ (1 << bit)
            return (x, c, w // (2 * self.s_count), (w // 2) % self.s_count, w % 2)

        return self.send(block, target)


def rms_scale(values):
    return lax.rsqrt(jnp.mean(values * values, axis=-1, keepdims=True) + epsilon)


def bucket_row(span, half_count):
    offset = lax.broadcasted_iota(jnp.int32, (1, span), 1) - span // 2
    distance = jnp.abs(offset)
    bucket = jnp.where(offset > 0, half_count, 0)
    for cutoff in cutoffs:
        bucket = bucket + jnp.where(distance >= cutoff, 1, 0)
    return bucket


def cost(microseconds):
    return pl.CostEstimate(
        flops=int(microseconds * 1.15e9), bytes_accessed=1024, transcendentals=0
    )


def kernel_call(
    body, name, smem, inputs, outputs, scratch=(), in_hbm=(), staged=(), mebibytes=4, us=3
):
    n_smem, n_in, n_out = len(smem), len(inputs), len(outputs)
    ins = [i for i in staged if not isinstance(i, tuple)]
    leaving = [i[1] for i in staged if isinstance(i, tuple)]

    def kernel(*refs):
        given = refs[n_smem : n_smem + n_in]
        results = refs[n_smem + n_in : n_smem + n_in + n_out]
        rest = refs[n_smem + n_in + n_out :]
        buffers = dict(zip(ins, rest))
        drafts = dict(zip(leaving, rest[len(ins) :]))
        arrivals = {}
        for at, i in enumerate(ins):
            arrivals[i] = pltpu.make_async_copy(given[i], buffers[i], rest[-1].at[at])
            arrivals[i].start()

        def get(i):
            if i in arrivals:
                arrivals.pop(i).wait()
            return buffers.get(i, given[i])

        outs = [drafts.get(i, results[i]) for i in range(n_out)]
        body(refs[:n_smem], get, outs, *rest[len(staged) : len(rest) - (1 if staged else 0)])
        for i in ins:
            get(i)
        departures = [
            pltpu.make_async_copy(drafts[i], results[i], rest[-1].at[len(ins) + at])
            for at, i in enumerate(leaving)
        ]
        for copy in departures:
            copy.start()
        for copy in departures:
            copy.wait()

    hbm = pl.BlockSpec(memory_space=pltpu.HBM)
    vmem = pl.BlockSpec(memory_space=pltpu.VMEM)
    copies = [pltpu.SemaphoreType.DMA((len(staged),))] if staged else []
    return pl.pallas_call(
        kernel,
        out_shape=outputs,
        in_specs=[pl.BlockSpec(memory_space=pltpu.SMEM)] * n_smem
        + [hbm if i in in_hbm or i in ins else vmem for i in range(n_in)],
        out_specs=[hbm if ("out", i) in in_hbm or i in leaving else vmem for i in range(n_out)],
        scratch_shapes=[pltpu.VMEM(inputs[i].shape, inputs[i].dtype) for i in ins]
        + [pltpu.VMEM(outputs[i].shape, outputs[i].dtype) for i in leaving]
        + list(scratch)
        + copies,
        compiler_params=pltpu.CompilerParams(vmem_limit_bytes=mebibytes * 2**20),
        cost_estimate=cost(us),
        name=name,
    )(*smem, *inputs)


def shaped(dtype, *shape):
    return jax.ShapeDtypeStruct(shape, dtype)


def group_window(group, local):
    start = (group * local) // 128 * 128
    return pl.multiple_of(start, 128), (group * local) % 128 != 0


def pack_body(smem, get, outs):
    (packet,) = outs
    tok, width = get(0).shape
    row = jnp.broadcast_to(get(1)[...].astype(f32), (packet.shape[0] - tok, tok))
    packet[tok:, :tok] = row.astype(bf16)
    packet[tok:, tok:] = jnp.zeros((packet.shape[0] - tok, width - tok), bf16)
    packet[:tok, :] = get(0)[...]


def packed(tokens, segment_ids):
    tok, width = tokens.shape
    return kernel_call(
        pack_body,
        "pack",
        [],
        [tokens, segment_ids],
        [shaped(bf16, tok + 16, width)],
        staged=(0, 1),
        mebibytes=60,
        us=1,
    )[0]


def bias_body(smem, get, outs):
    place, table = smem
    (rows_ref,) = outs
    span = rows_ref.shape[1]
    heads = table.shape[1] // groups
    buckets = bucket_row(span, table.shape[0] // 2)
    for h in range(heads):
        head = place[0] * heads + h
        row = jnp.full((1, span), table[0, head], f32)
        for b in range(1, table.shape[0]):
            row = jnp.where(buckets == b, table[b, head], row)
        rows_ref[h : h + 1, :] = row


def bias_rows(place, table, span):
    return kernel_call(bias_body, "bias_rows", [place, table], [], [shaped(f32, 8, span)], us=1)[0]


def project(place, tokens, segment_ids, gain, w_query, w_key, w_value):
    tok, width = tokens.shape
    span = -(-(3 * width // groups + 1) // 128) * 128
    return kernel_call(
        project_body,
        "project",
        [place],
        [tokens, segment_ids, gain, w_query, w_key, w_value],
        [shaped(bf16, tok, span)] * 4 + [shaped(bf16, tok, width)],
        scratch=[pltpu.VMEM((3, tok, width), bf16)],
        staged=(0, 1, 3, 4, 5),
        mebibytes=10,
        us=4,
    )


def project_body(smem, get, outs, weight_scr, normed_scr, all_scr, *, count):
    (place,) = smem
    kv_ref, q_ref, normed_ref = outs
    group = place[0]
    tok = q_ref.shape[1]
    s_count = kv_ref.shape[1]
    local = q_ref.shape[2]
    window, late = group_window(group, local)
    for i in range(3):
        both = get(count + 1 + i)[:, pl.ds(window, -(-local // 128) * 128)]
        weight_scr[:, i * local : (i + 1) * local] = jnp.where(
            late, both[:, both.shape[1] - local :], both[:, :local]
        )
    gain = get(count)[...]
    for e in range(s_count):
        for d in range(count):
            values = get(d)[e, :tok, :].astype(f32)
            normed_scr[d * tok : (d + 1) * tok, :] = (values * rms_scale(values) * gain).astype(bf16)
        all_scr[...] = dot(normed_scr[...], weight_scr[...], 1, 0).astype(bf16)
        for d in range(count):
            rows = all_scr[d * tok : (d + 1) * tok, :]
            kv_ref[d, e, :, : 2 * local] = rows[:, local:]
            row = jnp.broadcast_to(get(d)[e, tok : tok + 1, :tok].astype(f32), (tok, tok))
            kv_ref[d, e, :, 2 * local :] = jnp.transpose(row).astype(bf16)
            if e == 0:
                q_ref[d] = rows[:, :local]
                normed_ref[d * tok : (d + 1) * tok, :] = normed_scr[d * tok : (d + 1) * tok, :]


def project(place, blocks, gain, w_query, w_key, w_value):
    s_count, rows, width = blocks[0].shape
    tok = rows - 16
    local = width // groups
    count = len(blocks)
    return kernel_call(
        functools.partial(project_body, count=count),
        "project",
        [place],
        [*blocks, gain, w_query, w_key, w_value],
        [
            shaped(bf16, count, s_count, tok, 2 * local + tok),
            shaped(bf16, count, tok, local),
            shaped(bf16, count * tok, width),
        ],
        scratch=[
            pltpu.VMEM((width, 3 * local), bf16),
            pltpu.VMEM((count * tok, width), bf16),
            pltpu.VMEM((count * tok, 3 * local), bf16),
        ],
        mebibytes=8,
        us=3,
    )


def forward_body(smem, get, outs, segk, strip, s_scr, p_scr, sems, *, blocks, chunk):
    (place,) = smem
    ctx = outs[0:4]
    q_ref, k_ref, v_ref, o_ref, p_hbm = outs[4:9]
    group, core, s_own = place[0], place[1], place[2]
    tok = 128
    head_size = 64
    s_count = blocks // 8
    local = q_ref.shape[1]
    seq = blocks * tok
    chunks = seq // chunk

    def block_of(d, e, k):
        return (((group ^ d) * s_count + (s_own ^ e)) * 2) + (core if k == 0 else 1 - core)

    def load_chunk(e):
        for k in range(2):
            for d in range(4):
                source, at = (get(2 * k), d) if d < 3 else (get(2 * k + 1), 0)
                start = pl.multiple_of(block_of(d, e, k) * tok, tok)
                k_ref[pl.ds(start, tok), :] = source[at, e, :, :local]
                v_ref[pl.ds(start, tok), :] = source[at, e, :, local : 2 * local]
                row = jnp.transpose(source[at, e, :, 2 * local :].astype(f32))
                segk[0:1, pl.ds(start, tok)] = row[0:1]

    load_chunk(0)
    for d in range(4):
        q_ref[d * tok : (d + 1) * tok, :] = get(4)[d] if d < 3 else get(5)[0]
    if s_count > 1:

        @pl.loop(1, s_count)
        def _(e):
            load_chunk(e)

    def p_copy(slot, h, d):
        return pltpu.make_async_copy(
            p_scr.at[slot], p_hbm.at[h, :, pl.ds(d * tok, tok), :], sems.at[slot]
        )

    heads = local // head_size
    rows_at_once = 32
    pending = {}
    span = 4 * tok
    for h in range(heads):
        cols = slice(h * head_size, (h + 1) * head_size)
        bias_row = get(6)[h : h + 1, :]
        spread = jnp.broadcast_to(bias_row, (tok, span))
        near = pltpu.roll(spread, 0, 1, stride=1, stride_axis=0)
        strip[:, tok * (blocks - 2) : tok * (blocks + 1)] = near[:, tok : 4 * tok]
        strip[:, : tok * (blocks - 2)] = jnp.broadcast_to(
            bias_row[:, :1], (tok, tok * (blocks - 2))
        )
        strip[:, tok * (blocks + 1) :] = jnp.broadcast_to(
            bias_row[:, span - 1 :], (tok, tok * (blocks - 2))
        )
        for d in range(4):
            query_block = block_of(d, 0, 0)
            strip_base = tok * (blocks - 1) - query_block * tok
            source, at = (get(0), d) if d < 3 else (get(1), 0)
            seg_col = source[at, 0, :, 2 * local : 2 * local + 1].astype(f32)
            slot = (h * 4 + d) % 2
            if slot in pending:
                pending.pop(slot).wait()
            queries = q_ref[d * tok : (d + 1) * tok, cols]
            if chunks == 1:
                s_scr[slot] = dot(queries, k_ref[:, cols], 1, 1)
                for r in range(0, tok, rows_at_once):
                    rows = slice(r, r + rows_at_once)
                    bias = strip[rows, pl.ds(pl.multiple_of(strip_base, tok), seq)]
                    scores = s_scr[slot, rows, :] + bias
                    scores = jnp.where(seg_col[rows] == segk[0:1, :], scores, masked_score)
                    top = jnp.max(scores, axis=1, keepdims=True)
                    exps = jnp.exp(scores - top)
                    total = jnp.sum(exps, axis=1, keepdims=True)
                    p_scr[slot, 0, rows, :] = (exps * (1.0 / total)).astype(bf16)
                weighted = jnp.dot(
                    p_scr[slot, 0], v_ref[:, cols], preferred_element_type=f32
                )
            else:
                def score_chunk(i, top):
                    start = pl.multiple_of(i * chunk, chunk)
                    scores = dot(queries, k_ref[pl.ds(start, chunk), cols], 1, 1)
                    base = pl.multiple_of(strip_base + start, tok)
                    scores = scores + strip[:, pl.ds(base, chunk)]
                    same = seg_col == segk[0:1, pl.ds(start, chunk)]
                    scores = jnp.where(same, scores, masked_score)
                    s_scr[0, :, pl.ds(start, chunk)] = scores
                    return jnp.maximum(top, jnp.max(scores, axis=1, keepdims=True))

                top = lax.fori_loop(
                    0, chunks, score_chunk, jnp.full((tok, 1), -3e38, f32)
                )

                def exp_chunk(i, total):
                    start = pl.multiple_of(i * chunk, chunk)
                    exps = jnp.exp(s_scr[0, :, pl.ds(start, chunk)] - top)
                    s_scr[0, :, pl.ds(start, chunk)] = exps
                    return total + jnp.sum(exps, axis=1, keepdims=True)

                total = lax.fori_loop(0, chunks, exp_chunk, jnp.zeros((tok, 1), f32))
                inverse = 1.0 / total

                def weigh_chunk(i, weighted):
                    start = pl.multiple_of(i * chunk, chunk)
                    low = (s_scr[0, :, pl.ds(start, chunk)] * inverse).astype(bf16)
                    p_scr[slot, i] = low
                    return weighted + jnp.dot(
                        low, v_ref[pl.ds(start, chunk), cols], preferred_element_type=f32
                    )

                weighted = lax.fori_loop(
                    0, chunks, weigh_chunk, jnp.zeros((tok, head_size), f32)
                )
            copy = p_copy(slot, h, d)
            copy.start()
            pending[slot] = copy
            o_ref[d * tok : (d + 1) * tok, cols] = weighted
            ctx[d][:, cols] = weighted.astype(bf16)
    for copy in pending.values():
        copy.wait()


def attention_forward(place, kv, q, bias):
    s_count, tok = kv[0].shape[1:3]
    local = q[0].shape[2]
    blocks = 8 * s_count
    seq = blocks * tok
    chunk = min(seq, 1024)
    shapes = (
        [shaped(bf16, tok, local)] * 4
        + [shaped(bf16, 4 * tok, local)]
        + [shaped(bf16, seq, local)] * 2
        + [shaped(f32, 4 * tok, local)]
        + [shaped(bf16, local // 64, seq // chunk, 4 * tok, chunk)]
    )
    return kernel_call(
        functools.partial(forward_body, blocks=blocks, chunk=chunk),
        "attention_forward",
        [place],
        [*kv, *q, bias],
        shapes,
        scratch=[
            pltpu.VMEM((8, seq), f32),
            pltpu.VMEM((tok, (2 * blocks - 1) * tok), f32),
            pltpu.VMEM((2 if seq == chunk else 1, tok, seq), f32),
            pltpu.VMEM((2, seq // chunk, tok, chunk), bf16),
            pltpu.SemaphoreType.DMA((2,)),
        ],
        in_hbm=(("out", 8),),
        mebibytes=8 if s_count == 1 else 60,
        us=10,
    )


def backward_body(
    smem, get, outs, p_scr, ds_scr, dctx_scr, strip, dq_scr, kv_scr, rows_scr, sems, *, blocks, chunk
):
    (place,) = smem
    p_hbm = get(8)
    dq = outs[0:4]
    keep_ref, send_ref, table_ref = outs[4:7]
    group, core, s_own = place[0], place[1], place[2]
    tok = 128
    head_size = 64
    seq = blocks * tok
    chunks = seq // chunk
    s_count = blocks // 8

    def p_copy(h, i, slot):
        return pltpu.make_async_copy(p_hbm.at[h, i], p_scr.at[slot], sems.at[slot])

    p_copy(0, 0, 0).start()
    for d in range(4):
        dctx_scr[d * tok : (d + 1) * tok, :] = get(d)[...]
    q_ref, k_ref, v_ref, o_ref = get(4), get(5), get(6), get(7)
    heads = q_ref.shape[1] // head_size
    rows_scr[...] = jnp.zeros_like(rows_scr)
    rows_at_once = 32
    for h in range(heads):
        cols = slice(h * head_size, (h + 1) * head_size)
        strip[...] = jnp.zeros_like(strip)
        out_grad = dctx_scr[:, cols]
        delta = jnp.sum(out_grad.astype(f32) * o_ref[:, cols], axis=1, keepdims=True)

        def run_chunk(i, h=h, cols=cols, out_grad=out_grad, delta=delta):
            start = pl.multiple_of(i * chunk, chunk)
            slot = (h * chunks + i) % 2
            following = h * chunks + i + 1

            @pl.when(following < heads * chunks)
            def _():
                p_copy(following // chunks, following % chunks, 1 - slot).start()

            p_copy(h, i, slot).wait()
            keys = k_ref[pl.ds(start, chunk), cols]
            values = v_ref[pl.ds(start, chunk), cols]
            for d in range(4):
                query_block = ((group ^ d) * s_count + s_own) * 2 + core
                base = pl.multiple_of(tok * (blocks - 1) - query_block * tok + start, tok)
                prob_grad = dot(out_grad[d * tok : (d + 1) * tok], values, 1, 1)
                for r in range(0, tok, rows_at_once):
                    rows = slice(d * tok + r, d * tok + r + rows_at_once)
                    here = prob_grad[r : r + rows_at_once] - delta[rows]
                    low = (p_scr[slot, rows, :].astype(f32) * here).astype(bf16)
                    ds_scr[rows, :] = low
                    strip[r : r + rows_at_once, pl.ds(base, chunk)] += low.astype(f32)
            scores_grad = ds_scr[...]
            part = jnp.dot(scores_grad, keys, preferred_element_type=f32)
            if chunks == 1:
                dq_scr[:, cols] = part
            else:
                dq_scr[:, cols] += part
            queries = q_ref[:, cols]
            kv_scr[0, pl.ds(start, chunk), :] = dot(scores_grad, queries, 0, 0).astype(bf16)
            kv_scr[1, pl.ds(start, chunk), :] = dot(p_scr[slot], out_grad, 0, 0).astype(bf16)

        if chunks == 1:
            run_chunk(0)
        else:
            dq_scr[:, cols] = jnp.zeros((4 * tok, head_size), f32)
            pl.loop(0, chunks)(run_chunk)

        def place_rows(e, h=h, cols=cols):
            for d in range(4):
                for k, target in ((0, keep_ref), (1, send_ref)):
                    block = ((group ^ d) * s_count + (s_own ^ e)) * 2 + (core if k == 0 else 1 - core)
                    start = pl.multiple_of(block * tok, tok)
                    width = heads * head_size
                    target[e, d, :, cols] = kv_scr[0, pl.ds(start, tok), :]
                    shifted = slice(width + h * head_size, width + (h + 1) * head_size)
                    target[e, d, :, shifted] = kv_scr[1, pl.ds(start, tok), :]

        if s_count == 1:
            place_rows(0)
        else:
            pl.loop(0, s_count)(place_rows)
        near = strip[:, tok * (blocks - 2) : tok * (blocks + 1)]
        left = jnp.zeros((1, tok), f32)
        right = jnp.zeros((1, tok), f32)
        for t in range(blocks - 2):
            left = left + jnp.sum(strip[:, t * tok : (t + 1) * tok], axis=0, keepdims=True)
            far = (blocks + 1 + t) * tok
            right = right + jnp.sum(strip[:, far : far + tok], axis=0, keepdims=True)
        rows_scr[h : h + 1, :] = jnp.concatenate([left, jnp.zeros((1, 2 * tok), f32), right], axis=1)
        spread = jnp.concatenate([jnp.zeros((tok, tok), f32), near], axis=1)
        skewed = spread[:8]
        for j in range(1, tok // 8):
            skewed = skewed + pltpu.roll(spread[8 * j : 8 * j + 8], 4 * tok - 8 * j, 1)
        row = lax.broadcasted_iota(jnp.int32, skewed.shape, 0)
        for step in (1, 2, 4):
            moved = pltpu.roll(skewed, 4 * tok - step, 1)
            skewed = jnp.where((row & step) != 0, moved, skewed)
        rows_scr[h : h + 1, :] += jnp.sum(skewed, axis=0, keepdims=True)
    for d in range(4):
        dq[d][...] = dq_scr[d * tok : (d + 1) * tok, :].astype(bf16)
    span = 4 * tok
    bucket_count = 2 * (len(cutoffs) + 1)
    buckets = bucket_row(span, bucket_count // 2)
    sums = rows_scr[...]
    lane = lax.broadcasted_iota(jnp.int32, (8, tok), 1)
    table = jnp.zeros((8, tok), f32)
    for b in range(bucket_count):
        picked = jnp.where(buckets == b, sums, 0.0)
        table = jnp.where(lane == b, jnp.sum(picked, axis=1, keepdims=True), table)
    table_ref[...] = table


def attention_backward(place, dctx, q, k, v, o, p):
    tok, local = dctx[0].shape
    seq = k.shape[0]
    blocks = seq // tok
    s_count = blocks // 8
    chunk = p.shape[3]
    shapes = (
        [shaped(bf16, tok, local)] * 4
        + [shaped(bf16, s_count, 4, tok, 2 * local)] * 2
        + [shaped(f32, 8, tok)]
    )
    return kernel_call(
        functools.partial(backward_body, blocks=blocks, chunk=chunk),
        "attention_backward",
        [place],
        [*dctx, q, k, v, o, p],
        shapes,
        scratch=[
            pltpu.VMEM((2, 4 * tok, chunk), bf16),
            pltpu.VMEM((4 * tok, chunk), bf16),
            pltpu.VMEM((4 * tok, local), bf16),
            pltpu.VMEM((tok, (2 * blocks - 1) * tok), f32),
            pltpu.VMEM((4 * tok, local), f32),
            pltpu.VMEM((2, seq, 64), bf16),
            pltpu.VMEM((8, 4 * tok), f32),
            pltpu.SemaphoreType.DMA((2,)),
        ],
        in_hbm=(8,),
        staged=tuple(("out", i) for i in range(6)) if s_count == 1 else (),
        mebibytes=13 if s_count == 1 else 60,
        us=7,
    )


def gated(gate, up):
    root = 0.7978845608028654
    square = gate * gate
    bend = jnp.tanh(root * (gate + 0.044715 * (gate * square)))
    act = 0.5 * gate * (1.0 + bend)
    slope = 0.5 * (1.0 + bend) + 0.5 * gate * (1.0 - bend * bend) * (
        root * (1.0 + 3.0 * 0.044715 * square)
    )
    return act, up * slope


def ffn_forward_body(smem, get, outs):
    (place,) = smem
    middle_ref, normed_ref, hidden_ref, act_ref, slope_ref = outs
    count = 4
    w_out, w_gate, w_up = get(6), get(7), get(8)
    group = place[0]
    tok, width = middle_ref.shape
    local = width // groups
    total = get(4)[...].astype(f32)
    for d in range(4):
        start = pl.multiple_of((group ^ d) * local, local)
        total = total + dot(get(d)[...], w_out[pl.ds(start, local), :], 1, 0)
    middle_ref[...] = total
    normed = (total * rms_scale(total) * get(5)[...]).astype(bf16)
    normed_ref[...] = normed
    step = w_gate.shape[1] // count
    for i in range(count):
        cols = slice(i * step, (i + 1) * step)
        up = dot(normed, w_up[:, cols], 1, 0)
        act, slope = gated(dot(normed, w_gate[:, cols], 1, 0), up)
        act_ref[:, cols] = act
        slope_ref[:, cols] = slope
        hidden_ref[:, cols] = (act * up).astype(bf16)


def ffn_forward(place, ctx, tokens, gain, w_out, w_gate, w_up):
    tok, width = tokens.shape
    ff = w_gate.shape[1]
    return kernel_call(
        ffn_forward_body,
        "ffn_forward",
        [place],
        [*ctx, tokens, gain, w_out, w_gate, w_up],
        [
            shaped(f32, tok, width),
            shaped(bf16, tok, width),
            shaped(bf16, tok, ff),
            shaped(f32, tok, ff),
            shaped(f32, tok, ff),
        ],
        staged=(4,),
        us=14,
    )


def ffn_backward_body(smem, get, outs, attn_scr):
    (place,) = smem
    out_ref, grad_ref, gain_grad_ref = outs[0:3]
    dctx = outs[3:7]
    mine_ref, far_ref = outs[7:9]
    w_down, w_gate, w_up, w_out = get(10), get(11), get(12), get(13)
    count = 4
    group, across = place[0], place[4]
    tok, width = grad_ref.shape
    ff = w_gate.shape[1]
    local = width // groups
    cot = get(0)[...]
    step = ff // count
    act_ref, slope_ref = get(3), get(4)
    normed_grad = jnp.zeros((tok, width), f32)
    for i in range(count):
        cols = slice(i * step, (i + 1) * step)
        hidden_grad = dot(cot, w_down[cols, :], 1, 1)
        gate = (hidden_grad * slope_ref[:, cols]).astype(bf16)
        up = (hidden_grad * act_ref[:, cols]).astype(bf16)
        normed_grad = normed_grad + dot(gate, w_gate[:, cols], 1, 1) + dot(up, w_up[:, cols], 1, 1)
    middle = get(1)[...]
    scale = rms_scale(middle)
    unit = middle * scale
    scaled = normed_grad * get(5)[...]
    gain_grad_ref[...] = jnp.sum(normed_grad * unit, axis=0, keepdims=True)
    middle_grad = cot.astype(f32) + scale * (
        scaled - unit * jnp.mean(unit * scaled, axis=1, keepdims=True)
    )
    grad_ref[...] = middle_grad
    attn = middle_grad.astype(bf16)
    attn_scr[...] = attn
    for d in range(4):
        start = pl.multiple_of((group ^ d) * local, local)
        dctx[d][...] = dot(attn, w_out[pl.ds(start, local), :], 1, 1).astype(bf16)
    for ref, which in ((mine_ref, across), (far_ref, 1 - across)):
        for d in range(4):
            ref[:, d * local : (d + 1) * local] = get(6 + d)[...]
        start = pl.multiple_of(which * (width // 2), width // 2)
        ref[:, width:] = attn_scr[:, pl.ds(start, width // 2)]
    out_ref[...] = (middle + dot(get(2)[...], w_down[...], 1, 0)).astype(bf16)


def ffn_backward(place, cot, middle, hidden, act, slope, gain, ctx, w_down, w_gate, w_up, w_out):
    tok, width = cot.shape
    local = width // groups
    return kernel_call(
        ffn_backward_body,
        "ffn_backward",
        [place],
        [cot, middle, hidden, act, slope, gain, *ctx, w_down, w_gate, w_up, w_out],
        [shaped(bf16, tok, width), shaped(f32, tok, width), shaped(f32, 1, width)]
        + [shaped(bf16, tok, local)] * 4
        + [shaped(bf16, tok, width + width // 2)] * 2,
        scratch=[pltpu.VMEM((tok, width), bf16)],
        mebibytes=6,
        us=6,
    )


def split_rows(total, wide, odd, kept_ref, sent_ref, cols):
    block = total.shape[0] // wide
    for i in range(wide // 2):
        even_rows = total[2 * i * block : (2 * i + 1) * block, :]
        odd_rows = total[(2 * i + 1) * block : (2 * i + 2) * block, :]
        kept_ref[i, :, cols] = jnp.where(odd, odd_rows, even_rows)
        sent_ref[i, :, cols] = jnp.where(odd, even_rows, odd_rows).astype(bf16)


def down_grad_body(smem, get, outs, cot_scr, hidden_scr, total_scr, *, wide):
    (place,) = smem
    kept_ref, sent_ref, gate_ref, up_ref, normed_scr = outs
    odd = place[3] == 1
    rows, quarter = hidden_scr.shape
    tok = rows // 4
    width = normed_scr.shape[1]
    local = width // groups
    for i in range(4):
        normed_scr[i * tok : (i + 1) * tok, :] = get(i)[...]
        cot_scr[i * tok : (i + 1) * tok, :] = get(4 + i)[...]
    start = pl.multiple_of((place[4] * 2 + place[1]) * quarter, quarter)
    half = quarter // 2
    for i in range(2):
        cols = slice(i * half, (i + 1) * half)
        part = pl.ds(pl.multiple_of(start + i * half, half), half)
        up = dot(normed_scr[...], get(9)[:, part], 1, 0)
        act, slope = gated(dot(normed_scr[...], get(8)[:, part], 1, 0), up)
        hidden_scr[:, cols] = (act * up).astype(bf16)
        hidden_grad = dot(cot_scr[...], get(10)[part, :], 1, 1)
        gate_ref[:, cols] = (hidden_grad * slope).astype(bf16)
        up_ref[:, cols] = (hidden_grad * act).astype(bf16)
    total_scr[...] = dot(hidden_scr[...], cot_scr[...], 0, 0)
    blocks = wide // groups
    block = quarter // blocks
    for i in range(wide // 2):
        g, j = 2 * i // blocks, 2 * i % blocks
        cols = slice(g * local, (g + 1) * local)
        even_rows = total_scr[j * block : (j + 1) * block, cols]
        odd_rows = total_scr[(j + 1) * block : (j + 2) * block, cols]
        kept_ref[i] = jnp.where(odd, odd_rows, even_rows)
        sent_ref[i] = jnp.where(odd, even_rows, odd_rows).astype(bf16)


def down_grad(place, normed, cot, w_gate, w_up, w_down, wide):
    tok, width = normed[0].shape
    ff = w_gate.shape[1]
    shape = (wide // 2, ff // wide, width // groups)
    return kernel_call(
        functools.partial(down_grad_body, wide=wide),
        "down_grad",
        [place],
        [*normed, *cot, w_gate, w_up, w_down],
        [shaped(f32, *shape), shaped(bf16, *shape)]
        + [shaped(bf16, 4 * tok, ff // 4)] * 2
        + [shaped(bf16, 4 * tok, width)],
        scratch=[
            pltpu.VMEM((4 * tok, width), bf16),
            pltpu.VMEM((4 * tok, ff // 4), bf16),
            pltpu.VMEM((ff // 4, width), f32),
        ],
        mebibytes=10,
        us=1,
    )


def up_grad_body(smem, get, outs, total_scr, *, wide):
    (place,) = smem
    total_scr[...] = dot(get(0)[...], get(1)[...], 0, 0)
    split_rows(total_scr, wide, place[3] == 1, *outs, slice(None))


def up_grad(place, normed, grad, wide):
    width = normed.shape[1]
    quarter = grad.shape[1]
    shape = (wide // 2, width // wide, quarter)
    return kernel_call(
        functools.partial(up_grad_body, wide=wide),
        "up_grad",
        [place],
        [normed, grad],
        [shaped(f32, *shape), shaped(bf16, *shape)],
        scratch=[pltpu.VMEM((width, quarter), f32)],
        mebibytes=5,
        us=0.5,
    )


def gate_grad_body(
    smem, get, outs, ctx_scr, attn_scr, total_scr, out_scr, *, wide
):
    (place,) = smem
    group, core, odd = place[0], place[1], place[3] == 1
    rows, width = get(0).shape
    tok = rows // 4
    local = width // groups
    quarter = total_scr.shape[1]
    for i in range(4):
        rows = slice(i * tok, (i + 1) * tok)
        ctx_scr[rows, :] = get(2 + i)[:, :width]
        both = get(2 + i)[:, width:]
        attn_scr[rows, :] = jnp.where(core == 0, both[:, :local], both[:, local:])
    total_scr[...] = dot(get(0)[...], get(1)[...], 0, 0)
    split_rows(total_scr, wide, odd, *outs, slice(0, quarter))
    turned = dot(ctx_scr[...], attn_scr[...], 0, 0)
    for d in range(4):
        start = pl.multiple_of((group ^ d) * local, local)
        out_scr[pl.ds(start, local), :] = turned[d * local : (d + 1) * local]
    split_rows(out_scr, wide, odd, *outs, slice(quarter, quarter + local))


def gate_grad(place, normed, grad, attn, wide):
    rows, width = normed.shape
    quarter = grad.shape[1]
    local = width // groups
    shape = (wide // 2, width // wide, quarter + local)
    return kernel_call(
        functools.partial(gate_grad_body, wide=wide),
        "gate_grad",
        [place],
        [normed, grad, *attn],
        [shaped(f32, *shape), shaped(bf16, *shape)],
        scratch=[
            pltpu.VMEM((rows, width), bf16),
            pltpu.VMEM((rows, local), bf16),
            pltpu.VMEM((width, quarter), f32),
            pltpu.VMEM((width, local), f32),
        ],
        mebibytes=8,
        us=0.5,
    )


def collect_body(smem, get, outs):
    local = outs[0].shape[1] // 3
    for d in range(4):
        outs[d][:, :local] = get(d)[...]
    for d in range(4):
        total = get(4)[d].astype(f32) + get(5)[d].astype(f32)
        outs[d][:, local:] = total.astype(bf16)


def collect(dq, kept, received):
    tok, local = dq[0].shape
    return kernel_call(
        collect_body,
        "collect",
        [],
        [*dq, kept, received],
        [shaped(bf16, tok, 3 * local)] * 4,
        staged=tuple(range(6)),
        us=0.5,
    )


def exact(small):
    high = small.astype(bf16)
    return high, (small - high.astype(f32)).astype(bf16)


def attach(ref, rows, small):
    high, low = exact(small)
    ref[rows : rows + small.shape[0], : small.shape[1]] = high
    ref[rows : rows + small.shape[0], small.shape[1] : 2 * small.shape[1]] = low


def attached(ref, rows, small):
    count, lanes = small.shape
    high, low = exact(small)
    theirs = ref[rows : rows + count, :lanes].astype(f32)
    theirs = theirs + ref[rows : rows + count, lanes : 2 * lanes].astype(f32)
    return high.astype(f32) + low.astype(f32) + theirs


def qkv_grad_body(smem, get, outs, grad_scr, total_scr):
    (place,) = smem
    kept_ref, sent_ref, small_ref = outs
    group, core = place[0], place[1]
    width, span = total_scr.shape
    local = span // 3
    tok = grad_scr.shape[0] // 4
    for d in range(4):
        grad_scr[d * tok : (d + 1) * tok, :] = get(d)[...]
    total_scr[...] = dot(get(4)[...], grad_scr[: 3 * tok, :], 0, 0)
    total_scr[...] += dot(get(11)[...], grad_scr[3 * tok :, :], 0, 0)
    quarter = width // 4
    for i in range(2):
        start = pl.multiple_of((2 * i + core) * quarter, quarter)
        kept_ref[i] = total_scr[pl.ds(start, quarter), :]
        start = pl.multiple_of((2 * i + 1 - core) * quarter, quarter)
        sent_ref[i * quarter : (i + 1) * quarter, :] = total_scr[pl.ds(start, quarter), :].astype(bf16)
    window, late = group_window(group, local)
    ones = jnp.ones((8, local), bf16)
    gain_grad = jnp.zeros((8, width), f32)
    for i in range(3):
        both = get(8 + i)[:, pl.ds(window, -(-local // 128) * 128)]
        weight = jnp.where(late, both[:, both.shape[1] - local :], both[:, :local])
        product = total_scr[:, i * local : (i + 1) * local] * weight.astype(f32)
        high, rest = exact(product)
        gain_grad = gain_grad + dot(ones, high, 1, 1) + dot(ones, rest, 1, 1)
    gain_grad = gain_grad[0:1] / get(5)[...]
    ffn_gain = get(6)[...]
    lanes = 128
    rows = width // lanes
    for i in range(rows):
        small_ref[i : i + 1, :] = gain_grad[:, i * lanes : (i + 1) * lanes]
        small_ref[rows + i : rows + i + 1, :] = ffn_gain[:, i * lanes : (i + 1) * lanes]
    heads = (small_ref.shape[0] - 2 * rows) // groups
    table = get(7)[:heads, :]
    for i in range(groups):
        at = 2 * rows + i * heads
        small_ref[at : at + heads, :] = jnp.where(group == i, table, 0.0)
    sent_ref[2 * quarter :, :] = jnp.zeros((sent_ref.shape[0] - 2 * quarter, span), bf16)
    attach(sent_ref, 2 * quarter, small_ref[...])


def room(count):
    return -(-count // 16) * 16


def qkv_grad(
    place, grads, normed_first, normed_last, gain, gain_grad, table, head_count, w_query, w_key, w_value
):
    rows, width = 4 * grads[0].shape[0], normed_first.shape[1]
    span = grads[0].shape[1]
    count = 2 * width // 128 + head_count
    return kernel_call(
        qkv_grad_body,
        "qkv_grad",
        [place],
        [*grads, normed_first, gain, gain_grad, table, w_query, w_key, w_value, normed_last],
        [
            shaped(f32, 2, width // 4, span),
            shaped(bf16, width // 2 + room(count), span),
            shaped(f32, count, 128),
        ],
        scratch=[pltpu.VMEM((rows, span), bf16), pltpu.VMEM((width, span), f32)],
        mebibytes=7,
        us=0.5,
    )


def qkv_sum_body(smem, get, outs, *, axis):
    (place,) = smem
    kept, small, received = get(0), get(1), get(2)
    parts, rows, span = kept.shape
    totals = [
        kept[i] + received[i * rows : (i + 1) * rows, :].astype(f32) for i in range(parts)
    ]
    summed = attached(received, parts * rows, small[...])
    if axis == "y":
        for i in range(parts):
            outs[0][i] = totals[i].astype(outs[0].dtype)
        outs[1][...] = summed
        return
    kept_ref, sent_ref, small_ref = outs
    small_ref[...] = summed
    if axis == "core":
        far = place[4] == 1
        mine, theirs = jnp.where(far, totals[1], totals[0]), jnp.where(far, totals[0], totals[1])
        blocks, block = kept_ref.shape[0], kept_ref.shape[1]
        for i in range(blocks):
            kept_ref[i] = mine[i * block : (i + 1) * block]
        sent_ref[:rows, :] = theirs.astype(bf16)
    else:
        odd = place[3] == 1
        for i in range(parts // 2):
            kept_ref[i] = jnp.where(odd, totals[2 * i + 1], totals[2 * i])
            theirs = jnp.where(odd, totals[2 * i], totals[2 * i + 1])
            sent_ref[i * rows : (i + 1) * rows, :] = theirs.astype(bf16)
    filled = sent_ref.shape[0] - room(small.shape[0])
    sent_ref[filled:, :] = jnp.zeros((room(small.shape[0]), span), bf16)
    attach(sent_ref, filled, summed)


def qkv_sum(place, kept, small, received, axis, s_count, wide):
    parts, rows, span = kept.shape
    count = small.shape[0]
    if axis == "core":
        shape, sent = (2 * s_count, rows // (2 * s_count), span), rows
    else:
        shape, sent = (parts // 2, rows, span), parts // 2 * rows
    if axis == "y":
        outputs = [shaped(bf16 if s_count == 1 else f32, *kept.shape)]
    else:
        outputs = [shaped(f32, *shape), shaped(bf16, sent + room(count), span)]
    return kernel_call(
        functools.partial(qkv_sum_body, axis=axis),
        f"qkv_sum_{axis}",
        [place],
        [kept, small, received],
        outputs + [shaped(f32, count, 128)],
        us=0.5,
    )


def input_grad_body(smem, get, outs, all_scr):
    (place,) = smem
    group = place[0]
    weights = [get(7 + i) for i in range(3)]
    local = get(0).shape[1] // 3
    window = -(-local // 128) * 128
    tok = get(0).shape[0]
    spare = jnp.zeros((tok, window - local), bf16)
    all_scr[...] = jnp.zeros_like(all_scr)
    for d in range(4):
        start, late = group_window(group ^ d, local)
        grads = get(d)[...]
        for i in range(3):
            part = grads[:, i * local : (i + 1) * local]
            part = jnp.where(
                late,
                jnp.concatenate([spare, part], axis=1),
                jnp.concatenate([part, spare], axis=1),
            )
            all_scr[i, :, pl.ds(start, window)] += part
    normed_grad = dot(all_scr[0], weights[0][...], 1, 1)
    for i in range(1, 3):
        normed_grad = normed_grad + dot(all_scr[i], weights[i][...], 1, 1)
    values = get(4)[...].astype(f32)
    scale = rms_scale(values)
    unit = values * scale
    scaled = normed_grad * get(5)[...]
    outs[0][...] = get(6)[...] + scale * (
        scaled - unit * jnp.mean(unit * scaled, axis=1, keepdims=True)
    )


def final_input_grad(place, grads, tokens, gain, middle_grad, w_query, w_key, w_value):
    return kernel_call(
        input_grad_body,
        "input_grad",
        [place],
        [*grads, tokens, gain, middle_grad, w_query, w_key, w_value],
        [shaped(f32, *tokens.shape)],
        scratch=[pltpu.VMEM((3, *tokens.shape), bf16)],
        staged=(0, 1, 2, 3, 4, 6),
        mebibytes=6,
        us=0.5,
    )[0]


def add_split_body(smem, get, outs, *, bit, splits):
    (place,) = smem
    kept, received = get(0), get(1)
    if kept.shape[0] == 1:
        total = kept[0].astype(f32) + received[0].astype(f32)
        at = 0
        for i, span in enumerate(splits):
            outs[i][...] = total[:, at : at + span].astype(outs[i].dtype)
            at += span
        return
    odd = ((place[5] >> bit) & 1) == 1
    for i in range(kept.shape[0] // 2):
        even_rows = kept[2 * i].astype(f32) + received[2 * i].astype(f32)
        odd_rows = kept[2 * i + 1].astype(f32) + received[2 * i + 1].astype(f32)
        outs[1][i] = jnp.where(odd, even_rows, odd_rows).astype(bf16)
        outs[0][i] = jnp.where(odd, odd_rows, even_rows)


def wide_sum(layout, place, kept, sent, bit, splits, name, us, first=(), last=f32):
    received = layout.wide_bit(sent, bit)
    kept = after(kept, first)
    remaining, block, columns = kept.shape
    if remaining == 1:
        outputs = [shaped(last, block, span) for span in splits]
    else:
        shape = (remaining // 2, block, columns)
        outputs = [shaped(f32, *shape), shaped(bf16, *shape)]
    return kernel_call(
        functools.partial(add_split_body, bit=bit + 1, splits=splits),
        f"{name}_sum",
        [place],
        [kept, received],
        outputs,
        us=us,
    )


def turned_down_body(smem, get, outs):
    outs[0][...] = jnp.transpose(get(0)[...].astype(f32))


def turned_down(block):
    return kernel_call(
        turned_down_body, "down_out", [], [block], [shaped(f32, *block.shape[::-1])], us=1
    )[0]


def after(values, done):
    return lax.optimization_barrier((values, done))[0]


def halved(block, axis, keep):
    return (
        lax.dynamic_index_in_dim(block, keep, axis, keepdims=False),
        lax.dynamic_index_in_dim(block, 1 - keep, axis, keepdims=False),
    )


def on_device(
    inputs,
    segment_ids,
    gain_attn,
    w_query,
    w_key,
    w_value,
    w_out,
    gain_ffn,
    w_gate,
    w_up,
    w_down,
    bias_table,
    cotangent,
):
    layout = Layout(lax.axis_size("narrow"), lax.axis_size("wide"))
    s_count = layout.s_count
    tokens = inputs[0]
    out_grad = cotangent[0]
    tok, width = tokens.shape
    local = width // groups
    ff = w_gate.shape[1]
    bucket_count, head_count = bias_table.shape
    narrow = lax.axis_index("narrow")
    wide = lax.axis_index("wide")
    core = narrow % 2
    across = narrow // 2
    group = wide // (2 * s_count)
    s_own = (wide // 2) % s_count
    y_own = wide % 2
    place = jnp.stack([group, core, s_own, y_own, across, wide]).astype(jnp.int32)
    gain_attn = gain_attn[None]
    gain_ffn = gain_ffn[None]

    packet = packed(tokens, segment_ids)
    own = [layout.turned(packet, d)[None] for d in range(3)]
    own.append(layout.wide_bit(own[2], layout.wide.bit_length() - 3))
    for d in range(4):
        size = 1
        while size < s_count:
            own[d] = jnp.concatenate([own[d], layout.wide_bit(own[d], size.bit_length())], axis=0)
            size *= 2
    cot_across = layout.across(out_grad)
    bias = bias_rows(place, bias_table, 4 * tok)
    kv_first, q_first, normed_first = project(place, own[:3], gain_attn, w_query, w_key, w_value)
    kv_first = after(kv_first, (bias, cot_across))
    kv_last, q_last, normed_last = project(place, own[3:], gain_attn, w_query, w_key, w_value)
    kv = [kv_first, kv_last, layout.core(kv_first), layout.core(kv_last)]
    outs = attention_forward(place, kv, [q_first, q_last], bias)
    ctx_parts = outs[:4]
    q_own, k_all, v_all, o_own, probs = outs[4:]
    ctx = [layout.turned(ctx_parts[d], d) for d in range(4)]
    cot = [out_grad, layout.core(out_grad), cot_across, layout.core(cot_across)]
    ctx = after(ctx, cot)

    middle, normed_ffn, hidden, act, slope = ffn_forward(
        place, ctx, tokens, gain_ffn, w_out, w_gate, w_up
    )
    normed_across = layout.across(normed_ffn)
    back = ffn_backward(
        place, out_grad, middle, hidden, act, slope, gain_ffn, ctx, w_down, w_gate, w_up, w_out
    )
    output, middle_grad, grad_gain_ffn = back[0:3]
    dctx = [layout.turned(back[3 + d], d) for d in range(4)]
    mine, far = back[7:9]
    normed_near, normed_across = after((normed_ffn, normed_across), back[3:7])
    normed_core = layout.core(normed_near)
    normed = [normed_ffn, normed_core, normed_across, layout.core(normed_across)]
    *down, gate, up, normed = down_grad(place, normed, cot, w_gate, w_up, w_down, layout.wide)

    dctx = after(dctx, down)
    back = attention_backward(place, dctx, q_own, k_all, v_all, o_own, probs)
    dq, kept, sent, table_rows = back[:4], back[4], back[5], back[6]
    received = layout.core(sent)
    size = s_count
    while size > 1:
        size //= 2
        total = kept.astype(f32) + received.astype(f32)
        kept = total[:size]
        received = layout.wide_bit(total[size:].astype(bf16), size.bit_length())

    far, mine, up = after((far, mine, up), sent)
    far = layout.across(far)
    mine_core = layout.core(mine)
    up = up_grad(place, normed, up, layout.wide)
    quarter_ff = ff // layout.narrow
    bits = layout.wide.bit_length() - 1
    width_sum = functools.partial(wide_sum, layout, place)
    down = width_sum(*down, 0, (local,), "down", 0.5, up, last=bf16)
    low_grads = collect(dq, after(kept[0], down), received[0])
    qkv_kept, qkv_sent, small = qkv_grad(
        place,
        low_grads,
        normed_first,
        normed_last,
        gain_attn,
        grad_gain_ffn,
        table_rows,
        head_count,
        w_query,
        w_key,
        w_value,
    )
    up = width_sum(*up, 0, (quarter_ff,), "up", 0.5, qkv_sent)
    far = after(far, low_grads)
    outs_parts = [mine, mine_core, far, layout.core(far)]
    normed = after(normed, up[0])
    gate = gate_grad(place, normed, gate, outs_parts, layout.wide)
    low_grads = after(low_grads, gate[1])
    returned = [layout.turned(low_grads[d], d) for d in range(4)]
    down = width_sum(*down, 1, (local,), "down", 0.5, gate, last=bf16)
    step = qkv_sum(
        place, after(qkv_kept, down), small, layout.core(qkv_sent), "core", s_count, layout.wide
    )
    up = width_sum(*up, 1, (quarter_ff,), "up", 0.5, step)
    for bit in range(2, bits):
        down = width_sum(*down, bit, (local,), "down", 0.5, up, last=bf16)
    step = qkv_sum(
        place, after(step[0], down), step[2], layout.across(step[1]), "x", s_count, layout.wide
    )
    gate = width_sum(*gate, 0, (quarter_ff, local), "gate", 0.5, step)
    middle_grad = after(middle_grad, gate)
    input_grad = final_input_grad(
        place, returned, tokens, gain_attn, middle_grad, w_query, w_key, w_value
    )
    for bit in range(2, bits):
        up = width_sum(*up, bit, (quarter_ff,), "up", 0.5, input_grad)
    part, small = qkv_sum(
        place, after(step[0], up), step[2], layout.wide_bit(step[1], 0), "y", s_count, layout.wide
    )
    gate = width_sum(*gate, 1, (quarter_ff, local), "gate", 0.5, part)
    small = after(small, gate[0])
    for bit in range(2, bits):
        gate = width_sum(*gate, bit, (quarter_ff, local), "gate", 0.5, part)
    rows = width // layout.wide
    size = s_count
    bit = 1
    while size > 1:
        size //= 2
        part = part.reshape(size, 2, rows, 3 * local)
        kept, sent = halved(part, 1, (s_own >> (bit - 1)) & 1)
        part = kept + layout.wide_bit(sent.astype(bf16), bit).astype(f32)
        bit += 1
    part = part.reshape(rows, 3 * local).astype(bf16)

    def to_owner(x, c, g, s, y):
        return (g // 2, g % 2, x * 2 + c, s, y)

    final_qkv = layout.send(part, to_owner).astype(f32)
    final_down = turned_down(layout.send(down[0], to_owner)).T
    (final_up,), (final_gate, final_out) = up, gate

    for bit in range(1, bits):
        small = small + layout.wide_bit(small, bit)
    gain_rows = width // 128
    sum_gain_attn = small[:gain_rows].reshape(width)
    sum_gain_ffn = small[gain_rows : 2 * gain_rows].reshape(width)
    sum_table = small[2 * gain_rows :, :bucket_count].T
    return (
        output[None],
        input_grad[None],
        sum_gain_attn,
        final_qkv[:, :local],
        final_qkv[:, local : 2 * local],
        final_qkv[:, 2 * local :],
        final_out,
        sum_gain_ffn,
        final_gate,
        final_up,
        final_down,
        sum_table,
    )


def solution(mesh):
    tokens = P("narrow", "wide", None)
    share = P("wide", "narrow")
    return jax.shard_map(
        on_device,
        mesh=mesh,
        in_specs=(tokens, P("narrow", "wide")) + (P(),) * 10 + (tokens,),
        out_specs=(
            tokens,
            tokens,
            P(),
            share,
            share,
            share,
            share,
            P(),
            share,
            share,
            share,
            P(),
        ),
        check_vma=False,
    )
```

```python
import functools

import jax
import jax.numpy as jnp
import numpy as np
from jax import lax
from jax.experimental import pallas as pl
from jax.experimental.pallas import tpu as pltpu
from jax.sharding import PartitionSpec as P

cutoffs = (1, 2, 3, 4, 5, 6, 7, 8, 12, 16, 23, 32, 46, 64, 91)
epsilon = 1e-06
masked_score = -1000000000.0
highest = lax.Precision.HIGHEST
axes = ("narrow", "wide")
groups = 4
bf16 = jnp.bfloat16
f32 = jnp.float32


def dot(left, right, left_dim, right_dim):
    return lax.dot_general(
        left, right, (((left_dim,), (right_dim,)), ((), ())), preferred_element_type=f32
    )


class Layout:
    def __init__(self, narrow, wide):
        self.narrow = narrow
        self.wide = wide
        self.s_count = wide // (groups * 2)

    def index(self, x, c, g, s, y):
        return (x * 2 + c) * self.wide + (g * self.s_count + s) * 2 + y

    def send(self, block, target):
        route = []
        for x in range(self.narrow // 2):
            for c in range(2):
                for g in range(groups):
                    for s in range(self.s_count):
                        for y in range(2):
                            route.append(
                                (self.index(x, c, g, s, y), self.index(*target(x, c, g, s, y)))
                            )
        return lax.ppermute(block, axes, route)

    def turned(self, block, d):
        return self.send(block, lambda x, c, g, s, y: (x, y, g ^ d, s, c))

    def core(self, block):
        return self.send(block, lambda x, c, g, s, y: (x, 1 - c, g, s, y))

    def across(self, block):
        return self.send(block, lambda x, c, g, s, y: (x ^ 1, c, g, s, y))

    def far_group(self, block):
        return self.wide_mask(block, self.wide // 2)

    def near_group(self, block):
        return self.wide_mask(block, self.wide // 4)

    def wide_bit(self, block, bit):
        return self.wide_mask(block, 1 << bit)

    def wide_mask(self, block, mask):
        def target(x, c, g, s, y):
            w = ((g * self.s_count + s) * 2 + y) ^ mask
            return (x, c, w // (2 * self.s_count), (w // 2) % self.s_count, w % 2)

        return self.send(block, target)


def rms_scale(values):
    return lax.rsqrt(jnp.mean(values * values, axis=-1, keepdims=True) + epsilon)


def bucket_row(span, half_count):
    offset = lax.broadcasted_iota(jnp.int32, (1, span), 1) - span // 2
    distance = jnp.abs(offset)
    bucket = jnp.where(offset > 0, half_count, 0)
    for cutoff in cutoffs:
        bucket = bucket + jnp.where(distance >= cutoff, 1, 0)
    return bucket


def cost(microseconds):
    return pl.CostEstimate(
        flops=int(microseconds * 1.15e9), bytes_accessed=1024, transcendentals=0
    )


def kernel_call(
    body, name, smem, inputs, outputs, scratch=(), in_hbm=(), staged=(), mebibytes=4, us=3
):
    n_smem, n_in, n_out = len(smem), len(inputs), len(outputs)
    ins = [i for i in staged if not isinstance(i, tuple)]
    leaving = [i[1] for i in staged if isinstance(i, tuple)]

    def kernel(*refs):
        given = refs[n_smem : n_smem + n_in]
        results = refs[n_smem + n_in : n_smem + n_in + n_out]
        rest = refs[n_smem + n_in + n_out :]
        buffers = dict(zip(ins, rest))
        drafts = dict(zip(leaving, rest[len(ins) :]))
        arrivals = {}
        for at, i in enumerate(ins):
            arrivals[i] = pltpu.make_async_copy(given[i], buffers[i], rest[-1].at[at])
            arrivals[i].start()

        def get(i):
            if i in arrivals:
                arrivals.pop(i).wait()
            return buffers.get(i, given[i])

        outs = [drafts.get(i, results[i]) for i in range(n_out)]
        body(refs[:n_smem], get, outs, *rest[len(staged) : len(rest) - (1 if staged else 0)])
        for i in ins:
            get(i)
        departures = [
            pltpu.make_async_copy(drafts[i], results[i], rest[-1].at[len(ins) + at])
            for at, i in enumerate(leaving)
        ]
        for copy in departures:
            copy.start()
        for copy in departures:
            copy.wait()

    hbm = pl.BlockSpec(memory_space=pltpu.HBM)
    vmem = pl.BlockSpec(memory_space=pltpu.VMEM)
    copies = [pltpu.SemaphoreType.DMA((len(staged),))] if staged else []
    return pl.pallas_call(
        kernel,
        out_shape=outputs,
        in_specs=[pl.BlockSpec(memory_space=pltpu.SMEM)] * n_smem
        + [hbm if i in in_hbm or i in ins else vmem for i in range(n_in)],
        out_specs=[hbm if ("out", i) in in_hbm or i in leaving else vmem for i in range(n_out)],
        scratch_shapes=[pltpu.VMEM(inputs[i].shape, inputs[i].dtype) for i in ins]
        + [pltpu.VMEM(outputs[i].shape, outputs[i].dtype) for i in leaving]
        + list(scratch)
        + copies,
        compiler_params=pltpu.CompilerParams(vmem_limit_bytes=mebibytes * 2**20),
        cost_estimate=cost(us),
        name=name,
    )(*smem, *inputs)


def shaped(dtype, *shape):
    return jax.ShapeDtypeStruct(shape, dtype)


def group_window(group, local):
    start = (group * local) // 128 * 128
    return pl.multiple_of(start, 128), (group * local) % 128 != 0


def pack_body(smem, get, outs):
    (packet,) = outs
    tok, width = get(0).shape
    row = jnp.broadcast_to(get(1)[...].astype(f32), (packet.shape[0] - tok, tok))
    packet[tok:, :tok] = row.astype(bf16)
    packet[tok:, tok:] = jnp.zeros((packet.shape[0] - tok, width - tok), bf16)
    packet[:tok, :] = get(0)[...]


def packed(tokens, segment_ids):
    tok, width = tokens.shape
    return kernel_call(
        pack_body,
        "pack",
        [],
        [tokens, segment_ids],
        [shaped(bf16, tok + 16, width)],
        staged=(0, 1),
        mebibytes=60,
        us=1,
    )[0]


def bias_body(smem, get, outs):
    place, table = smem
    (rows_ref,) = outs
    span = rows_ref.shape[1]
    heads = table.shape[1] // groups
    buckets = bucket_row(span, table.shape[0] // 2)
    for h in range(heads):
        head = place[0] * heads + h
        row = jnp.full((1, span), table[0, head], f32)
        for b in range(1, table.shape[0]):
            row = jnp.where(buckets == b, table[b, head], row)
        rows_ref[h : h + 1, :] = row


def bias_rows(place, table, span):
    return kernel_call(bias_body, "bias_rows", [place, table], [], [shaped(f32, 8, span)], us=1)[0]


def project(place, tokens, segment_ids, gain, w_query, w_key, w_value):
    tok, width = tokens.shape
    span = -(-(3 * width // groups + 1) // 128) * 128
    return kernel_call(
        project_body,
        "project",
        [place],
        [tokens, segment_ids, gain, w_query, w_key, w_value],
        [shaped(bf16, tok, span)] * 4 + [shaped(bf16, tok, width)],
        scratch=[pltpu.VMEM((3, tok, width), bf16)],
        staged=(0, 1, 3, 4, 5),
        mebibytes=10,
        us=4,
    )


def project_body(smem, get, outs, weight_scr, normed_scr, all_scr, *, count):
    (place,) = smem
    kv_ref, q_ref, normed_ref = outs
    group = place[0]
    tok = q_ref.shape[1]
    s_count = kv_ref.shape[1]
    local = q_ref.shape[2]
    window, late = group_window(group, local)
    for i in range(3):
        both = get(count + 1 + i)[:, pl.ds(window, -(-local // 128) * 128)]
        weight_scr[:, i * local : (i + 1) * local] = jnp.where(
            late, both[:, both.shape[1] - local :], both[:, :local]
        )
    gain = get(count)[...]
    for e in range(s_count):
        for d in range(count):
            values = get(d)[e, :tok, :].astype(f32)
            normed_scr[d * tok : (d + 1) * tok, :] = (values * rms_scale(values) * gain).astype(bf16)
        all_scr[...] = dot(normed_scr[...], weight_scr[...], 1, 0).astype(bf16)
        for d in range(count):
            rows = all_scr[d * tok : (d + 1) * tok, :]
            kv_ref[d, e, :, : 2 * local] = rows[:, local:]
            row = jnp.broadcast_to(get(d)[e, tok : tok + 1, :tok].astype(f32), (tok, tok))
            kv_ref[d, e, :, 2 * local :] = jnp.transpose(row).astype(bf16)
            if e == 0:
                q_ref[d] = rows[:, :local]
                normed_ref[d * tok : (d + 1) * tok, :] = normed_scr[d * tok : (d + 1) * tok, :]


def project(place, blocks, gain, w_query, w_key, w_value):
    s_count, rows, width = blocks[0].shape
    tok = rows - 16
    local = width // groups
    count = len(blocks)
    return kernel_call(
        functools.partial(project_body, count=count),
        "project",
        [place],
        [*blocks, gain, w_query, w_key, w_value],
        [
            shaped(bf16, count, s_count, tok, 2 * local + tok),
            shaped(bf16, count, tok, local),
            shaped(bf16, count * tok, width),
        ],
        scratch=[
            pltpu.VMEM((width, 3 * local), bf16),
            pltpu.VMEM((count * tok, width), bf16),
            pltpu.VMEM((count * tok, 3 * local), bf16),
        ],
        mebibytes=8,
        us=3,
    )


def forward_body(smem, get, outs, segk, strip, s_scr, p_scr, sems, *, blocks, chunk):
    (place,) = smem
    ctx = outs[0:4]
    q_ref, k_ref, v_ref, o_ref, p_hbm = outs[4:9]
    group, core, s_own = place[0], place[1], place[2]
    tok = 128
    head_size = 64
    s_count = blocks // 8
    local = q_ref.shape[1]
    seq = blocks * tok
    chunks = seq // chunk

    def block_of(d, e, k):
        return (((group ^ d) * s_count + (s_own ^ e)) * 2) + (core if k == 0 else 1 - core)

    def load_chunk(e):
        for k in range(2):
            for d in range(4):
                source, at = (get(2 * k), d) if d < 3 else (get(2 * k + 1), 0)
                start = pl.multiple_of(block_of(d, e, k) * tok, tok)
                k_ref[pl.ds(start, tok), :] = source[at, e, :, :local]
                v_ref[pl.ds(start, tok), :] = source[at, e, :, local : 2 * local]
                row = jnp.transpose(source[at, e, :, 2 * local :].astype(f32))
                segk[0:1, pl.ds(start, tok)] = row[0:1]

    load_chunk(0)
    for d in range(4):
        q_ref[d * tok : (d + 1) * tok, :] = get(4)[d] if d < 3 else get(5)[0]
    if s_count > 1:

        @pl.loop(1, s_count)
        def _(e):
            load_chunk(e)

    def p_copy(slot, h, d):
        return pltpu.make_async_copy(
            p_scr.at[slot], p_hbm.at[h, :, pl.ds(d * tok, tok), :], sems.at[slot]
        )

    heads = local // head_size
    rows_at_once = 32
    pending = {}
    span = 4 * tok
    for h in range(heads):
        cols = slice(h * head_size, (h + 1) * head_size)
        bias_row = get(6)[h : h + 1, :]
        spread = jnp.broadcast_to(bias_row, (tok, span))
        near = pltpu.roll(spread, 0, 1, stride=1, stride_axis=0)
        strip[:, tok * (blocks - 2) : tok * (blocks + 1)] = near[:, tok : 4 * tok]
        strip[:, : tok * (blocks - 2)] = jnp.broadcast_to(
            bias_row[:, :1], (tok, tok * (blocks - 2))
        )
        strip[:, tok * (blocks + 1) :] = jnp.broadcast_to(
            bias_row[:, span - 1 :], (tok, tok * (blocks - 2))
        )
        for d in range(4):
            query_block = block_of(d, 0, 0)
            strip_base = tok * (blocks - 1) - query_block * tok
            source, at = (get(0), d) if d < 3 else (get(1), 0)
            seg_col = source[at, 0, :, 2 * local : 2 * local + 1].astype(f32)
            slot = (h * 4 + d) % 2
            if slot in pending:
                pending.pop(slot).wait()
            queries = q_ref[d * tok : (d + 1) * tok, cols]
            if chunks == 1:
                s_scr[slot] = dot(queries, k_ref[:, cols], 1, 1)
                for r in range(0, tok, rows_at_once):
                    rows = slice(r, r + rows_at_once)
                    bias = strip[rows, pl.ds(pl.multiple_of(strip_base, tok), seq)]
                    scores = s_scr[slot, rows, :] + bias
                    scores = jnp.where(seg_col[rows] == segk[0:1, :], scores, masked_score)
                    top = jnp.max(scores, axis=1, keepdims=True)
                    exps = jnp.exp(scores - top)
                    total = jnp.sum(exps, axis=1, keepdims=True)
                    p_scr[slot, 0, rows, :] = (exps * (1.0 / total)).astype(bf16)
                weighted = jnp.dot(
                    p_scr[slot, 0], v_ref[:, cols], preferred_element_type=f32
                )
            else:
                def score_chunk(i, top):
                    start = pl.multiple_of(i * chunk, chunk)
                    scores = dot(queries, k_ref[pl.ds(start, chunk), cols], 1, 1)
                    base = pl.multiple_of(strip_base + start, tok)
                    scores = scores + strip[:, pl.ds(base, chunk)]
                    same = seg_col == segk[0:1, pl.ds(start, chunk)]
                    scores = jnp.where(same, scores, masked_score)
                    s_scr[0, :, pl.ds(start, chunk)] = scores
                    return jnp.maximum(top, jnp.max(scores, axis=1, keepdims=True))

                top = lax.fori_loop(
                    0, chunks, score_chunk, jnp.full((tok, 1), -3e38, f32)
                )

                def exp_chunk(i, total):
                    start = pl.multiple_of(i * chunk, chunk)
                    exps = jnp.exp(s_scr[0, :, pl.ds(start, chunk)] - top)
                    s_scr[0, :, pl.ds(start, chunk)] = exps
                    return total + jnp.sum(exps, axis=1, keepdims=True)

                total = lax.fori_loop(0, chunks, exp_chunk, jnp.zeros((tok, 1), f32))
                inverse = 1.0 / total

                def weigh_chunk(i, weighted):
                    start = pl.multiple_of(i * chunk, chunk)
                    low = (s_scr[0, :, pl.ds(start, chunk)] * inverse).astype(bf16)
                    p_scr[slot, i] = low
                    return weighted + jnp.dot(
                        low, v_ref[pl.ds(start, chunk), cols], preferred_element_type=f32
                    )

                weighted = lax.fori_loop(
                    0, chunks, weigh_chunk, jnp.zeros((tok, head_size), f32)
                )
            copy = p_copy(slot, h, d)
            copy.start()
            pending[slot] = copy
            o_ref[d * tok : (d + 1) * tok, cols] = weighted
            ctx[d][:, cols] = weighted.astype(bf16)
    for copy in pending.values():
        copy.wait()


def attention_forward(place, kv, q, bias):
    s_count, tok = kv[0].shape[1:3]
    local = q[0].shape[2]
    blocks = 8 * s_count
    seq = blocks * tok
    chunk = min(seq, 1024)
    shapes = (
        [shaped(bf16, tok, local)] * 4
        + [shaped(bf16, 4 * tok, local)]
        + [shaped(bf16, seq, local)] * 2
        + [shaped(f32, 4 * tok, local)]
        + [shaped(bf16, local // 64, seq // chunk, 4 * tok, chunk)]
    )
    return kernel_call(
        functools.partial(forward_body, blocks=blocks, chunk=chunk),
        "attention_forward",
        [place],
        [*kv, *q, bias],
        shapes,
        scratch=[
            pltpu.VMEM((8, seq), f32),
            pltpu.VMEM((tok, (2 * blocks - 1) * tok), f32),
            pltpu.VMEM((2 if seq == chunk else 1, tok, seq), f32),
            pltpu.VMEM((2, seq // chunk, tok, chunk), bf16),
            pltpu.SemaphoreType.DMA((2,)),
        ],
        in_hbm=(("out", 8),),
        mebibytes=8 if s_count == 1 else 60,
        us=10,
    )


def backward_body(
    smem, get, outs, p_scr, ds_scr, dctx_scr, strip, dq_scr, kv_scr, rows_scr, sems, *, blocks, chunk
):
    (place,) = smem
    p_hbm = get(8)
    dq = outs[0:4]
    keep_ref, send_ref, table_ref = outs[4:7]
    group, core, s_own = place[0], place[1], place[2]
    tok = 128
    head_size = 64
    seq = blocks * tok
    chunks = seq // chunk
    s_count = blocks // 8

    def p_copy(h, i, slot):
        return pltpu.make_async_copy(p_hbm.at[h, i], p_scr.at[slot], sems.at[slot])

    p_copy(0, 0, 0).start()
    for d in range(4):
        dctx_scr[d * tok : (d + 1) * tok, :] = get(d)[...]
    q_ref, k_ref, v_ref, o_ref = get(4), get(5), get(6), get(7)
    heads = q_ref.shape[1] // head_size
    rows_scr[...] = jnp.zeros_like(rows_scr)
    rows_at_once = 32
    for h in range(heads):
        cols = slice(h * head_size, (h + 1) * head_size)
        strip[...] = jnp.zeros_like(strip)
        out_grad = dctx_scr[:, cols]
        delta = jnp.sum(out_grad.astype(f32) * o_ref[:, cols], axis=1, keepdims=True)

        def run_chunk(i, h=h, cols=cols, out_grad=out_grad, delta=delta):
            start = pl.multiple_of(i * chunk, chunk)
            slot = (h * chunks + i) % 2
            following = h * chunks + i + 1

            @pl.when(following < heads * chunks)
            def _():
                p_copy(following // chunks, following % chunks, 1 - slot).start()

            p_copy(h, i, slot).wait()
            keys = k_ref[pl.ds(start, chunk), cols]
            values = v_ref[pl.ds(start, chunk), cols]
            for d in range(4):
                query_block = ((group ^ d) * s_count + s_own) * 2 + core
                base = pl.multiple_of(tok * (blocks - 1) - query_block * tok + start, tok)
                prob_grad = dot(out_grad[d * tok : (d + 1) * tok], values, 1, 1)
                for r in range(0, tok, rows_at_once):
                    rows = slice(d * tok + r, d * tok + r + rows_at_once)
                    here = prob_grad[r : r + rows_at_once] - delta[rows]
                    low = (p_scr[slot, rows, :].astype(f32) * here).astype(bf16)
                    ds_scr[rows, :] = low
                    strip[r : r + rows_at_once, pl.ds(base, chunk)] += low.astype(f32)
            scores_grad = ds_scr[...]
            part = jnp.dot(scores_grad, keys, preferred_element_type=f32)
            if chunks == 1:
                dq_scr[:, cols] = part
            else:
                dq_scr[:, cols] += part
            queries = q_ref[:, cols]
            kv_scr[0, pl.ds(start, chunk), :] = dot(scores_grad, queries, 0, 0).astype(bf16)
            kv_scr[1, pl.ds(start, chunk), :] = dot(p_scr[slot], out_grad, 0, 0).astype(bf16)

        if chunks == 1:
            run_chunk(0)
        else:
            dq_scr[:, cols] = jnp.zeros((4 * tok, head_size), f32)
            pl.loop(0, chunks)(run_chunk)

        def place_rows(e, h=h, cols=cols):
            for d in range(4):
                for k, target in ((0, keep_ref), (1, send_ref)):
                    block = ((group ^ d) * s_count + (s_own ^ e)) * 2 + (core if k == 0 else 1 - core)
                    start = pl.multiple_of(block * tok, tok)
                    width = heads * head_size
                    target[e, d, :, cols] = kv_scr[0, pl.ds(start, tok), :]
                    shifted = slice(width + h * head_size, width + (h + 1) * head_size)
                    target[e, d, :, shifted] = kv_scr[1, pl.ds(start, tok), :]

        if s_count == 1:
            place_rows(0)
        else:
            pl.loop(0, s_count)(place_rows)
        near = strip[:, tok * (blocks - 2) : tok * (blocks + 1)]
        left = jnp.zeros((1, tok), f32)
        right = jnp.zeros((1, tok), f32)
        for t in range(blocks - 2):
            left = left + jnp.sum(strip[:, t * tok : (t + 1) * tok], axis=0, keepdims=True)
            far = (blocks + 1 + t) * tok
            right = right + jnp.sum(strip[:, far : far + tok], axis=0, keepdims=True)
        rows_scr[h : h + 1, :] = jnp.concatenate([left, jnp.zeros((1, 2 * tok), f32), right], axis=1)
        spread = jnp.concatenate([jnp.zeros((tok, tok), f32), near], axis=1)
        skewed = spread[:8]
        for j in range(1, tok // 8):
            skewed = skewed + pltpu.roll(spread[8 * j : 8 * j + 8], 4 * tok - 8 * j, 1)
        row = lax.broadcasted_iota(jnp.int32, skewed.shape, 0)
        for step in (1, 2, 4):
            moved = pltpu.roll(skewed, 4 * tok - step, 1)
            skewed = jnp.where((row & step) != 0, moved, skewed)
        rows_scr[h : h + 1, :] += jnp.sum(skewed, axis=0, keepdims=True)
    for d in range(4):
        dq[d][...] = dq_scr[d * tok : (d + 1) * tok, :].astype(bf16)
    span = 4 * tok
    bucket_count = 2 * (len(cutoffs) + 1)
    buckets = bucket_row(span, bucket_count // 2)
    sums = rows_scr[...]
    lane = lax.broadcasted_iota(jnp.int32, (8, tok), 1)
    table = jnp.zeros((8, tok), f32)
    for b in range(bucket_count):
        picked = jnp.where(buckets == b, sums, 0.0)
        table = jnp.where(lane == b, jnp.sum(picked, axis=1, keepdims=True), table)
    table_ref[...] = table


def attention_backward(place, dctx, q, k, v, o, p):
    tok, local = dctx[0].shape
    seq = k.shape[0]
    blocks = seq // tok
    s_count = blocks // 8
    chunk = p.shape[3]
    shapes = (
        [shaped(bf16, tok, local)] * 4
        + [shaped(bf16, s_count, 4, tok, 2 * local)] * 2
        + [shaped(f32, 8, tok)]
    )
    return kernel_call(
        functools.partial(backward_body, blocks=blocks, chunk=chunk),
        "attention_backward",
        [place],
        [*dctx, q, k, v, o, p],
        shapes,
        scratch=[
            pltpu.VMEM((2, 4 * tok, chunk), bf16),
            pltpu.VMEM((4 * tok, chunk), bf16),
            pltpu.VMEM((4 * tok, local), bf16),
            pltpu.VMEM((tok, (2 * blocks - 1) * tok), f32),
            pltpu.VMEM((4 * tok, local), f32),
            pltpu.VMEM((2, seq, 64), bf16),
            pltpu.VMEM((8, 4 * tok), f32),
            pltpu.SemaphoreType.DMA((2,)),
        ],
        in_hbm=(8,),
        staged=tuple(("out", i) for i in range(6)) if s_count == 1 else (),
        mebibytes=13 if s_count == 1 else 60,
        us=0.01,
    )


def gated(gate, up):
    root = 0.7978845608028654
    square = gate * gate
    bend = jnp.tanh(root * (gate + 0.044715 * (gate * square)))
    act = 0.5 * gate * (1.0 + bend)
    slope = 0.5 * (1.0 + bend) + 0.5 * gate * (1.0 - bend * bend) * (
        root * (1.0 + 3.0 * 0.044715 * square)
    )
    return act, up * slope


def ffn_forward_body(smem, get, outs):
    (place,) = smem
    middle_ref, normed_ref, hidden_ref, act_ref, slope_ref = outs
    count = 4
    w_out, w_gate, w_up = get(6), get(7), get(8)
    group = place[0]
    tok, width = middle_ref.shape
    local = width // groups
    total = get(4)[...].astype(f32)
    for d in range(4):
        start = pl.multiple_of((group ^ d) * local, local)
        total = total + dot(get(d)[...], w_out[pl.ds(start, local), :], 1, 0)
    middle_ref[...] = total
    normed = (total * rms_scale(total) * get(5)[...]).astype(bf16)
    normed_ref[...] = normed
    step = w_gate.shape[1] // count
    for i in range(count):
        cols = slice(i * step, (i + 1) * step)
        up = dot(normed, w_up[:, cols], 1, 0)
        act, slope = gated(dot(normed, w_gate[:, cols], 1, 0), up)
        act_ref[:, cols] = act
        slope_ref[:, cols] = slope
        hidden_ref[:, cols] = (act * up).astype(bf16)


def ffn_forward(place, ctx, tokens, gain, w_out, w_gate, w_up):
    tok, width = tokens.shape
    ff = w_gate.shape[1]
    return kernel_call(
        ffn_forward_body,
        "ffn_forward",
        [place],
        [*ctx, tokens, gain, w_out, w_gate, w_up],
        [
            shaped(f32, tok, width),
            shaped(bf16, tok, width),
            shaped(bf16, tok, ff),
            shaped(f32, tok, ff),
            shaped(f32, tok, ff),
        ],
        staged=(4,),
        us=14,
    )


def ffn_backward_body(smem, get, outs, attn_scr):
    (place,) = smem
    out_ref, grad_ref, gain_grad_ref = outs[0:3]
    dctx = outs[3:7]
    w_down, w_gate, w_up, w_out = get(6), get(7), get(8), get(9)
    count = 4
    group = place[0]
    tok, width = grad_ref.shape
    ff = w_gate.shape[1]
    local = width // groups
    cot = get(0)[...]
    step = ff // count
    act_ref, slope_ref = get(3), get(4)
    normed_grad = jnp.zeros((tok, width), f32)
    for i in range(count):
        cols = slice(i * step, (i + 1) * step)
        hidden_grad = dot(cot, w_down[cols, :], 1, 1)
        gate = (hidden_grad * slope_ref[:, cols]).astype(bf16)
        up = (hidden_grad * act_ref[:, cols]).astype(bf16)
        normed_grad = normed_grad + dot(gate, w_gate[:, cols], 1, 1) + dot(up, w_up[:, cols], 1, 1)
    middle = get(1)[...]
    scale = rms_scale(middle)
    unit = middle * scale
    scaled = normed_grad * get(5)[...]
    gain_grad_ref[...] = jnp.sum(normed_grad * unit, axis=0, keepdims=True)
    middle_grad = cot.astype(f32) + scale * (
        scaled - unit * jnp.mean(unit * scaled, axis=1, keepdims=True)
    )
    grad_ref[...] = middle_grad
    attn = middle_grad.astype(bf16)
    attn_scr[...] = attn
    for d in range(4):
        start = pl.multiple_of((group ^ d) * local, local)
        dctx[d][...] = dot(attn, w_out[pl.ds(start, local), :], 1, 1).astype(bf16)
    for ref, which in ((outs[7], place[4]), (outs[8], 1 - place[4])):
        for d in range(4):
            ref[:, d * local : (d + 1) * local] = get(10 + d)[...]
        start = pl.multiple_of(which * (width // 2), width // 2)
        ref[:, width:] = attn_scr[:, pl.ds(start, width // 2)]
    out_ref[...] = (middle + dot(get(2)[...], w_down[...], 1, 0)).astype(bf16)


def ffn_backward(place, cot, middle, hidden, act, slope, gain, ctx, w_down, w_gate, w_up, w_out):
    tok, width = cot.shape
    local = width // groups
    return kernel_call(
        ffn_backward_body,
        "ffn_backward",
        [place],
        [cot, middle, hidden, act, slope, gain, w_down, w_gate, w_up, w_out, *ctx],
        [shaped(bf16, tok, width), shaped(f32, tok, width), shaped(f32, 1, width)]
        + [shaped(bf16, tok, local)] * 4
        + [shaped(bf16, tok, width + width // 2)] * 2,
        scratch=[pltpu.VMEM((tok, width), bf16)],
        mebibytes=6,
        us=6,
    )


def ffn_grad_body(
    smem, get, outs, normed_scr, cot_scr, hidden_scr, gate_scr, up_scr, both_scr, down_scr, *, s_count
):
    (place,) = smem
    kept_ref, sent_ref = outs
    group, core, far = place[0], place[1], place[4] == 1
    rows, eighth = hidden_scr.shape
    tok = rows // 8
    width = normed_scr.shape[1]
    local = width // groups
    for i in range(8):
        normed_scr[i * tok : (i + 1) * tok, :] = get(i)[...]
        cot_scr[i * tok : (i + 1) * tok, :] = get(8 + i)[...]
    start = ((group % 2) * 2 + core) * 2 * eighth + (group // 2) * eighth
    part = pl.ds(pl.multiple_of(start, eighth), eighth)
    w_gate, w_up, w_down = get(16)[:, part], get(17)[:, part], get(18)[part, :]
    half = rows // 2
    for i in range(2):
        span = slice(i * half, (i + 1) * half)
        up = dot(normed_scr[span, :], w_up, 1, 0)
        act, slope = gated(dot(normed_scr[span, :], w_gate, 1, 0), up)
        hidden_scr[span, :] = (act * up).astype(bf16)
        hidden_grad = dot(cot_scr[span, :], w_down, 1, 1)
        gate_scr[span, :] = (hidden_grad * slope).astype(bf16)
        up_scr[span, :] = (hidden_grad * act).astype(bf16)
    both_scr[:, :eighth] = dot(normed_scr[...], gate_scr[...], 0, 0)
    both_scr[:, eighth:] = dot(normed_scr[...], up_scr[...], 0, 0)
    down_scr[...] = dot(hidden_scr[...], cot_scr[...], 0, 0)
    unit = kept_ref.shape[1]
    block = 3 * unit // 2

    def pieces(x, s, y):
        found = []
        for k in range(3):
            parts = []
            for j in range(2):
                at = (((x + 2 * j) * s_count + s) * 2 + y) * block
                low, high = max(k * unit - j * block, 0), min((k + 1) * unit - j * block, block)
                if low < high:
                    parts.append(both_scr[at + low : at + high, :])
            found.append(parts[0] if len(parts) == 1 else jnp.concatenate(parts, axis=0))
        for k in range(4):
            at = (s * 4 + k) * unit
            cols = slice((x * 2 + y) * local, (x * 2 + y + 1) * local)
            found.append(down_scr[at : at + unit, cols])
        return found

    for s in range(s_count):
        for y in range(2):
            lane = 0
            for near, other in zip(pieces(0, s, y), pieces(1, s, y)):
                cols = slice(lane, lane + near.shape[1])
                kept_ref[s * 2 + y, :, cols] = jnp.where(far, other, near)
                sent_ref[s * 2 + y, :, cols] = jnp.where(far, near, other).astype(bf16)
                lane += near.shape[1]


def ffn_grad(place, normed, cot, w_gate, w_up, w_down, s_count):
    tok, width = normed[0].shape
    ff = w_gate.shape[1]
    eighth = ff // 8
    unit = eighth // (4 * s_count)
    shape = (2 * s_count, unit, 3 * 2 * eighth + 4 * width // groups)
    return kernel_call(
        functools.partial(ffn_grad_body, s_count=s_count),
        "ffn_grad",
        [place],
        [*normed, *cot, w_gate, w_up, w_down],
        [shaped(f32, *shape), shaped(bf16, *shape)],
        scratch=[
            pltpu.VMEM((8 * tok, width), bf16),
            pltpu.VMEM((8 * tok, width), bf16),
            pltpu.VMEM((8 * tok, eighth), bf16),
            pltpu.VMEM((8 * tok, eighth), bf16),
            pltpu.VMEM((8 * tok, eighth), bf16),
            pltpu.VMEM((width, 2 * eighth), f32),
            pltpu.VMEM((eighth, width), f32),
        ],
        mebibytes=16,
        us=0.01,
    )


def out_grad_body(smem, get, outs, ctx_scr, attn_scr, out_scr):
    (place,) = smem
    kept_ref, sent_ref = outs
    group, core, odd = place[0], place[1], place[3] == 1
    tok = ctx_scr.shape[0] // 4
    width = ctx_scr.shape[1]
    local = width // groups
    for i in range(4):
        rows = slice(i * tok, (i + 1) * tok)
        ctx_scr[rows, :] = get(i)[:, :width]
        both = get(i)[:, width:]
        attn_scr[rows, :] = jnp.where(core == 0, both[:, :local], both[:, local:])
    turned = dot(ctx_scr[...], attn_scr[...], 0, 0)
    for d in range(4):
        start = pl.multiple_of((group ^ d) * local, local)
        out_scr[pl.ds(start, local), :] = turned[d * local : (d + 1) * local]
    pieces, block, unused = kept_ref.shape
    for i in range(pieces):
        even = out_scr[2 * i * block : (2 * i + 1) * block, :]
        other = out_scr[(2 * i + 1) * block : (2 * i + 2) * block, :]
        kept_ref[i] = jnp.where(odd, other, even)
        sent_ref[i * block : (i + 1) * block, :] = jnp.where(odd, even, other).astype(bf16)


def out_weight_grad(place, parts, wide):
    tok, span = parts[0].shape
    width = span * 2 // 3
    local = width // groups
    shape = (wide // 2, width // wide, local)
    return kernel_call(
        out_grad_body,
        "out_grad",
        [place],
        parts,
        [shaped(f32, *shape), shaped(bf16, width // 2, local)],
        scratch=[
            pltpu.VMEM((4 * tok, width), bf16),
            pltpu.VMEM((4 * tok, local), bf16),
            pltpu.VMEM((width, local), f32),
        ],
        mebibytes=5,
        us=0.01,
    )


def out_sum_body(smem, get, outs, *, bit, riding):
    (place,) = smem
    kept, received = get(0), get(1)
    remaining, block, unused = kept.shape
    totals = [
        kept[i] + received[i * block : (i + 1) * block, :].astype(f32) for i in range(remaining)
    ]
    if riding:
        small = get(2)[...]
        if "in" in riding:
            small = attached(received, remaining * block, small)
            outs[-1][...] = small
    if remaining == 1:
        outs[0][...] = totals[0]
        return
    odd = ((place[5] >> bit) & 1) == 1
    for i in range(remaining // 2):
        outs[0][i] = jnp.where(odd, totals[2 * i + 1], totals[2 * i])
        theirs = jnp.where(odd, totals[2 * i], totals[2 * i + 1])
        outs[1][i * block : (i + 1) * block, :] = theirs.astype(bf16)
    if riding:
        filled = remaining // 2 * block
        rest = outs[1].shape[0] - filled
        outs[1][filled:, :] = jnp.zeros((rest, outs[1].shape[1]), bf16)
        attach_rows(outs[1], filled, small)


def out_sum(layout, place, kept, sent, bit, small=None, riding=()):
    remaining, block, local = kept.shape
    extra = 2 * room(small.shape[0]) if riding else 0
    if remaining == 1:
        outputs = [shaped(f32, block, local)]
    else:
        outputs = [
            shaped(f32, remaining // 2, block, local),
            shaped(bf16, remaining // 2 * block + extra, local),
        ]
    if "in" in riding:
        outputs.append(shaped(f32, *small.shape))
    return kernel_call(
        functools.partial(out_sum_body, bit=bit + 1, riding=riding),
        "out_sum",
        [place],
        [kept, layout.wide_bit(sent, bit)] + ([small] if riding else []),
        outputs,
        us=0.01,
    )


def ffn_sum_body(smem, get, outs):
    (place,) = smem
    odd = place[3] == 1
    for i in range(outs[0].shape[0]):
        even = get(0)[2 * i] + get(1)[2 * i].astype(f32)
        other = get(0)[2 * i + 1] + get(1)[2 * i + 1].astype(f32)
        outs[0][i] = jnp.where(odd, other, even)
        outs[1][i] = jnp.where(odd, even, other).astype(bf16)


def ffn_sum(place, kept, received):
    pieces, unit, span = kept.shape
    return kernel_call(
        ffn_sum_body,
        "ffn_sum",
        [place],
        [kept, received],
        [shaped(f32, pieces // 2, unit, span), shaped(bf16, pieces // 2, unit, span)],
        us=0.01,
    )


def ffn_last_body(smem, get, outs, both_scr):
    (place,) = smem
    total = get(0)[0].astype(f32) + get(1)[0].astype(f32)
    unit = total.shape[0]
    block, span = outs[0].shape
    local = outs[2].shape[1]
    for k in range(3):
        both_scr[k * unit : (k + 1) * unit, :] = total[:, k * span : (k + 1) * span]
    for k in range(4):
        at = 3 * span + k * local
        outs[2][k * unit : (k + 1) * unit, :] = total[:, at : at + local].astype(bf16)
    low = place[0] // 2 == 0
    first, second = both_scr[:block, :], both_scr[block:, :]
    outs[0][...] = jnp.where(low, first, second).astype(bf16)
    outs[1][...] = jnp.where(low, second, first).astype(bf16)


def ffn_last(place, kept, received, local):
    unused, unit, span = kept.shape
    both = (span - 4 * local) // 3
    return kernel_call(
        ffn_last_body,
        "ffn_last",
        [place],
        [kept, received],
        [shaped(bf16, 3 * unit // 2, both)] * 2 + [shaped(bf16, 4 * unit, local)],
        scratch=[pltpu.VMEM((3 * unit, both), f32)],
        us=0.01,
    )


def ffn_owned_body(smem, get, outs):
    (place,) = smem
    low = place[0] // 2 == 0
    eighth = get(0).shape[1] // 2
    own, other = get(0)[...].astype(f32), get(1)[...].astype(f32)
    first, second = jnp.where(low, own, other), jnp.where(low, other, own)
    for i in range(2):
        cols = slice(i * eighth, (i + 1) * eighth)
        outs[i][:, :eighth] = first[:, cols]
        outs[i][:, eighth:] = second[:, cols]
    outs[2][...] = jnp.transpose(get(2)[...].astype(f32))


def ffn_owned(place, own, other, down):
    return kernel_call(
        ffn_owned_body,
        "ffn_owned",
        [place],
        [own, other, down],
        [shaped(f32, *own.shape)] * 2 + [shaped(f32, *down.shape[::-1])],
        us=1,
    )


def collect_body(smem, get, outs):
    local = outs[0].shape[2] // 3
    for d in range(4):
        outs[d // 2][d % 2, :, :local] = get(d)[...]
    for d in range(4):
        total = get(4)[d].astype(f32) + get(5)[d].astype(f32)
        outs[d // 2][d % 2, :, local:] = total.astype(bf16)


def collect(dq, kept, received):
    tok, local = dq[0].shape
    return kernel_call(
        collect_body,
        "collect",
        [],
        [*dq, kept, received],
        [shaped(bf16, 2, tok, 3 * local)] * 2,
        staged=tuple(range(6)),
        us=0.01,
    )


def exact(small):
    high = small.astype(bf16)
    return high, (small - high.astype(f32)).astype(bf16)


def attach(ref, rows, small):
    high, low = exact(small)
    ref[rows : rows + small.shape[0], : small.shape[1]] = high
    ref[rows : rows + small.shape[0], small.shape[1] : 2 * small.shape[1]] = low


def attach_rows(ref, rows, small):
    high, low = exact(small)
    count, lanes = small.shape
    ref[rows : rows + count, :lanes] = high
    below = rows + room(count)
    ref[below : below + count, :lanes] = low


def attached(ref, rows, small):
    count, lanes = small.shape
    high, low = exact(small)
    theirs = ref[rows : rows + count, :lanes].astype(f32)
    if ref.shape[1] >= 2 * lanes:
        theirs = theirs + ref[rows : rows + count, lanes : 2 * lanes].astype(f32)
    else:
        below = rows + room(count)
        theirs = theirs + ref[below : below + count, :lanes].astype(f32)
    return high.astype(f32) + low.astype(f32) + theirs


def qkv_grad_body(smem, get, outs, grad_scr, total_scr):
    (place,) = smem
    kept_ref, sent_ref, small_ref = outs
    group, core = place[0], place[1]
    width, span = total_scr.shape
    local = span // 3
    tok = grad_scr.shape[0] // 4
    for d in range(4):
        grad_scr[d * tok : (d + 1) * tok, :] = get(d // 2)[d % 2]
    total_scr[...] = dot(get(2)[...], grad_scr[: 3 * tok, :], 0, 0)
    total_scr[...] += dot(get(9)[...], grad_scr[3 * tok :, :], 0, 0)
    quarter = width // 4
    for i in range(2):
        start = pl.multiple_of((2 * i + core) * quarter, quarter)
        kept_ref[i] = total_scr[pl.ds(start, quarter), :]
        start = pl.multiple_of((2 * i + 1 - core) * quarter, quarter)
        sent_ref[i * quarter : (i + 1) * quarter, :] = total_scr[pl.ds(start, quarter), :].astype(bf16)
    window, late = group_window(group, local)
    ones = jnp.ones((8, local), bf16)
    gain_grad = jnp.zeros((8, width), f32)
    for i in range(3):
        both = get(6 + i)[:, pl.ds(window, -(-local // 128) * 128)]
        weight = jnp.where(late, both[:, both.shape[1] - local :], both[:, :local])
        product = total_scr[:, i * local : (i + 1) * local] * weight.astype(f32)
        high, rest = exact(product)
        gain_grad = gain_grad + dot(ones, high, 1, 1) + dot(ones, rest, 1, 1)
    gain_grad = gain_grad[0:1] / get(3)[...]
    ffn_gain = get(4)[...]
    lanes = 128
    rows = width // lanes
    for i in range(rows):
        small_ref[i : i + 1, :] = gain_grad[:, i * lanes : (i + 1) * lanes]
        small_ref[rows + i : rows + i + 1, :] = ffn_gain[:, i * lanes : (i + 1) * lanes]
    heads = (small_ref.shape[0] - 2 * rows) // groups
    table = get(5)[:heads, :]
    for i in range(groups):
        at = 2 * rows + i * heads
        small_ref[at : at + heads, :] = jnp.where(group == i, table, 0.0)
    sent_ref[2 * quarter :, :] = jnp.zeros((sent_ref.shape[0] - 2 * quarter, span), bf16)
    attach(sent_ref, 2 * quarter, small_ref[...])


def room(count):
    return -(-count // 16) * 16


def qkv_grad(
    place,
    grads,
    normed_first,
    normed_last,
    gain,
    gain_grad,
    table,
    head_count,
    w_query,
    w_key,
    w_value,
):
    rows, width = 4 * grads[0].shape[1], normed_first.shape[1]
    local = width // groups
    count = 2 * width // 128 + head_count
    return kernel_call(
        qkv_grad_body,
        "qkv_grad",
        [place],
        [
            *grads,
            normed_first,
            gain,
            gain_grad,
            table,
            w_query,
            w_key,
            w_value,
            normed_last,
        ],
        [
            shaped(f32, 2, width // 4, 3 * local),
            shaped(bf16, width // 2 + room(count), 3 * local),
            shaped(f32, count, 128),
        ],
        scratch=[
            pltpu.VMEM((rows, 3 * local), bf16),
            pltpu.VMEM((width, 3 * local), f32),
        ],
        mebibytes=10,
        us=0.01,
    )


def qkv_sum_body(smem, get, outs, *, axis):
    (place,) = smem
    kept, small, received = get(0), get(1), get(2)
    parts, rows, span = kept.shape
    totals = [
        kept[i] + received[i * rows : (i + 1) * rows, :].astype(f32) for i in range(parts)
    ]
    summed = attached(received, parts * rows, small[...])
    if axis == "y":
        outs[-1][...] = summed
        for i in range(parts):
            outs[0][i] = totals[i].astype(outs[0].dtype)
        return
    kept_ref, sent_ref, small_ref = outs
    small_ref[...] = summed
    if axis == "core":
        far = place[4] == 1
        mine, theirs = jnp.where(far, totals[1], totals[0]), jnp.where(far, totals[0], totals[1])
        blocks, block = kept_ref.shape[0], kept_ref.shape[1]
        for i in range(blocks):
            kept_ref[i] = mine[i * block : (i + 1) * block]
        sent_ref[:rows, :] = theirs.astype(bf16)
    else:
        odd = place[3] == 1
        for i in range(parts // 2):
            kept_ref[i] = jnp.where(odd, totals[2 * i + 1], totals[2 * i])
            theirs = jnp.where(odd, totals[2 * i], totals[2 * i + 1])
            sent_ref[i * rows : (i + 1) * rows, :] = theirs.astype(bf16)
    filled = sent_ref.shape[0] - room(small.shape[0])
    sent_ref[filled:, :] = jnp.zeros((room(small.shape[0]), span), bf16)
    attach(sent_ref, filled, summed)


def qkv_sum(place, kept, small, received, axis, s_count, wide):
    parts, rows, span = kept.shape
    count = small.shape[0]
    if axis == "core":
        shape, sent = (2 * s_count, rows // (2 * s_count), span), rows
    else:
        shape, sent = (parts // 2, rows, span), parts // 2 * rows
    if axis == "y":
        outputs = [shaped(bf16 if s_count == 1 else f32, *kept.shape)]
    else:
        outputs = [shaped(f32, *shape), shaped(bf16, sent + room(count), span)]
    return kernel_call(
        functools.partial(qkv_sum_body, axis=axis),
        f"qkv_sum_{axis}",
        [place],
        [kept, small, received],
        outputs + [shaped(f32, count, 128)],
        us=0.01,
    )


def input_grad_body(smem, get, outs, all_scr):
    (place,) = smem
    group = place[0]
    weights = [get(6 + i) for i in range(3)]
    local = get(0).shape[2] // 3
    window = -(-local // 128) * 128
    tok = get(0).shape[1]
    spare = jnp.zeros((tok, window - local), bf16)
    all_scr[...] = jnp.zeros_like(all_scr)
    for d in range(4):
        start, late = group_window(group ^ d, local)
        grads = get((0, 2, 1, 2)[d])[d // 3]
        for i in range(3):
            part = grads[:, i * local : (i + 1) * local]
            part = jnp.where(
                late,
                jnp.concatenate([spare, part], axis=1),
                jnp.concatenate([part, spare], axis=1),
            )
            all_scr[i, :, pl.ds(start, window)] += part
    normed_grad = dot(all_scr[0], weights[0][...], 1, 1)
    for i in range(1, 3):
        normed_grad = normed_grad + dot(all_scr[i], weights[i][...], 1, 1)
    values = get(3)[...].astype(f32)
    scale = rms_scale(values)
    unit = values * scale
    scaled = normed_grad * get(4)[...]
    outs[0][...] = get(5)[...] + scale * (
        scaled - unit * jnp.mean(unit * scaled, axis=1, keepdims=True)
    )


def final_input_grad(place, grads, tokens, gain, middle_grad, w_query, w_key, w_value):
    return kernel_call(
        input_grad_body,
        "input_grad",
        [place],
        [*grads, tokens, gain, middle_grad, w_query, w_key, w_value],
        [shaped(f32, *tokens.shape)],
        scratch=[pltpu.VMEM((3, *tokens.shape), bf16)],
        staged=(0, 1, 2, 3, 5),
        mebibytes=6,
        us=0.01,
    )[0]


def stacked_body(smem, get, outs):
    rows = get(0).shape[0]
    outs[0][:rows, :] = get(0)[...]
    outs[0][rows:, :] = get(1)[...]


def stacked(first, second):
    rows, width = first.shape
    return kernel_call(
        stacked_body, "stacked", [], [first, second], [shaped(bf16, 2 * rows, width)], us=0.01
    )[0]


def forwarded_body(smem, get, outs):
    outs[0][0] = get(0)[1]
    outs[0][1] = get(1)[1]


def forwarded(near, far):
    return kernel_call(
        forwarded_body, "forwarded", [], [near, far], [shaped(bf16, *near.shape)], us=0.01
    )[0]


def after(values, done):
    return lax.optimization_barrier((values, done))[0]


def halved(block, axis, keep):
    return (
        lax.dynamic_index_in_dim(block, keep, axis, keepdims=False),
        lax.dynamic_index_in_dim(block, 1 - keep, axis, keepdims=False),
    )


def on_device(
    inputs,
    segment_ids,
    gain_attn,
    w_query,
    w_key,
    w_value,
    w_out,
    gain_ffn,
    w_gate,
    w_up,
    w_down,
    bias_table,
    cotangent,
):
    layout = Layout(lax.axis_size("narrow"), lax.axis_size("wide"))
    s_count = layout.s_count
    tokens = inputs[0]
    out_grad = cotangent[0]
    tok, width = tokens.shape
    local = width // groups
    ff = w_gate.shape[1]
    bucket_count, head_count = bias_table.shape
    narrow = lax.axis_index("narrow")
    wide = lax.axis_index("wide")
    core = narrow % 2
    across = narrow // 2
    group = wide // (2 * s_count)
    s_own = (wide // 2) % s_count
    y_own = wide % 2
    place = jnp.stack([group, core, s_own, y_own, across, wide]).astype(jnp.int32)
    gain_attn = gain_attn[None]
    gain_ffn = gain_ffn[None]

    packet = packed(tokens, segment_ids)
    own = [layout.turned(packet, d)[None] for d in range(3)]
    own.append(layout.wide_bit(own[2], layout.wide.bit_length() - 3))
    for d in range(4):
        size = 1
        while size < s_count:
            own[d] = jnp.concatenate([own[d], layout.wide_bit(own[d], size.bit_length())], axis=0)
            size *= 2
    bias = bias_rows(place, bias_table, 4 * tok)
    kv_first, q_first, normed_first = project(place, own[:3], gain_attn, w_query, w_key, w_value)
    kv_first = after(kv_first, bias)
    cot = after(out_grad, kv_first)
    cot = [out_grad, layout.near_group(cot), layout.far_group(cot)]
    kv_last, q_last, normed_last = project(place, own[3:], gain_attn, w_query, w_key, w_value)
    kv = [kv_first, kv_last, layout.core(kv_first), layout.core(kv_last)]
    outs = attention_forward(place, kv, [q_first, q_last], bias)
    ctx_parts = outs[:4]
    q_own, k_all, v_all, o_own, probs = outs[4:]
    ctx_parts = after(ctx_parts, cot)
    ctx = [layout.turned(ctx_parts[d], d) for d in range(4)]
    cot.append(layout.near_group(after(cot[2], ctx)))

    middle, normed_ffn, hidden, act, slope = ffn_forward(
        place, ctx, tokens, gain_ffn, w_out, w_gate, w_up
    )
    bits = layout.wide.bit_length() - 1
    normed_far = layout.far_group(normed_ffn)
    back = ffn_backward(
        place, out_grad, middle, hidden, act, slope, gain_ffn, ctx, w_down, w_gate, w_up, w_out
    )
    output, middle_grad, grad_gain_ffn = back[0:3]
    dctx = [layout.turned(back[3 + d], d) for d in range(4)]
    mine, far = back[7:9]
    far = layout.across(after(far, dctx[0]))
    normed_near, normed_far = after((normed_ffn, normed_far), dctx[1])
    normed = [
        normed_ffn,
        layout.near_group(normed_near),
        normed_far,
        layout.near_group(normed_far),
    ]

    dctx = after(dctx, cot[3])
    back = attention_backward(place, dctx, q_own, k_all, v_all, o_own, probs)
    dq, kept, sent, table_rows = back[:4], back[4], back[5], back[6]

    received = layout.core(sent)
    size = s_count
    while size > 1:
        size //= 2
        total = kept.astype(f32) + received.astype(f32)
        kept = total[:size]
        received = layout.wide_bit(total[size:].astype(bf16), size.bit_length())
    normed, cot, mine, far = after((normed, cot, mine, far), sent)
    normed = normed + [layout.core(block) for block in normed]
    cot = cot + [layout.core(block) for block in cot]
    out_parts = [mine, layout.core(mine), far, layout.core(far)]
    low_grads = collect(dq, kept[0], received[0])
    ffn_kept, ffn_sent = ffn_grad(
        place, after(normed, low_grads), cot, w_gate, w_up, w_down, s_count
    )
    normed_first = after(normed_first, ffn_sent)
    qkv_kept, qkv_sent, small = qkv_grad(
        place,
        low_grads,
        normed_first,
        normed_last,
        gain_attn,
        grad_gain_ffn,
        table_rows,
        head_count,
        w_query,
        w_key,
        w_value,
    )
    out = out_weight_grad(place, after(out_parts, qkv_sent), layout.wide)

    returned = [layout.turned(low_grads[0], 0), layout.turned(low_grads[1], 2)]
    qkv_kept = after(qkv_kept, out)
    step = qkv_sum(place, qkv_kept, small, layout.core(qkv_sent), "core", s_count, layout.wide)
    ffn_kept, ffn_sent = ffn_sum(place, after(ffn_kept, step), layout.across(ffn_sent))
    out_kept, out_sent = after(out, ffn_sent)
    step = qkv_sum(
        place, after(step[0], ffn_kept), step[2], layout.across(step[1]), "x", s_count, layout.wide
    )
    received = layout.wide_bit(ffn_sent, 0)
    size = s_count
    bit = 1
    while size > 1:
        size //= 2
        total = (ffn_kept + received.astype(f32)).reshape(size, 2, *ffn_kept.shape[1:])
        ffn_kept, ffn_sent = halved(total, 1, (s_own >> (bit - 1)) & 1)
        received = layout.wide_bit(ffn_sent.astype(bf16), bit)
        bit += 1
    onward = forwarded(returned[0], after(returned[1], step))
    returned.append(layout.wide_bit(onward, bits - 2))
    ffn_parts = ffn_last(place, after(ffn_kept, onward), received, local)
    part, small = qkv_sum(
        place,
        after(step[0], ffn_parts),
        step[2],
        layout.wide_bit(step[1], 0),
        "y",
        s_count,
        layout.wide,
    )
    rows = width // layout.wide
    size = s_count
    bit = 1
    while size > 1:
        size //= 2
        part = part.reshape(size, 2, rows, 3 * local)
        kept, sent = halved(part, 1, (s_own >> (bit - 1)) & 1)
        part = kept + layout.wide_bit(sent.astype(bf16), bit).astype(f32)
        small = small + layout.wide_bit(small, bit)
        bit += 1
    part = part.reshape(rows, 3 * local).astype(bf16)

    for bit in range(bits - 1):
        riding = ("in",) * (bit > bits - 3) + ("out",) * (bit > bits - 4)
        first = small if riding else part
        if bit == bits - 2:
            middle_grad = after(middle_grad, out_sent)
            input_grad = final_input_grad(
                place, returned, tokens, gain_attn, middle_grad, w_query, w_key, w_value
            )
            first = input_grad
        outs = out_sum(layout, place, after(out_kept, first), out_sent, bit, small, riding)
        out_kept, out_sent = outs[:2]
        if "in" in riding:
            small = outs[2]

    def half_owner(flip):
        return lambda x, c, g, s, y: (g % 2, c, x + 2 * (g // 2 ^ flip), s, y)

    def down_owner(x, c, g, s, y):
        at = g // 2 * s_count + s
        return (x, y, g % 2 * 2 + c, at // 2, at % 2)

    final_gate, final_up, final_down = ffn_owned(
        place,
        layout.send(ffn_parts[0], half_owner(0)),
        layout.send(ffn_parts[1], half_owner(1)),
        layout.send(ffn_parts[2], down_owner),
    )
    part = layout.send(part, lambda x, c, g, s, y: (g // 2, g % 2, x * 2 + c, s, y)).astype(f32)
    final_query, final_key, final_value = (
        part[:, :local],
        part[:, local : 2 * local],
        part[:, 2 * local :],
    )

    out_kept = after(out_kept, final_gate)
    final_out, small = out_sum(
        layout, place, out_kept, out_sent, bits - 1, small, ("in",)
    )
    gain_rows = width // 128
    sum_gain_attn = small[:gain_rows].reshape(width)
    sum_gain_ffn = small[gain_rows : 2 * gain_rows].reshape(width)
    sum_table = small[2 * gain_rows :, :bucket_count].T
    return (
        output[None],
        input_grad[None],
        sum_gain_attn,
        final_query,
        final_key,
        final_value,
        final_out,
        sum_gain_ffn,
        final_gate,
        final_up,
        final_down.T,
        sum_table,
    )


def solution(mesh):
    tokens = P("narrow", "wide", None)
    share = P("wide", "narrow")
    return jax.shard_map(
        on_device,
        mesh=mesh,
        in_specs=(tokens, P("narrow", "wide")) + (P(),) * 10 + (tokens,),
        out_specs=(
            tokens,
            tokens,
            P(),
            share,
            share,
            share,
            share,
            P(),
            share,
            share,
            share,
            P(),
        ),
        check_vma=False,
    )
```

```python
import functools

import jax
import jax.numpy as jnp
import numpy as np
from jax import lax
from jax.experimental import pallas as pl
from jax.experimental.pallas import tpu as pltpu
from jax.sharding import PartitionSpec as P

cutoffs = (1, 2, 3, 4, 5, 6, 7, 8, 12, 16, 23, 32, 46, 64, 91)
epsilon = 1e-06
masked_score = -1000000000.0
highest = lax.Precision.HIGHEST
axes = ("narrow", "wide")
groups = 4
bf16 = jnp.bfloat16
f32 = jnp.float32


def dot(left, right, left_dim, right_dim):
    return lax.dot_general(
        left, right, (((left_dim,), (right_dim,)), ((), ())), preferred_element_type=f32
    )


class Layout:
    def __init__(self, narrow, wide):
        self.narrow = narrow
        self.wide = wide
        self.s_count = wide // (groups * 2)

    def index(self, x, c, g, s, y):
        return (x * 2 + c) * self.wide + (g * self.s_count + s) * 2 + y

    def send(self, block, target):
        route = []
        for x in range(self.narrow // 2):
            for c in range(2):
                for g in range(groups):
                    for s in range(self.s_count):
                        for y in range(2):
                            route.append(
                                (self.index(x, c, g, s, y), self.index(*target(x, c, g, s, y)))
                            )
        return lax.ppermute(block, axes, route)

    def turned(self, block, d):
        return self.send(block, lambda x, c, g, s, y: (x, y, g ^ d, s, c))

    def core(self, block):
        return self.send(block, lambda x, c, g, s, y: (x, 1 - c, g, s, y))

    def across(self, block):
        return self.send(block, lambda x, c, g, s, y: (x ^ 1, c, g, s, y))

    def far_group(self, block):
        return self.wide_mask(block, self.wide // 2)

    def near_group(self, block):
        return self.wide_mask(block, self.wide // 4)

    def wide_bit(self, block, bit):
        return self.wide_mask(block, 1 << bit)

    def wide_mask(self, block, mask):
        def target(x, c, g, s, y):
            w = ((g * self.s_count + s) * 2 + y) ^ mask
            return (x, c, w // (2 * self.s_count), (w // 2) % self.s_count, w % 2)

        return self.send(block, target)


def rms_scale(values):
    return lax.rsqrt(jnp.mean(values * values, axis=-1, keepdims=True) + epsilon)


def bucket_row(span, half_count):
    offset = lax.broadcasted_iota(jnp.int32, (1, span), 1) - span // 2
    distance = jnp.abs(offset)
    bucket = jnp.where(offset > 0, half_count, 0)
    for cutoff in cutoffs:
        bucket = bucket + jnp.where(distance >= cutoff, 1, 0)
    return bucket


def cost(microseconds):
    return pl.CostEstimate(
        flops=int(microseconds * 1.15e9), bytes_accessed=1024, transcendentals=0
    )


def kernel_call(
    body, name, smem, inputs, outputs, scratch=(), in_hbm=(), staged=(), mebibytes=4, us=3
):
    n_smem, n_in, n_out = len(smem), len(inputs), len(outputs)
    ins = [i for i in staged if not isinstance(i, tuple)]
    leaving = [i[1] for i in staged if isinstance(i, tuple)]

    def kernel(*refs):
        given = refs[n_smem : n_smem + n_in]
        results = refs[n_smem + n_in : n_smem + n_in + n_out]
        rest = refs[n_smem + n_in + n_out :]
        buffers = dict(zip(ins, rest))
        drafts = dict(zip(leaving, rest[len(ins) :]))
        arrivals = {}
        for at, i in enumerate(ins):
            arrivals[i] = pltpu.make_async_copy(given[i], buffers[i], rest[-1].at[at])
            arrivals[i].start()

        def get(i):
            if i in arrivals:
                arrivals.pop(i).wait()
            return buffers.get(i, given[i])

        outs = [drafts.get(i, results[i]) for i in range(n_out)]
        body(refs[:n_smem], get, outs, *rest[len(staged) : len(rest) - (1 if staged else 0)])
        for i in ins:
            get(i)
        departures = [
            pltpu.make_async_copy(drafts[i], results[i], rest[-1].at[len(ins) + at])
            for at, i in enumerate(leaving)
        ]
        for copy in departures:
            copy.start()
        for copy in departures:
            copy.wait()

    hbm = pl.BlockSpec(memory_space=pltpu.HBM)
    vmem = pl.BlockSpec(memory_space=pltpu.VMEM)
    copies = [pltpu.SemaphoreType.DMA((len(staged),))] if staged else []
    return pl.pallas_call(
        kernel,
        out_shape=outputs,
        in_specs=[pl.BlockSpec(memory_space=pltpu.SMEM)] * n_smem
        + [hbm if i in in_hbm or i in ins else vmem for i in range(n_in)],
        out_specs=[hbm if ("out", i) in in_hbm or i in leaving else vmem for i in range(n_out)],
        scratch_shapes=[pltpu.VMEM(inputs[i].shape, inputs[i].dtype) for i in ins]
        + [pltpu.VMEM(outputs[i].shape, outputs[i].dtype) for i in leaving]
        + list(scratch)
        + copies,
        compiler_params=pltpu.CompilerParams(vmem_limit_bytes=mebibytes * 2**20),
        cost_estimate=cost(us),
        name=name,
    )(*smem, *inputs)


def shaped(dtype, *shape):
    return jax.ShapeDtypeStruct(shape, dtype)


def group_window(group, local):
    start = (group * local) // 128 * 128
    return pl.multiple_of(start, 128), (group * local) % 128 != 0


def pack_body(smem, get, outs):
    (packet,) = outs
    tok, width = get(0).shape
    row = jnp.broadcast_to(get(1)[...].astype(f32), (packet.shape[0] - tok, tok))
    packet[tok:, :tok] = row.astype(bf16)
    packet[tok:, tok:] = jnp.zeros((packet.shape[0] - tok, width - tok), bf16)
    packet[:tok, :] = get(0)[...]


def packed(tokens, segment_ids):
    tok, width = tokens.shape
    return kernel_call(
        pack_body,
        "pack",
        [],
        [tokens, segment_ids],
        [shaped(bf16, tok + 16, width)],
        staged=(0, 1),
        mebibytes=60,
        us=1,
    )[0]


def bias_body(smem, get, outs):
    place, table = smem
    (rows_ref,) = outs
    span = rows_ref.shape[1]
    heads = table.shape[1] // groups
    buckets = bucket_row(span, table.shape[0] // 2)
    for h in range(heads):
        head = place[0] * heads + h
        row = jnp.full((1, span), table[0, head], f32)
        for b in range(1, table.shape[0]):
            row = jnp.where(buckets == b, table[b, head], row)
        rows_ref[h : h + 1, :] = row


def bias_rows(place, table, span):
    return kernel_call(bias_body, "bias_rows", [place, table], [], [shaped(f32, 8, span)], us=1)[0]


def project(place, tokens, segment_ids, gain, w_query, w_key, w_value):
    tok, width = tokens.shape
    span = -(-(3 * width // groups + 1) // 128) * 128
    return kernel_call(
        project_body,
        "project",
        [place],
        [tokens, segment_ids, gain, w_query, w_key, w_value],
        [shaped(bf16, tok, span)] * 4 + [shaped(bf16, tok, width)],
        scratch=[pltpu.VMEM((3, tok, width), bf16)],
        staged=(0, 1, 3, 4, 5),
        mebibytes=10,
        us=4,
    )


def project_body(smem, get, outs, weight_scr, normed_scr, all_scr, *, count):
    (place,) = smem
    kv_ref, q_ref, normed_ref = outs
    group = place[0]
    tok = q_ref.shape[1]
    s_count = kv_ref.shape[1]
    local = q_ref.shape[2]
    window, late = group_window(group, local)
    for i in range(3):
        both = get(count + 1 + i)[:, pl.ds(window, -(-local // 128) * 128)]
        weight_scr[:, i * local : (i + 1) * local] = jnp.where(
            late, both[:, both.shape[1] - local :], both[:, :local]
        )
    gain = get(count)[...]
    for e in range(s_count):
        for d in range(count):
            values = get(d)[e, :tok, :].astype(f32)
            normed_scr[d * tok : (d + 1) * tok, :] = (values * rms_scale(values) * gain).astype(bf16)
        all_scr[...] = dot(normed_scr[...], weight_scr[...], 1, 0).astype(bf16)
        for d in range(count):
            rows = all_scr[d * tok : (d + 1) * tok, :]
            kv_ref[d, e, :, : 2 * local] = rows[:, local:]
            row = jnp.broadcast_to(get(d)[e, tok : tok + 1, :tok].astype(f32), (tok, tok))
            kv_ref[d, e, :, 2 * local :] = jnp.transpose(row).astype(bf16)
            if e == 0:
                q_ref[d] = rows[:, :local]
                normed_ref[d * tok : (d + 1) * tok, :] = normed_scr[d * tok : (d + 1) * tok, :]


def project(place, blocks, gain, w_query, w_key, w_value):
    s_count, rows, width = blocks[0].shape
    tok = rows - 16
    local = width // groups
    count = len(blocks)
    return kernel_call(
        functools.partial(project_body, count=count),
        "project",
        [place],
        [*blocks, gain, w_query, w_key, w_value],
        [
            shaped(bf16, count, s_count, tok, 2 * local + tok),
            shaped(bf16, count, tok, local),
            shaped(bf16, count * tok, width),
        ],
        scratch=[
            pltpu.VMEM((width, 3 * local), bf16),
            pltpu.VMEM((count * tok, width), bf16),
            pltpu.VMEM((count * tok, 3 * local), bf16),
        ],
        mebibytes=8,
        us=3,
    )


def forward_body(smem, get, outs, segk, strip, s_scr, p_scr, sems, *, blocks, chunk):
    (place,) = smem
    ctx = outs[0:4]
    q_ref, k_ref, v_ref, o_ref, p_ref = outs[4:9]
    group, core, s_own = place[0], place[1], place[2]
    tok = 128
    head_size = 64
    s_count = blocks // 8
    local = q_ref.shape[1]
    seq = blocks * tok
    chunks = seq // chunk

    def block_of(d, e, k):
        return (((group ^ d) * s_count + (s_own ^ e)) * 2) + (core if k == 0 else 1 - core)

    def load_chunk(e):
        for k in range(2):
            for d in range(4):
                source, at = (get(2 * k), d) if d < 3 else (get(2 * k + 1), 0)
                start = pl.multiple_of(block_of(d, e, k) * tok, tok)
                k_ref[pl.ds(start, tok), :] = source[at, e, :, :local]
                v_ref[pl.ds(start, tok), :] = source[at, e, :, local : 2 * local]
                row = jnp.transpose(source[at, e, :, 2 * local :].astype(f32))
                segk[0:1, pl.ds(start, tok)] = row[0:1]

    load_chunk(0)
    for d in range(4):
        q_ref[d * tok : (d + 1) * tok, :] = get(4)[d] if d < 3 else get(5)[0]
    if s_count > 1:

        @pl.loop(1, s_count)
        def _(e):
            load_chunk(e)

    def p_copy(slot, h, d):
        return pltpu.make_async_copy(
            p_scr.at[slot], p_ref.at[h, :, pl.ds(d * tok, tok), :], sems.at[slot]
        )

    heads = local // head_size
    rows_at_once = 32
    pending = {}
    span = 4 * tok
    for h in range(heads):
        cols = slice(h * head_size, (h + 1) * head_size)
        bias_row = get(6)[h : h + 1, :]
        spread = jnp.broadcast_to(bias_row, (tok, span))
        near = pltpu.roll(spread, 0, 1, stride=1, stride_axis=0)
        strip[:, tok * (blocks - 2) : tok * (blocks + 1)] = near[:, tok : 4 * tok]
        strip[:, : tok * (blocks - 2)] = jnp.broadcast_to(
            bias_row[:, :1], (tok, tok * (blocks - 2))
        )
        strip[:, tok * (blocks + 1) :] = jnp.broadcast_to(
            bias_row[:, span - 1 :], (tok, tok * (blocks - 2))
        )
        if chunks == 1:
            s_scr[...] = dot(q_ref[:, cols], k_ref[:, cols], 1, 1)
        for d in range(4):
            query_block = block_of(d, 0, 0)
            strip_base = tok * (blocks - 1) - query_block * tok
            source, at = (get(0), d) if d < 3 else (get(1), 0)
            seg_col = source[at, 0, :, 2 * local : 2 * local + 1].astype(f32)
            slot = (h * 4 + d) % 2
            if slot in pending:
                pending.pop(slot).wait()
            queries = q_ref[d * tok : (d + 1) * tok, cols]
            if chunks == 1:
                for r in range(0, tok, rows_at_once):
                    rows = slice(r, r + rows_at_once)
                    bias = strip[rows, pl.ds(pl.multiple_of(strip_base, tok), seq)]
                    scores = s_scr[d * tok + r : d * tok + r + rows_at_once, :] + bias
                    scores = jnp.where(seg_col[rows] == segk[0:1, :], scores, masked_score)
                    top = jnp.max(scores, axis=1, keepdims=True)
                    exps = jnp.exp(scores - top)
                    total = jnp.sum(exps, axis=1, keepdims=True)
                    at = d * tok + r
                    p_ref[h, 0, at : at + rows_at_once, :] = (exps * (1.0 / total)).astype(bf16)
                if d < 3:
                    continue
                all_weighted = dot(p_ref[h, 0], v_ref[:, cols], 1, 0)
                o_ref[:, cols] = all_weighted
                for k in range(4):
                    ctx[k][:, cols] = all_weighted[k * tok : (k + 1) * tok].astype(bf16)
                continue
            else:
                def score_chunk(i, top):
                    start = pl.multiple_of(i * chunk, chunk)
                    scores = dot(queries, k_ref[pl.ds(start, chunk), cols], 1, 1)
                    base = pl.multiple_of(strip_base + start, tok)
                    scores = scores + strip[:, pl.ds(base, chunk)]
                    same = seg_col == segk[0:1, pl.ds(start, chunk)]
                    scores = jnp.where(same, scores, masked_score)
                    s_scr[0, :, pl.ds(start, chunk)] = scores
                    return jnp.maximum(top, jnp.max(scores, axis=1, keepdims=True))

                top = lax.fori_loop(
                    0, chunks, score_chunk, jnp.full((tok, 1), -3e38, f32)
                )

                def exp_chunk(i, total):
                    start = pl.multiple_of(i * chunk, chunk)
                    exps = jnp.exp(s_scr[0, :, pl.ds(start, chunk)] - top)
                    s_scr[0, :, pl.ds(start, chunk)] = exps
                    return total + jnp.sum(exps, axis=1, keepdims=True)

                total = lax.fori_loop(0, chunks, exp_chunk, jnp.zeros((tok, 1), f32))
                inverse = 1.0 / total

                def weigh_chunk(i, weighted):
                    start = pl.multiple_of(i * chunk, chunk)
                    low = (s_scr[0, :, pl.ds(start, chunk)] * inverse).astype(bf16)
                    p_scr[slot, i] = low
                    return weighted + jnp.dot(
                        low, v_ref[pl.ds(start, chunk), cols], preferred_element_type=f32
                    )

                weighted = lax.fori_loop(
                    0, chunks, weigh_chunk, jnp.zeros((tok, head_size), f32)
                )
            if chunks > 1:
                copy = p_copy(slot, h, d)
                copy.start()
                pending[slot] = copy
            o_ref[d * tok : (d + 1) * tok, cols] = weighted
            ctx[d][:, cols] = weighted.astype(bf16)
    for copy in pending.values():
        copy.wait()


def attention_forward(place, kv, q, bias):
    s_count, tok = kv[0].shape[1:3]
    local = q[0].shape[2]
    blocks = 8 * s_count
    seq = blocks * tok
    chunk = min(seq, 1024)
    shapes = (
        [shaped(bf16, tok, local)] * 4
        + [shaped(bf16, 4 * tok, local)]
        + [shaped(bf16, seq, local)] * 2
        + [shaped(f32, 4 * tok, local)]
        + [shaped(bf16, local // 64, seq // chunk, 4 * tok, chunk)]
    )
    return kernel_call(
        functools.partial(forward_body, blocks=blocks, chunk=chunk),
        "attention_forward",
        [place],
        [*kv, *q, bias],
        shapes,
        scratch=[
            pltpu.VMEM((8, seq), f32),
            pltpu.VMEM((tok, (2 * blocks - 1) * tok), f32),
            pltpu.VMEM((4 * tok, seq) if seq == chunk else (1, tok, seq), f32),
            pltpu.VMEM((2, seq // chunk, tok, chunk) if s_count > 1 else (2, 1, 16, 128), bf16),
            pltpu.SemaphoreType.DMA((2,)),
        ],
        in_hbm=(("out", 8),) if s_count > 1 else (),
        mebibytes=9 if s_count == 1 else 60,
        us=10,
    )


def backward_body(
    smem, get, outs, p_scr, ds_scr, dctx_scr, strip, dq_scr, kv_scr, rows_scr, dp_scr, sems, *, blocks, chunk
):
    (place,) = smem
    p_ref = get(8)
    dq = outs[0:4]
    keep_ref, send_ref, table_ref = outs[4:7]
    group, core, s_own = place[0], place[1], place[2]
    tok = 128
    head_size = 64
    seq = blocks * tok
    chunks = seq // chunk
    s_count = blocks // 8

    def p_copy(h, i, slot):
        return pltpu.make_async_copy(p_ref.at[h, i], p_scr.at[slot], sems.at[slot])

    if chunks > 1:
        p_copy(0, 0, 0).start()
    for d in range(4):
        dctx_scr[d * tok : (d + 1) * tok, :] = get(d)[...]
    q_ref, k_ref, v_ref, o_ref = get(4), get(5), get(6), get(7)
    heads = q_ref.shape[1] // head_size
    rows_scr[...] = jnp.zeros_like(rows_scr)
    rows_at_once = 32
    for h in range(heads):
        cols = slice(h * head_size, (h + 1) * head_size)
        strip[...] = jnp.zeros_like(strip)
        out_grad = dctx_scr[:, cols]
        delta = jnp.sum(out_grad.astype(f32) * o_ref[:, cols], axis=1, keepdims=True)

        def run_chunk(i, h=h, cols=cols, out_grad=out_grad, delta=delta):
            start = pl.multiple_of(i * chunk, chunk)
            slot = (h * chunks + i) % 2
            if chunks > 1:
                following = h * chunks + i + 1

                @pl.when(following < heads * chunks)
                def _():
                    p_copy(following // chunks, following % chunks, 1 - slot).start()

                p_copy(h, i, slot).wait()
                probs = p_scr.at[slot]
            else:
                probs = p_ref.at[h, 0]
            keys = k_ref[pl.ds(start, chunk), cols]
            values = v_ref[pl.ds(start, chunk), cols]
            dp_scr[...] = dot(out_grad, values, 1, 1)
            for d in range(4):
                query_block = ((group ^ d) * s_count + s_own) * 2 + core
                base = pl.multiple_of(tok * (blocks - 1) - query_block * tok + start, tok)
                for r in range(0, tok, rows_at_once):
                    rows = slice(d * tok + r, d * tok + r + rows_at_once)
                    here = dp_scr[rows, :] - delta[rows]
                    low = (probs[rows, :].astype(f32) * here).astype(bf16)
                    ds_scr[rows, :] = low
                    strip[r : r + rows_at_once, pl.ds(base, chunk)] += low.astype(f32)
            scores_grad = ds_scr[...]
            part = jnp.dot(scores_grad, keys, preferred_element_type=f32)
            if chunks == 1:
                dq_scr[:, cols] = part
            else:
                dq_scr[:, cols] += part
            queries = q_ref[:, cols]
            kv_scr[0, pl.ds(start, chunk), :] = jnp.transpose(dot(jnp.transpose(queries), scores_grad, 1, 0).astype(bf16))
            kv_scr[1, pl.ds(start, chunk), :] = jnp.transpose(dot(jnp.transpose(out_grad), probs[...], 1, 0).astype(bf16))

        if chunks == 1:
            run_chunk(0)
        else:
            dq_scr[:, cols] = jnp.zeros((4 * tok, head_size), f32)
            pl.loop(0, chunks)(run_chunk)

        def place_rows(e, h=h, cols=cols):
            for d in range(4):
                for k, target in ((0, keep_ref), (1, send_ref)):
                    block = ((group ^ d) * s_count + (s_own ^ e)) * 2 + (core if k == 0 else 1 - core)
                    start = pl.multiple_of(block * tok, tok)
                    width = heads * head_size
                    target[e, d, :, cols] = kv_scr[0, pl.ds(start, tok), :]
                    shifted = slice(width + h * head_size, width + (h + 1) * head_size)
                    target[e, d, :, shifted] = kv_scr[1, pl.ds(start, tok), :]

        if s_count == 1:
            place_rows(0)
        else:
            pl.loop(0, s_count)(place_rows)
        near = strip[:, tok * (blocks - 2) : tok * (blocks + 1)]
        left = jnp.zeros((1, tok), f32)
        right = jnp.zeros((1, tok), f32)
        for t in range(blocks - 2):
            left = left + jnp.sum(strip[:, t * tok : (t + 1) * tok], axis=0, keepdims=True)
            far = (blocks + 1 + t) * tok
            right = right + jnp.sum(strip[:, far : far + tok], axis=0, keepdims=True)
        rows_scr[h : h + 1, :] = jnp.concatenate([left, jnp.zeros((1, 2 * tok), f32), right], axis=1)
        spread = jnp.concatenate([jnp.zeros((tok, tok), f32), near], axis=1)
        skewed = spread[:8]
        for j in range(1, tok // 8):
            skewed = skewed + pltpu.roll(spread[8 * j : 8 * j + 8], 4 * tok - 8 * j, 1)
        row = lax.broadcasted_iota(jnp.int32, skewed.shape, 0)
        for step in (1, 2, 4):
            moved = pltpu.roll(skewed, 4 * tok - step, 1)
            skewed = jnp.where((row & step) != 0, moved, skewed)
        rows_scr[h : h + 1, :] += jnp.sum(skewed, axis=0, keepdims=True)
    for d in range(4):
        dq[d][...] = dq_scr[d * tok : (d + 1) * tok, :].astype(bf16)
    span = 4 * tok
    bucket_count = 2 * (len(cutoffs) + 1)
    buckets = bucket_row(span, bucket_count // 2)
    sums = rows_scr[...]
    lane = lax.broadcasted_iota(jnp.int32, (8, tok), 1)
    table = jnp.zeros((8, tok), f32)
    for b in range(bucket_count):
        picked = jnp.where(buckets == b, sums, 0.0)
        table = jnp.where(lane == b, jnp.sum(picked, axis=1, keepdims=True), table)
    table_ref[...] = table


def attention_backward(place, dctx, q, k, v, o, p):
    tok, local = dctx[0].shape
    seq = k.shape[0]
    blocks = seq // tok
    s_count = blocks // 8
    chunk = p.shape[3]
    shapes = (
        [shaped(bf16, tok, local)] * 4
        + [shaped(bf16, s_count, 4, tok, 2 * local)] * 2
        + [shaped(f32, 8, tok)]
    )
    return kernel_call(
        functools.partial(backward_body, blocks=blocks, chunk=chunk),
        "attention_backward",
        [place],
        [*dctx, q, k, v, o, p],
        shapes,
        scratch=[
            pltpu.VMEM((2, 4 * tok, chunk) if s_count > 1 else (2, 16, 128), bf16),
            pltpu.VMEM((4 * tok, chunk), bf16),
            pltpu.VMEM((4 * tok, local), bf16),
            pltpu.VMEM((tok, (2 * blocks - 1) * tok), f32),
            pltpu.VMEM((4 * tok, local), f32),
            pltpu.VMEM((2, seq, 64), bf16),
            pltpu.VMEM((8, 4 * tok), f32),
            pltpu.VMEM((4 * tok, chunk), f32),
            pltpu.SemaphoreType.DMA((2,)),
        ],
        in_hbm=(8,) if s_count > 1 else (),
        staged=tuple(("out", i) for i in range(6)) if s_count == 1 else (),
        mebibytes=15 if s_count == 1 else 60,
        us=0.01,
    )


def gated(gate, up):
    root = 0.7978845608028654
    square = gate * gate
    bend = jnp.tanh(root * (gate + 0.044715 * (gate * square)))
    act = 0.5 * gate * (1.0 + bend)
    slope = 0.5 * (1.0 + bend) + 0.5 * gate * (1.0 - bend * bend) * (
        root * (1.0 + 3.0 * 0.044715 * square)
    )
    return act, up * slope


def ffn_forward_body(smem, get, outs):
    (place,) = smem
    middle_ref, normed_ref, hidden_ref, act_ref, slope_ref = outs
    count = 4
    w_out, w_gate, w_up = get(6), get(7), get(8)
    group = place[0]
    tok, width = middle_ref.shape
    local = width // groups
    total = get(4)[...].astype(f32)
    for d in range(4):
        start = pl.multiple_of((group ^ d) * local, local)
        total = total + dot(get(d)[...], w_out[pl.ds(start, local), :], 1, 0)
    middle_ref[...] = total
    normed = (total * rms_scale(total) * get(5)[...]).astype(bf16)
    normed_ref[...] = normed
    step = w_gate.shape[1] // count
    for i in range(count):
        cols = slice(i * step, (i + 1) * step)
        up = dot(normed, w_up[:, cols], 1, 0)
        act, slope = gated(dot(normed, w_gate[:, cols], 1, 0), up)
        act_ref[:, cols] = act
        slope_ref[:, cols] = slope
        hidden_ref[:, cols] = (act * up).astype(bf16)


def ffn_forward(place, ctx, tokens, gain, w_out, w_gate, w_up):
    tok, width = tokens.shape
    ff = w_gate.shape[1]
    return kernel_call(
        ffn_forward_body,
        "ffn_forward",
        [place],
        [*ctx, tokens, gain, w_out, w_gate, w_up],
        [
            shaped(f32, tok, width),
            shaped(bf16, tok, width),
            shaped(bf16, tok, ff),
            shaped(f32, tok, ff),
            shaped(f32, tok, ff),
        ],
        staged=(4,),
        us=14,
    )


def ffn_backward_body(smem, get, outs, attn_scr):
    (place,) = smem
    out_ref, grad_ref, gain_grad_ref = outs[0:3]
    dctx = outs[3:7]
    w_down, w_gate, w_up, w_out = get(6), get(7), get(8), get(9)
    count = 4
    group = place[0]
    tok, width = grad_ref.shape
    ff = w_gate.shape[1]
    local = width // groups
    cot = get(0)[...]
    step = ff // count
    act_ref, slope_ref = get(3), get(4)
    normed_grad = jnp.zeros((tok, width), f32)
    for i in range(count):
        cols = slice(i * step, (i + 1) * step)
        hidden_grad = dot(cot, w_down[cols, :], 1, 1)
        gate = (hidden_grad * slope_ref[:, cols]).astype(bf16)
        up = (hidden_grad * act_ref[:, cols]).astype(bf16)
        normed_grad = normed_grad + dot(gate, w_gate[:, cols], 1, 1) + dot(up, w_up[:, cols], 1, 1)
    middle = get(1)[...]
    scale = rms_scale(middle)
    unit = middle * scale
    scaled = normed_grad * get(5)[...]
    gain_grad_ref[...] = jnp.sum(normed_grad * unit, axis=0, keepdims=True)
    middle_grad = cot.astype(f32) + scale * (
        scaled - unit * jnp.mean(unit * scaled, axis=1, keepdims=True)
    )
    grad_ref[...] = middle_grad
    attn = middle_grad.astype(bf16)
    attn_scr[...] = attn
    for d in range(4):
        start = pl.multiple_of((group ^ d) * local, local)
        dctx[d][...] = dot(attn, w_out[pl.ds(start, local), :], 1, 1).astype(bf16)
    for ref, which in ((outs[7], place[4]), (outs[8], 1 - place[4])):
        for d in range(4):
            ref[:, d * local : (d + 1) * local] = get(10 + d)[...]
        start = pl.multiple_of(which * (width // 2), width // 2)
        ref[:, width:] = attn_scr[:, pl.ds(start, width // 2)]
    out_ref[...] = (middle + dot(get(2)[...], w_down[...], 1, 0)).astype(bf16)


def ffn_backward(place, cot, middle, hidden, act, slope, gain, ctx, w_down, w_gate, w_up, w_out):
    tok, width = cot.shape
    local = width // groups
    return kernel_call(
        ffn_backward_body,
        "ffn_backward",
        [place],
        [cot, middle, hidden, act, slope, gain, w_down, w_gate, w_up, w_out, *ctx],
        [shaped(bf16, tok, width), shaped(f32, tok, width), shaped(f32, 1, width)]
        + [shaped(bf16, tok, local)] * 4
        + [shaped(bf16, tok, width + width // 2)] * 2,
        scratch=[pltpu.VMEM((tok, width), bf16)],
        mebibytes=6,
        us=6,
    )


def ffn_grad_body(
    smem, get, outs, normed_scr, cot_scr, hidden_scr, gate_scr, up_scr, both_scr, down_scr, *, s_count
):
    (place,) = smem
    kept_ref, sent_ref = outs
    group, core, far = place[0], place[1], place[4] == 1
    rows, eighth = hidden_scr.shape
    tok = rows // 8
    width = normed_scr.shape[1]
    local = width // groups
    for i in range(8):
        normed_scr[i * tok : (i + 1) * tok, :] = get(i)[...]
        cot_scr[i * tok : (i + 1) * tok, :] = get(8 + i)[...]
    start = ((group % 2) * 2 + core) * 2 * eighth + (group // 2) * eighth
    part = pl.ds(pl.multiple_of(start, eighth), eighth)
    w_gate, w_up, w_down = get(16)[:, part], get(17)[:, part], get(18)[part, :]
    half = rows // 2
    for i in range(2):
        span = slice(i * half, (i + 1) * half)
        up = dot(normed_scr[span, :], w_up, 1, 0)
        act, slope = gated(dot(normed_scr[span, :], w_gate, 1, 0), up)
        hidden_scr[span, :] = (act * up).astype(bf16)
        hidden_grad = dot(cot_scr[span, :], w_down, 1, 1)
        gate_scr[span, :] = (hidden_grad * slope).astype(bf16)
        up_scr[span, :] = (hidden_grad * act).astype(bf16)
    both_scr[:, :eighth] = dot(normed_scr[...], gate_scr[...], 0, 0)
    both_scr[:, eighth:] = dot(normed_scr[...], up_scr[...], 0, 0)
    down_scr[...] = dot(hidden_scr[...], cot_scr[...], 0, 0)
    unit = kept_ref.shape[1]
    block = 3 * unit // 2

    def pieces(x, s, y):
        found = []
        for k in range(3):
            parts = []
            for j in range(2):
                at = (((x + 2 * j) * s_count + s) * 2 + y) * block
                low, high = max(k * unit - j * block, 0), min((k + 1) * unit - j * block, block)
                if low < high:
                    parts.append(both_scr[at + low : at + high, :])
            found.append(parts[0] if len(parts) == 1 else jnp.concatenate(parts, axis=0))
        for k in range(4):
            at = (s * 4 + k) * unit
            cols = slice((x * 2 + y) * local, (x * 2 + y + 1) * local)
            found.append(down_scr[at : at + unit, cols])
        return found

    for s in range(s_count):
        for y in range(2):
            lane = 0
            for near, other in zip(pieces(0, s, y), pieces(1, s, y)):
                cols = slice(lane, lane + near.shape[1])
                kept_ref[s * 2 + y, :, cols] = jnp.where(far, other, near)
                sent_ref[s * 2 + y, :, cols] = jnp.where(far, near, other).astype(bf16)
                lane += near.shape[1]


def ffn_grad(place, normed, cot, w_gate, w_up, w_down, s_count):
    tok, width = normed[0].shape
    ff = w_gate.shape[1]
    eighth = ff // 8
    unit = eighth // (4 * s_count)
    shape = (2 * s_count, unit, 3 * 2 * eighth + 4 * width // groups)
    return kernel_call(
        functools.partial(ffn_grad_body, s_count=s_count),
        "ffn_grad",
        [place],
        [*normed, *cot, w_gate, w_up, w_down],
        [shaped(f32, *shape), shaped(bf16, *shape)],
        scratch=[
            pltpu.VMEM((8 * tok, width), bf16),
            pltpu.VMEM((8 * tok, width), bf16),
            pltpu.VMEM((8 * tok, eighth), bf16),
            pltpu.VMEM((8 * tok, eighth), bf16),
            pltpu.VMEM((8 * tok, eighth), bf16),
            pltpu.VMEM((width, 2 * eighth), f32),
            pltpu.VMEM((eighth, width), f32),
        ],
        mebibytes=16,
        us=0.01,
    )


def out_grad_body(smem, get, outs, ctx_scr, attn_scr, out_scr, *, order):
    (place,) = smem
    kept_ref, sent_ref = outs
    group, core, odd = place[0], place[1], ((place[5] >> order[0]) & 1) == 1
    tok = ctx_scr.shape[0] // 4
    width = ctx_scr.shape[1]
    local = width // groups
    for i in range(4):
        rows = slice(i * tok, (i + 1) * tok)
        ctx_scr[rows, :] = get(i)[:, :width]
        both = get(i)[:, width:]
        attn_scr[rows, :] = jnp.where(core == 0, both[:, :local], both[:, local:])
    turned = dot(ctx_scr[...], attn_scr[...], 0, 0)
    for d in range(4):
        start = pl.multiple_of((group ^ d) * local, local)
        out_scr[pl.ds(start, local), :] = turned[d * local : (d + 1) * local]
    pieces, block, unused = kept_ref.shape
    for i in range(pieces):
        first, second = (
            sum(((n >> k) & 1) << bit for k, bit in enumerate(order)) for n in (2 * i, 2 * i + 1)
        )
        even = out_scr[first * block : (first + 1) * block, :]
        other = out_scr[second * block : (second + 1) * block, :]
        kept_ref[i] = jnp.where(odd, other, even)
        sent_ref[i] = jnp.where(odd, even, other).astype(bf16)


def out_weight_grad(place, parts, wide, order):
    tok, span = parts[0].shape
    width = span * 2 // 3
    local = width // groups
    shape = (wide // 2, width // wide, local)
    return kernel_call(
        functools.partial(out_grad_body, order=order),
        "out_grad",
        [place],
        parts,
        [shaped(f32, *shape), shaped(bf16, *shape)],
        scratch=[
            pltpu.VMEM((4 * tok, width), bf16),
            pltpu.VMEM((4 * tok, local), bf16),
            pltpu.VMEM((width, local), f32),
        ],
        mebibytes=5,
        us=0.01,
    )


def out_sum_body(smem, get, outs, *, following):
    (place,) = smem
    kept, received = get(0), get(1)
    remaining = kept.shape[0]
    if remaining == 1:
        outs[0][...] = kept[0] + received[0].astype(f32)
        return
    odd = ((place[5] >> following) & 1) == 1
    for i in range(remaining // 2):
        even = kept[2 * i] + received[2 * i].astype(f32)
        other = kept[2 * i + 1] + received[2 * i + 1].astype(f32)
        outs[0][i] = jnp.where(odd, other, even)
        outs[1][i] = jnp.where(odd, even, other).astype(bf16)


def out_sum(layout, place, kept, sent, order, step):
    remaining, block, local = kept.shape
    if remaining == 1:
        outputs = [shaped(f32, block, local)]
    else:
        shape = (remaining // 2, block, local)
        outputs = [shaped(f32, *shape), shaped(bf16, *shape)]
    following = order[step + 1] if step + 1 < len(order) else 0
    return kernel_call(
        functools.partial(out_sum_body, following=following),
        "out_sum",
        [place],
        [kept, layout.wide_bit(sent, order[step])],
        outputs,
        us=0.01,
    )


def ffn_sum_body(smem, get, outs):
    (place,) = smem
    odd = place[3] == 1
    for i in range(outs[0].shape[0]):
        even = get(0)[2 * i] + get(1)[2 * i].astype(f32)
        other = get(0)[2 * i + 1] + get(1)[2 * i + 1].astype(f32)
        outs[0][i] = jnp.where(odd, other, even)
        outs[1][i] = jnp.where(odd, even, other).astype(bf16)


def ffn_sum(place, kept, received):
    pieces, unit, span = kept.shape
    return kernel_call(
        ffn_sum_body,
        "ffn_sum",
        [place],
        [kept, received],
        [shaped(f32, pieces // 2, unit, span), shaped(bf16, pieces // 2, unit, span)],
        us=0.01,
    )


def ffn_last_body(smem, get, outs, both_scr):
    (place,) = smem
    total = get(0)[0].astype(f32) + get(1)[0].astype(f32)
    unit = total.shape[0]
    block, span = outs[0].shape
    local = outs[2].shape[1]
    for k in range(3):
        both_scr[k * unit : (k + 1) * unit, :] = total[:, k * span : (k + 1) * span]
    for k in range(4):
        at = 3 * span + k * local
        outs[2][k * unit : (k + 1) * unit, :] = total[:, at : at + local].astype(bf16)
    low = place[0] // 2 == 0
    first, second = both_scr[:block, :], both_scr[block:, :]
    outs[0][...] = jnp.where(low, first, second).astype(bf16)
    outs[1][...] = jnp.where(low, second, first).astype(bf16)


def ffn_last(place, kept, received, local):
    unused, unit, span = kept.shape
    both = (span - 4 * local) // 3
    return kernel_call(
        ffn_last_body,
        "ffn_last",
        [place],
        [kept, received],
        [shaped(bf16, 3 * unit // 2, both)] * 2 + [shaped(bf16, 4 * unit, local)],
        scratch=[pltpu.VMEM((3 * unit, both), f32)],
        us=0.01,
    )


def ffn_owned_body(smem, get, outs):
    (place,) = smem
    low = place[0] // 2 == 0
    eighth = get(0).shape[1] // 2
    own, other = get(0)[...].astype(f32), get(1)[...].astype(f32)
    first, second = jnp.where(low, own, other), jnp.where(low, other, own)
    for i in range(2):
        cols = slice(i * eighth, (i + 1) * eighth)
        outs[i][:, :eighth] = first[:, cols]
        outs[i][:, eighth:] = second[:, cols]
    outs[2][...] = jnp.transpose(get(2)[...].astype(f32))


def ffn_owned(place, own, other, down):
    return kernel_call(
        ffn_owned_body,
        "ffn_owned",
        [place],
        [own, other, down],
        [shaped(f32, *own.shape)] * 2 + [shaped(f32, *down.shape[::-1])],
        us=1,
    )


def collect_body(smem, get, outs):
    local = outs[0].shape[2] // 3
    for d in range(4):
        outs[d // 2][d % 2, :, :local] = get(d)[...]
    for d in range(4):
        total = get(4)[d].astype(f32) + get(5)[d].astype(f32)
        outs[d // 2][d % 2, :, local:] = total.astype(bf16)


def collect(dq, kept, received):
    tok, local = dq[0].shape
    return kernel_call(
        collect_body,
        "collect",
        [],
        [*dq, kept, received],
        [shaped(bf16, 2, tok, 3 * local)] * 2,
        staged=tuple(range(6)),
        us=0.01,
    )


def exact(small):
    high = small.astype(bf16)
    return high, (small - high.astype(f32)).astype(bf16)


def attach(ref, rows, small):
    high, low = exact(small)
    ref[rows : rows + small.shape[0], : small.shape[1]] = high
    ref[rows : rows + small.shape[0], small.shape[1] : 2 * small.shape[1]] = low


def attach_rows(ref, rows, small):
    high, low = exact(small)
    count, lanes = small.shape
    ref[rows : rows + count, :lanes] = high
    below = rows + room(count)
    ref[below : below + count, :lanes] = low


def attached(ref, rows, small):
    count, lanes = small.shape
    high, low = exact(small)
    theirs = ref[rows : rows + count, :lanes].astype(f32)
    if ref.shape[1] >= 2 * lanes:
        theirs = theirs + ref[rows : rows + count, lanes : 2 * lanes].astype(f32)
    else:
        below = rows + room(count)
        theirs = theirs + ref[below : below + count, :lanes].astype(f32)
    return high.astype(f32) + low.astype(f32) + theirs


def qkv_grad_body(smem, get, outs, grad_scr, total_scr):
    (place,) = smem
    kept_ref, sent_ref, small_ref = outs
    group, core = place[0], place[1]
    width, span = total_scr.shape
    local = span // 3
    tok = grad_scr.shape[0] // 4
    for d in range(4):
        grad_scr[d * tok : (d + 1) * tok, :] = get(d // 2)[d % 2]
    total_scr[...] = dot(get(2)[...], grad_scr[: 3 * tok, :], 0, 0)
    total_scr[...] += dot(get(9)[...], grad_scr[3 * tok :, :], 0, 0)
    quarter = width // 4
    for i in range(2):
        start = pl.multiple_of((2 * i + core) * quarter, quarter)
        kept_ref[i] = total_scr[pl.ds(start, quarter), :]
        start = pl.multiple_of((2 * i + 1 - core) * quarter, quarter)
        sent_ref[i * quarter : (i + 1) * quarter, :] = total_scr[pl.ds(start, quarter), :].astype(bf16)
    window, late = group_window(group, local)
    ones = jnp.ones((8, local), bf16)
    gain_grad = jnp.zeros((8, width), f32)
    for i in range(3):
        both = get(6 + i)[:, pl.ds(window, -(-local // 128) * 128)]
        weight = jnp.where(late, both[:, both.shape[1] - local :], both[:, :local])
        product = total_scr[:, i * local : (i + 1) * local] * weight.astype(f32)
        high, rest = exact(product)
        gain_grad = gain_grad + dot(ones, high, 1, 1) + dot(ones, rest, 1, 1)
    gain_grad = gain_grad[0:1] / get(3)[...]
    ffn_gain = get(4)[...]
    lanes = 128
    rows = width // lanes
    for i in range(rows):
        small_ref[i : i + 1, :] = gain_grad[:, i * lanes : (i + 1) * lanes]
        small_ref[rows + i : rows + i + 1, :] = ffn_gain[:, i * lanes : (i + 1) * lanes]
    heads = (small_ref.shape[0] - 2 * rows) // groups
    table = get(5)[:heads, :]
    for i in range(groups):
        at = 2 * rows + i * heads
        small_ref[at : at + heads, :] = jnp.where(group == i, table, 0.0)
    sent_ref[2 * quarter :, :] = jnp.zeros((sent_ref.shape[0] - 2 * quarter, span), bf16)
    attach(sent_ref, 2 * quarter, small_ref[...])


def room(count):
    return -(-count // 16) * 16


def qkv_grad(
    place,
    grads,
    normed_first,
    normed_last,
    gain,
    gain_grad,
    table,
    head_count,
    w_query,
    w_key,
    w_value,
):
    rows, width = 4 * grads[0].shape[1], normed_first.shape[1]
    local = width // groups
    count = 2 * width // 128 + head_count
    return kernel_call(
        qkv_grad_body,
        "qkv_grad",
        [place],
        [
            *grads,
            normed_first,
            gain,
            gain_grad,
            table,
            w_query,
            w_key,
            w_value,
            normed_last,
        ],
        [
            shaped(f32, 2, width // 4, 3 * local),
            shaped(bf16, width // 2 + room(count), 3 * local),
            shaped(f32, count, 128),
        ],
        scratch=[
            pltpu.VMEM((rows, 3 * local), bf16),
            pltpu.VMEM((width, 3 * local), f32),
        ],
        mebibytes=10,
        us=0.01,
    )


def qkv_sum_body(smem, get, outs, *, axis, s_count):
    (place,) = smem
    kept, small, received = get(0), get(1), get(2)
    parts, rows, span = kept.shape
    totals = [
        kept[i] + received[i * rows : (i + 1) * rows, :].astype(f32) for i in range(parts)
    ]
    summed = attached(received, parts * rows, small[...])
    outs[-1][...] = summed
    if axis == "x":
        for i in range(parts):
            outs[0][i] = totals[i].astype(outs[0].dtype)
        return
    kept_ref, sent_ref = outs[:2]
    blocks, block = kept_ref.shape[0], kept_ref.shape[1]
    if axis == "core":
        other = place[3] == 1
        pairs = []
        for i in range(blocks):
            source, at = totals[i // s_count], 2 * (i % s_count) * block
            pairs.append((source[at : at + block], source[at + block : at + 2 * block]))
    else:
        other = place[4] == 1
        pairs = [(totals[i], totals[blocks + i]) for i in range(blocks)]
    for i, (first, second) in enumerate(pairs):
        kept_ref[i] = jnp.where(other, second, first)
        theirs = jnp.where(other, first, second)
        sent_ref[i * block : (i + 1) * block, :] = theirs.astype(bf16)
    filled = blocks * block
    sent_ref[filled:, :] = jnp.zeros((sent_ref.shape[0] - filled, span), bf16)
    attach(sent_ref, filled, summed)


def qkv_sum(place, kept, small, received, axis, s_count):
    parts, rows, span = kept.shape
    count = small.shape[0]
    if axis == "x":
        outputs = [shaped(bf16 if s_count == 1 else f32, *kept.shape)]
    else:
        shape = (parts * s_count, rows // (2 * s_count), span)
        if axis == "y":
            shape = (parts // 2, rows, span)
        outputs = [
            shaped(f32, *shape),
            shaped(bf16, shape[0] * shape[1] + room(count), span),
        ]
    return kernel_call(
        functools.partial(qkv_sum_body, axis=axis, s_count=s_count),
        f"qkv_sum_{axis}",
        [place],
        [kept, small, received],
        outputs + [shaped(f32, count, 128)],
        us=0.01,
    )


def input_grad_body(smem, get, outs, all_scr):
    (place,) = smem
    group = place[0]
    weights = [get(6 + i) for i in range(3)]
    local = get(0).shape[2] // 3
    window = -(-local // 128) * 128
    tok = get(0).shape[1]
    spare = jnp.zeros((tok, window - local), bf16)
    all_scr[...] = jnp.zeros_like(all_scr)
    for d in range(4):
        start, late = group_window(group ^ d, local)
        grads = get((0, 2, 1, 2)[d])[d // 3]
        for i in range(3):
            part = grads[:, i * local : (i + 1) * local]
            part = jnp.where(
                late,
                jnp.concatenate([spare, part], axis=1),
                jnp.concatenate([part, spare], axis=1),
            )
            all_scr[i, :, pl.ds(start, window)] += part
    normed_grad = dot(all_scr[0], weights[0][...], 1, 1)
    for i in range(1, 3):
        normed_grad = normed_grad + dot(all_scr[i], weights[i][...], 1, 1)
    values = get(3)[...].astype(f32)
    scale = rms_scale(values)
    unit = values * scale
    scaled = normed_grad * get(4)[...]
    outs[0][...] = get(5)[...] + scale * (
        scaled - unit * jnp.mean(unit * scaled, axis=1, keepdims=True)
    )


def final_input_grad(place, grads, tokens, gain, middle_grad, w_query, w_key, w_value):
    return kernel_call(
        input_grad_body,
        "input_grad",
        [place],
        [*grads, tokens, gain, middle_grad, w_query, w_key, w_value],
        [shaped(f32, *tokens.shape)],
        scratch=[pltpu.VMEM((3, *tokens.shape), bf16)],
        staged=(0, 1, 2, 3, 5),
        mebibytes=6,
        us=0.01,
    )[0]


def stacked_body(smem, get, outs):
    rows = get(0).shape[0]
    outs[0][:rows, :] = get(0)[...]
    outs[0][rows:, :] = get(1)[...]


def stacked(first, second):
    rows, width = first.shape
    return kernel_call(
        stacked_body, "stacked", [], [first, second], [shaped(bf16, 2 * rows, width)], us=0.01
    )[0]


def forwarded_body(smem, get, outs):
    outs[0][0] = get(0)[1]
    outs[0][1] = get(1)[1]


def forwarded(near, far):
    return kernel_call(
        forwarded_body, "forwarded", [], [near, far], [shaped(bf16, *near.shape)], us=0.01
    )[0]


def after(values, done):
    return lax.optimization_barrier((values, done))[0]


def halved(block, axis, keep):
    return (
        lax.dynamic_index_in_dim(block, keep, axis, keepdims=False),
        lax.dynamic_index_in_dim(block, 1 - keep, axis, keepdims=False),
    )


def on_device(
    inputs,
    segment_ids,
    gain_attn,
    w_query,
    w_key,
    w_value,
    w_out,
    gain_ffn,
    w_gate,
    w_up,
    w_down,
    bias_table,
    cotangent,
):
    layout = Layout(lax.axis_size("narrow"), lax.axis_size("wide"))
    s_count = layout.s_count
    tokens = inputs[0]
    out_grad = cotangent[0]
    tok, width = tokens.shape
    local = width // groups
    ff = w_gate.shape[1]
    bucket_count, head_count = bias_table.shape
    narrow = lax.axis_index("narrow")
    wide = lax.axis_index("wide")
    core = narrow % 2
    across = narrow // 2
    group = wide // (2 * s_count)
    s_own = (wide // 2) % s_count
    y_own = wide % 2
    place = jnp.stack([group, core, s_own, y_own, across, wide]).astype(jnp.int32)
    gain_attn = gain_attn[None]
    gain_ffn = gain_ffn[None]

    packet = packed(tokens, segment_ids)
    own = [layout.turned(packet, d)[None] for d in range(3)]
    own.append(layout.wide_bit(own[2], layout.wide.bit_length() - 3))
    for d in range(4):
        size = 1
        while size < s_count:
            own[d] = jnp.concatenate([own[d], layout.wide_bit(own[d], size.bit_length())], axis=0)
            size *= 2
    bias = bias_rows(place, bias_table, 4 * tok)
    kv_first, q_first, normed_first = project(place, own[:3], gain_attn, w_query, w_key, w_value)
    kv_first = after(kv_first, bias)
    cot = after(out_grad, kv_first)
    cot = [out_grad, layout.near_group(cot), layout.far_group(cot)]
    kv_last, q_last, normed_last = project(place, own[3:], gain_attn, w_query, w_key, w_value)
    kv = [kv_first, kv_last, layout.core(kv_first), layout.core(kv_last)]
    outs = attention_forward(place, kv, [q_first, q_last], bias)
    ctx_parts = outs[:4]
    q_own, k_all, v_all, o_own, probs = outs[4:]
    ctx_parts = after(ctx_parts, cot)
    ctx = [layout.turned(ctx_parts[d], d) for d in range(4)]
    cot.append(layout.near_group(after(cot[2], ctx)))

    middle, normed_ffn, hidden, act, slope = ffn_forward(
        place, ctx, tokens, gain_ffn, w_out, w_gate, w_up
    )
    bits = layout.wide.bit_length() - 1
    normed_far = layout.far_group(normed_ffn)
    back = ffn_backward(
        place, out_grad, middle, hidden, act, slope, gain_ffn, ctx, w_down, w_gate, w_up, w_out
    )
    output, middle_grad, grad_gain_ffn = back[0:3]
    dctx = [layout.turned(back[3 + d], d) for d in range(4)]
    mine, far = back[7:9]
    far = layout.across(after(far, dctx[0]))
    normed_near, normed_far = after((normed_ffn, normed_far), dctx[1])
    normed = [
        normed_ffn,
        layout.near_group(normed_near),
        normed_far,
        layout.near_group(normed_far),
    ]

    dctx = after(dctx, cot[3])
    back = attention_backward(place, dctx, q_own, k_all, v_all, o_own, probs)
    dq, kept, sent, table_rows = back[:4], back[4], back[5], back[6]

    received = layout.core(sent)
    size = s_count
    while size > 1:
        size //= 2
        total = kept.astype(f32) + received.astype(f32)
        kept = total[:size]
        received = layout.wide_bit(total[size:].astype(bf16), size.bit_length())
    normed, cot, mine, far = after((normed, cot, mine, far), sent)
    normed = normed + [layout.core(block) for block in normed]
    cot = cot + [layout.core(block) for block in cot]
    out_parts = [mine, layout.core(mine), far, layout.core(far)]
    low_grads = collect(dq, kept[0], received[0])
    ffn_kept, ffn_sent = ffn_grad(
        place, after(normed, low_grads), cot, w_gate, w_up, w_down, s_count
    )
    normed_first = after(normed_first, ffn_sent)
    qkv_kept, qkv_sent, small = qkv_grad(
        place,
        low_grads,
        normed_first,
        normed_last,
        gain_attn,
        grad_gain_ffn,
        table_rows,
        head_count,
        w_query,
        w_key,
        w_value,
    )
    order = (bits - 2, bits - 1, *range(bits - 2))
    out = out_weight_grad(place, after(out_parts, qkv_sent), layout.wide, order)

    returned = [layout.turned(low_grads[0], 0), layout.turned(low_grads[1], 2)]
    qkv_kept = after(qkv_kept, out)
    step = qkv_sum(place, qkv_kept, small, layout.core(qkv_sent), "core", s_count)
    out = out_sum(layout, place, after(out[0], step), out[1], order, 0)
    ffn_kept, ffn_sent = ffn_sum(place, after(ffn_kept, out), layout.across(ffn_sent))
    step = qkv_sum(
        place, after(step[0], ffn_kept), step[2], layout.wide_bit(step[1], 0), "y", s_count
    )
    onward = forwarded(returned[0], after(returned[1], step))
    returned.append(layout.wide_bit(onward, bits - 2))
    part, small = qkv_sum(
        place, after(step[0], onward), step[2], layout.across(step[1]), "x", s_count
    )
    out = out_sum(layout, place, after(out[0], part), out[1], order, 1)
    rows = width // layout.wide
    size = s_count
    bit = 1
    while size > 1:
        size //= 2
        part = part.reshape(size, 2, rows, 3 * local)
        kept, sent = halved(part, 1, (s_own >> (bit - 1)) & 1)
        part = kept + layout.wide_bit(sent.astype(bf16), bit).astype(f32)
        small = small + layout.wide_bit(small, bit)
        bit += 1
    part = part.reshape(rows, 3 * local).astype(bf16)
    received = layout.wide_bit(ffn_sent, 0)
    size = s_count
    bit = 1
    while size > 1:
        size //= 2
        total = (ffn_kept + received.astype(f32)).reshape(size, 2, *ffn_kept.shape[1:])
        ffn_kept, ffn_sent = halved(total, 1, (s_own >> (bit - 1)) & 1)
        received = layout.wide_bit(ffn_sent.astype(bf16), bit)
        bit += 1
    ffn_parts = ffn_last(place, after(ffn_kept, out), received, local)
    small = small + layout.wide_bit(small, bits - 2)
    small = small + layout.wide_bit(small, bits - 1)

    def half_owner(flip):
        return lambda x, c, g, s, y: (g % 2, c, x + 2 * (g // 2 ^ flip), s, y)

    def down_owner(x, c, g, s, y):
        at = g // 2 * s_count + s
        return (x, y, g % 2 * 2 + c, at // 2, at % 2)

    final_gate, final_up, final_down = ffn_owned(
        place,
        layout.send(ffn_parts[0], half_owner(0)),
        layout.send(ffn_parts[1], half_owner(1)),
        layout.send(ffn_parts[2], down_owner),
    )
    part = layout.send(part, lambda x, c, g, s, y: (g // 2, g % 2, x * 2 + c, s, y)).astype(f32)
    final_query, final_key, final_value = (
        part[:, :local],
        part[:, local : 2 * local],
        part[:, 2 * local :],
    )
    middle_grad = after(middle_grad, ffn_parts)
    input_grad = final_input_grad(
        place, returned, tokens, gain_attn, middle_grad, w_query, w_key, w_value
    )
    for step in range(2, bits):
        out = out_sum(layout, place, after(out[0], input_grad), out[1], order, step)
    (final_out,) = out

    gain_rows = width // 128
    sum_gain_attn = small[:gain_rows].reshape(width)
    sum_gain_ffn = small[gain_rows : 2 * gain_rows].reshape(width)
    sum_table = small[2 * gain_rows :, :bucket_count].T
    return (
        output[None],
        input_grad[None],
        sum_gain_attn,
        final_query,
        final_key,
        final_value,
        final_out,
        sum_gain_ffn,
        final_gate,
        final_up,
        final_down.T,
        sum_table,
    )


def solution(mesh):
    tokens = P("narrow", "wide", None)
    share = P("wide", "narrow")
    return jax.shard_map(
        on_device,
        mesh=mesh,
        in_specs=(tokens, P("narrow", "wide")) + (P(),) * 10 + (tokens,),
        out_specs=(
            tokens,
            tokens,
            P(),
            share,
            share,
            share,
            share,
            P(),
            share,
            share,
            share,
            P(),
        ),
        check_vma=False,
    )
```
